32 devices in a mesh: section: 4 (over x, core), dp: 8 (over z, y).
Axes of the slice: x: 2, y: 2, z: 4, core: 2. Of those that a mesh axis runs over, the one named last changes fastest.
Arguments:
- tokens: bfloat16 [4096, 1024], P('dp'), may hold values from -6 to 6
- segments: int32 [16, 256], P('dp'), may hold values from 0 to 4, never falling along the last dimension, each value on 1 to 96 neighbouring positions
- qkv_weight: bfloat16 [2048, 3072], P('section'), may hold values from -0.1875 to 0.1875
- qv_bias: bfloat16 [4096], P('section'), may hold values from -3 to 3
- out_weight: bfloat16 [2048, 1024], P('section'), may hold values from -1 to 1
- out_bias: bfloat16 [2048], P('section'), may hold values from -3 to 3
- up_weight: bfloat16 [2048, 4096], P('section'), may hold values from -0.1875 to 0.1875
- up_bias: bfloat16 [8192], P('section'), may hold values from -3 to 3
- down_weight: bfloat16 [8192, 1024], P('section'), may hold values from -0.125 to 0.125
- down_bias: bfloat16 [2048], P('section'), may hold values from -3 to 3
- norm_gain: float32 [4, 1024], P('section'), may hold values from 0.1 to 1.9
- norm_shift: float32 [4, 1024], P('section'), may hold values from -2 to 2
- cotangent: bfloat16 [4096, 1024], P('dp'), may hold values from -6 to 6
Outputs:
- block_output: bfloat16 [4096, 1024], P('dp', 'section')
- input_gradient: bfloat16 [4096, 1024], P('dp', 'section')
- grad_qkv_weight: float32 [2048, 3072], P(('section', 'dp'))
- grad_qv_bias: float32 [4096], P(('section', 'dp'))
- grad_out_weight: float32 [2048, 1024], P(('section', 'dp'))
- grad_out_bias: float32 [2048], P(('section', 'dp'))
- grad_up_weight: float32 [2048, 4096], P(('section', 'dp'))
- grad_up_bias: float32 [8192], P(('section', 'dp'))
- grad_down_weight: float32 [8192, 1024], P(('section', 'dp'))
- grad_down_bias: float32 [2048], P(('section', 'dp'))
- grad_norm_gain: float32 [4, 1024], P('section', 'dp')
- grad_norm_shift: float32 [4, 1024], P('section', 'dp')
The draws below stay inside these ranges and needn't reach their ends.
Inputs may be any that keep to these rules, and one draw needn't show every extreme that they name: `segments`: segment numbers never fall along a row of 256 tokens; each of the 5 numbers appears in every row.
All inputs are finite; a program needn't handle non-finite values.
Results may differ from the reference program's by a relative error of at most 0.017.
Values may be sent and summed in bfloat16 or wider, within the bound.
No kernel may reach another device: no remote copies, remote signals or barrier semaphores. Data moves between devices by JAX's collectives and lax.ppermute only.
A program may use at most 640 MiB of HBM per device.

```python
import math
import jax
import jax.numpy as jnp
import numpy as np
from jax import lax

D = 1024
HEADS = 16
FF = 4096
ROW_LEN = 256
ROWS = 16
TOKENS = 4096


def steps_of(rng, shape, split, least, high):
    factor_of, own = 1.0, jax.random.fold_in(rng, 6)
    for axis_at, shards_of in split:
        steps = jnp.exp(jax.random.uniform(jax.random.fold_in(own, axis_at), (shards_of,), jnp.float32, least / len(split), high / len(split)))
        factor_of = factor_of * jnp.repeat(steps, shape[axis_at] // shards_of).reshape([-1 if axis == axis_at else 1 for axis in range(len(shape))])
    return factor_of


def split_up(amount, total, bound, slope):
    loads = [(1 << 20) // math.isqrt(rank ** slope) + 1 for rank in range(2, amount + 1)]
    rest, counts = total - bound - (amount - 1), [1] * (amount - 1)
    while rest > 0:
        free = [i for i in range(amount - 1) if counts[i] < bound]
        pool, remaining = sum([loads[i] for i in free]), rest
        for i in free:
            addition = min(bound - counts[i], max(1, remaining * loads[i] // pool), rest)
            counts[i] = counts[i] + addition
            rest = rest - addition
    return np.array([bound] + counts)


def ragged(stream_key, amount, total, most, skew):
    if amount == 2:
        one = jax.random.randint(stream_key, (), max(1, total - most), min(most, total - 1) + 1)
        return jnp.stack([one, total - one])
    tallies = jnp.asarray(split_up(amount, total, most, skew), jnp.int32)
    couples = (amount - 1) // 2
    giver, taker = tallies[1:1 + 2 * couples:2], tallies[2:2 + 2 * couples:2]
    margin = jnp.minimum(giver - 1, most - taker)
    passed = jax.random.randint(jax.random.fold_in(stream_key, 1), (couples,), 0, 1 << 20) % (margin + 1)
    tallies = tallies.at[1:1 + 2 * couples:2].set(giver - passed).at[2:2 + 2 * couples:2].set(taker + passed)
    return tallies[jax.random.permutation(jax.random.fold_in(stream_key, 2), amount)]


def noise(rng, extent, deviation, bound, cuts=(), held_as=jnp.bfloat16):
    drawn = jax.random.normal(rng, extent, jnp.float32) * deviation
    if len(cuts) > 0:
        drawn = steps_of(rng, extent, cuts, -0.22, 0.18) * drawn
    return jnp.clip(drawn, min=-bound, max=bound).astype(held_as)


def setup_inputs(seed: int = 0) -> dict:
    streams_of = jax.random.split(jax.random.key(seed), 14)
    tokens = noise(streams_of[0], (TOKENS, D), 1.0, 6.0, ((0, 8),))
    segments = jax.vmap(lambda own: jnp.searchsorted(jnp.cumsum(ragged(own, 5, ROW_LEN, ROW_LEN * 3 // 8, 1)), jnp.arange(ROW_LEN), side="right"))(jax.random.split(streams_of[1], ROWS)).reshape((ROWS, ROW_LEN)).astype(jnp.int32)
    qkv_weight = noise(streams_of[2], (2 * D, 3 * D), D ** -0.5, 0.1875, ((0, 4),))
    qv_bias = noise(streams_of[3], (4 * D,), 0.5, 3.0, ((0, 4),))
    out_weight = noise(streams_of[4], (2 * D, D), (D // 32) ** -0.5, 1.0, ((0, 4),))
    out_bias = noise(streams_of[5], (2 * D,), 0.5, 3.0, ((0, 4),))
    up_weight = noise(streams_of[6], (2 * D, FF), D ** -0.5, 0.1875, ((0, 4),))
    up_bias = noise(streams_of[7], (2 * FF,), 0.5, 3.0, ((0, 4),))
    down_weight = noise(streams_of[8], (2 * FF, D), (FF // 2) ** -0.5, 0.125, ((0, 4),))
    down_bias = noise(streams_of[9], (2 * D,), 0.5, 3.0, ((0, 4),))
    norm_gain = jnp.clip(1.0 + 0.18 * jax.random.normal(streams_of[10], (4, D), jnp.float32), 0.1, 1.9)
    norm_shift = noise(streams_of[11], (4, D), 0.3, 2.0, ((0, 4),), jnp.float32)
    cotangent = noise(streams_of[12], (TOKENS, D), 1.0, 6.0, ((0, 8),))
    return {"tokens": tokens, "segments": segments, "qkv_weight": qkv_weight, "qv_bias": qv_bias, "out_weight": out_weight, "out_bias": out_bias, "up_weight": up_weight, "up_bias": up_bias, "down_weight": down_weight, "down_bias": down_bias, "norm_gain": norm_gain, "norm_shift": norm_shift, "cotangent": cotangent}


HIGHEST_PRECISION = lax.Precision.HIGHEST
EPSILON = 1e-06

@jax.custom_vjp
def low(v):
    return lax.optimization_barrier(v.astype(jnp.bfloat16)).astype(jnp.float32)

@jax.custom_vjp
def low_back(v):
    return v

def low_keep(v):
    return (low(v), None)

def low_pass(kept, grad):
    return (grad,)

def back_keep(v):
    return (v, None)

def back_low(kept, grad):
    return (low(grad),)
low.defvjp(low_keep, low_pass)
low_back.defvjp(back_keep, back_low)

def layer_norm(values, gain_vector, shift_vector):
    center = values - lax.optimization_barrier(jnp.mean(values, axis=-1, keepdims=True))
    spread = lax.optimization_barrier(jnp.mean(center * center, axis=-1, keepdims=True))
    return center * lax.rsqrt(spread + EPSILON) * gain_vector + shift_vector

def carry_on(values):
    return low(low_back(values))

def attention(residual, seg_ids, w_qkv, b_qv, w_out, b_out, gain_vector, shift_vector):
    row_count, length, model_width = residual.shape
    head_dim = model_width // HEADS
    normed = low(layer_norm(residual, gain_vector, shift_vector))
    projected = jnp.einsum('bld,de->ble', normed, w_qkv, precision=HIGHEST_PRECISION)
    queries = low(low_back(projected[..., :model_width] + b_qv[:model_width]))
    key_rows = low(low_back(projected[..., model_width:2 * model_width]))
    values = low(low_back(projected[..., 2 * model_width:] + b_qv[model_width:]))
    queries = queries.reshape(row_count, length, HEADS, head_dim)
    key_rows = key_rows.reshape(row_count, length, HEADS, head_dim)
    values = values.reshape(row_count, length, HEADS, head_dim)
    scores = low_back(jnp.einsum('bqhd,bkhd->bhqk', queries, key_rows, precision=HIGHEST_PRECISION) * head_dim ** (-0.5))
    allowed = (seg_ids[:, :, None] == seg_ids[:, None, :])[:, None]
    scores = jnp.where(allowed, scores, -1e+30)
    softmax_weights = low(jax.nn.softmax(scores, axis=-1))
    attended = jnp.einsum('bhqk,bkhd->bqhd', softmax_weights, values, precision=HIGHEST_PRECISION)
    attended = low(low_back(attended.reshape(row_count, length, model_width)))
    return residual + jnp.einsum('bld,de->ble', attended, w_out, precision=HIGHEST_PRECISION) + b_out

def feed_forward(residual, w_up, b_up, w_down, b_down, gain_vector, shift_vector):
    normed = low(layer_norm(residual, gain_vector, shift_vector))
    hidden = low_back(jnp.einsum('bld,df->blf', normed, w_up, precision=HIGHEST_PRECISION) + b_up)
    active = low(jax.nn.gelu(hidden, approximate=False))
    return residual + jnp.einsum('blf,fd->bld', active, w_down, precision=HIGHEST_PRECISION) + b_down

def forward_block(block_tokens, params, seg_ids):
    qkv_all, qv_all, out_all, ob_all, up_all, ub_all, down_all, db_all, gain_all, shift_all = params
    residual = block_tokens
    for layer_index in range(2):
        rows_d = slice(layer_index * D, (layer_index + 1) * D)
        rows_f = slice(layer_index * FF, (layer_index + 1) * FF)
        rows_qv = slice(layer_index * 2 * D, (layer_index + 1) * 2 * D)
        residual = carry_on(attention(residual, seg_ids, qkv_all[rows_d], qv_all[rows_qv], out_all[rows_d], ob_all[rows_d], gain_all[2 * layer_index], shift_all[2 * layer_index]))
        residual = carry_on(feed_forward(residual, up_all[rows_d], ub_all[rows_f], down_all[rows_f], db_all[rows_d], gain_all[2 * layer_index + 1], shift_all[2 * layer_index + 1]))
    return residual

def reference(tokens, segments, qkv_weight, qv_bias, out_weight, out_bias, up_weight, up_bias, down_weight, down_bias, norm_gain, norm_shift, cotangent):
    params = tuple((array.astype(jnp.float32) for array in (qkv_weight, qv_bias, out_weight, out_bias, up_weight, up_bias, down_weight, down_bias, norm_gain, norm_shift)))
    rows_all = segments.shape[0]
    block_rows = math.gcd(rows_all, 8)
    blocks = rows_all // block_rows
    token_blocks = tokens.astype(jnp.float32).reshape(blocks, block_rows, ROW_LEN, D)
    seg_blocks = segments.reshape(blocks, block_rows, ROW_LEN)
    cot_blocks = cotangent.astype(jnp.float32).reshape(blocks, block_rows, ROW_LEN, D)

    def one_block(totals, pieces):
        part_tokens, part_segs, part_cot = pieces
        outputs, pullback = jax.vjp(lambda tok_vals, par_vals: forward_block(tok_vals, par_vals, part_segs), part_tokens, params)
        grad_tokens, grad_params = pullback(part_cot)
        return (jax.tree.map(jnp.add, totals, grad_params), (outputs, grad_tokens))
    zeros = jax.tree.map(jnp.zeros_like, params)
    gradients, (outputs_all, grads_all) = lax.scan(one_block, zeros, (token_blocks, seg_blocks, cot_blocks))
    block_output = outputs_all.reshape(TOKENS, D).astype(jnp.bfloat16)
    input_gradient = grads_all.reshape(TOKENS, D).astype(jnp.bfloat16)
    return (block_output, input_gradient, gradients[0], gradients[1], gradients[2], gradients[3], gradients[4], gradients[5], gradients[6], gradients[7], gradients[8], gradients[9])
```

```python
import jax
import jax.numpy as jnp
from jax import lax
from jax.sharding import PartitionSpec as P

HEADS = 16
ROW_LEN = 256
EPSILON = 1e-06
BF = jnp.bfloat16
F32 = jnp.float32


def layer_norm(values, gain_vector, shift_vector):
    center = values - jnp.mean(values, axis=-1, keepdims=True)
    spread = jnp.mean(center * center, axis=-1, keepdims=True)
    return center * lax.rsqrt(spread + EPSILON) * gain_vector + shift_vector


def core_swap(x):
    return lax.ppermute(x, "section", [(i, i ^ 1) for i in range(lax.axis_size("section"))])


def x_hop(x, pairs):
    return lax.ppermute(x, "section", pairs)


def y_swap(x):
    return lax.ppermute(x, "dp", [(i, i ^ 1) for i in range(lax.axis_size("dp"))])


def pick(x, index, axis=0):
    return lax.dynamic_index_in_dim(x, index, axis, keepdims=False)


def line_sum(blocks, place):
    count = blocks.shape[0]
    received = None
    total = pick(blocks, place).astype(F32)
    for step in range(count - 1):
        length = count - 1 - step
        rightward = place == step
        out = lax.dynamic_slice_in_dim(blocks, jnp.where(rightward, step + 1, 0), length, 0)
        if received is not None:
            part = lax.dynamic_slice_in_dim(received, jnp.where(rightward, 1, 0), length, 0)
            out = (out.astype(F32) + part.astype(F32)).astype(BF)
        pairs = []
        for source, target in ((step, step + 1), (count - 1 - step, count - 2 - step)):
            pairs += [(2 * source + y, 2 * target + y) for y in range(2)]
        received = lax.ppermute(out, "dp", pairs)
        from_left = place == step + 1
        total = total + pick(received, jnp.where(from_left, 0, length - 1)).astype(F32)
    return total


def sum_y_first(chunk, y, z):
    got = y_swap(pick(chunk, 1 - y, 1))
    mine = (pick(chunk, y, 1).astype(F32) + got.astype(F32)).astype(BF)
    return line_sum(mine, z)


def sum_z_first(chunk, y, z):
    mine = line_sum(chunk, z)
    got = y_swap(pick(mine, 1 - y).astype(BF))
    return pick(mine, y) + got.astype(F32)


def attention_forward(x, seg, w):
    w_qkv, b_qv, w_out, b_out, gain, shift = w
    d = x.shape[1]
    dh = d // HEADS
    r = x.astype(F32)
    a = layer_norm(r, gain, shift).astype(BF)
    joint = jnp.dot(a, w_qkv, preferred_element_type=F32)
    bias = jnp.concatenate([b_qv[:d], jnp.zeros_like(b_qv[:d]), b_qv[d:]])
    qkv = (joint + bias).astype(BF)
    q, k, v = (qkv[:, i * d : (i + 1) * d].reshape(-1, HEADS, dh) for i in range(3))
    p = softmax_of(q, k, seg)
    o = jnp.einsum("hqk,khd->qhd", p.astype(BF), v, preferred_element_type=F32)
    o = o.reshape(-1, d).astype(BF)
    y = (r + jnp.dot(o, w_out, preferred_element_type=F32) + b_out).astype(BF)
    return y, (x, a, qkv, o)


def softmax_of(q, k, seg):
    s = jnp.einsum("qhd,khd->hqk", q, k, preferred_element_type=F32) * q.shape[-1] ** -0.5
    s = jnp.where((seg[:, None] == seg[None, :])[None], s, -1e30)
    e = jnp.exp(s - jnp.max(s, axis=-1, keepdims=True))
    return e / jnp.sum(e, axis=-1, keepdims=True)


def norm_backward(x, da, gain, shift, g):
    _, pullback = jax.vjp(layer_norm, x.astype(F32), gain, shift)
    dr, dgain, dshift = pullback(da)
    return (g.astype(F32) + dr).astype(BF), dgain, dshift


def attention_backward(g, seg, saved, w):
    w_qkv, b_qv, w_out, b_out, gain, shift = w
    x, a, qkv, o = saved
    d = x.shape[1]
    dh = d // HEADS
    q, k, v = (qkv[:, i * d : (i + 1) * d].reshape(-1, HEADS, dh) for i in range(3))
    p = softmax_of(q, k, seg)
    do = lax.dot_general(g, w_out, (((1,), (1,)), ((), ())), preferred_element_type=F32)
    do = do.astype(BF).reshape(-1, HEADS, dh)
    dp = jnp.einsum("qhd,khd->hqk", do, v, preferred_element_type=F32)
    dv = jnp.einsum("hqk,qhd->khd", p.astype(BF), do, preferred_element_type=F32)
    ds = (p * (dp - jnp.sum(p * dp, axis=-1, keepdims=True))).astype(BF)
    scale = dh**-0.5
    dq = jnp.einsum("hqk,khd->qhd", ds, k, preferred_element_type=F32) * scale
    dk = jnp.einsum("hqk,qhd->khd", ds, q, preferred_element_type=F32) * scale
    dqkv = jnp.concatenate([m.reshape(-1, d).astype(BF) for m in (dq, dk, dv)], axis=1)
    da = lax.dot_general(dqkv, w_qkv, (((1,), (1,)), ((), ())), preferred_element_type=F32)
    return norm_backward(x, da, gain, shift, g) + (dqkv,)


def mlp_forward(x, w):
    w_up, b_up, w_down, b_down, gain, shift = w
    r = x.astype(F32)
    a = layer_norm(r, gain, shift).astype(BF)
    u = jnp.dot(a, w_up, preferred_element_type=F32) + b_up
    phi = 0.5 * (1.0 + lax.erf(u * 0.5**0.5))
    g = (u * phi).astype(BF)
    slope = (phi + u * jnp.exp(-0.5 * u * u) * (2 * jnp.pi) ** -0.5).astype(BF)
    y = (r + jnp.dot(g, w_down, preferred_element_type=F32) + b_down).astype(BF)
    return y, (x, a, g, slope)


def mlp_backward(g, saved, w):
    w_up, b_up, w_down, b_down, gain, shift = w
    x, a, act, slope = saved
    dg = lax.dot_general(g, w_down, (((1,), (1,)), ((), ())), preferred_element_type=F32)
    du = (dg * slope.astype(F32)).astype(BF)
    da = lax.dot_general(du, w_up, (((1,), (1,)), ((), ())), preferred_element_type=F32)
    return norm_backward(x, da, gain, shift, g) + (du,)


def weight_grad(left, right):
    return lax.dot_general(left, right, (((0,), (0,)), ((), ())), preferred_element_type=F32).astype(BF)


def per_device(
    tokens, segments, qkv_weight, qv_bias, out_weight, out_bias, up_weight, up_bias, down_weight, down_bias,
    norm_gain, norm_shift, cotangent,
):
    d = tokens.shape[1]
    ff = up_weight.shape[1]
    section = lax.axis_index("section")
    core, x = section % 2, section // 2
    dp = lax.axis_index("dp")
    y, z = dp % 2, dp // 2
    zs = lax.axis_size("dp") // 2
    later = x == 1
    fwd_pairs, bwd_pairs = [(0, 2), (1, 3)], [(2, 0), (3, 1)]

    vec = jnp.concatenate(
        [m.astype(F32).reshape(-1) for m in (qv_bias, out_bias, up_bias, down_bias, norm_gain, norm_shift)]
    )
    vec_got = core_swap(vec)
    qkv_got = core_swap(qkv_weight)
    out_got = core_swap(out_weight)
    up_got = core_swap(up_weight)
    down_got = core_swap(down_weight)

    def natural(own, got):
        return jnp.where(core == 0, jnp.concatenate([own, got]), jnp.concatenate([got, own]))

    sizes = [qv_bias.shape[0], out_bias.shape[0], up_bias.shape[0], down_bias.shape[0], d, d]
    parts, at = [], 0
    for size in sizes:
        parts.append(natural(vec[at : at + size], vec_got[at : at + size]))
        at += size
    b_qv, b_out, b_up, b_down, gains, shifts = parts
    w_attn = (natural(qkv_weight, qkv_got), b_qv, natural(out_weight, out_got), b_out, gains[:d], shifts[:d])
    w_mlp = (natural(up_weight, up_got), b_up, natural(down_weight, down_got), b_down, gains[d:], shifts[d:])

    rows = lambda m: pick(m.reshape(2, ROW_LEN, d), core)
    own_tokens, own_cot = rows(tokens), rows(cotangent)
    seg = pick(segments, core)

    r1, _ = attention_forward(own_tokens, seg, w_attn)
    r2, _ = mlp_forward(r1, w_mlp)
    hopped = x_hop(r2, fwd_pairs)
    entering = jnp.where(later, hopped, own_tokens)
    r1, saved_attn = attention_forward(entering, seg, w_attn)
    r2, saved_mlp = mlp_forward(r1, w_mlp)

    g1 = mlp_backward(own_cot, saved_mlp, w_mlp)[0]
    g0 = attention_backward(g1, seg, saved_attn, w_attn)[0]
    hopped = x_hop(g0, bwd_pairs)
    g_mlp = jnp.where(later, own_cot, hopped)

    def half(m, index):
        return pick(m.reshape(m.shape[0], 2, -1), index, 1)

    def both_rows(m):
        return jnp.concatenate([m, core_swap(m)])

    def both_halves(m):
        return jnp.concatenate([half(m, core), core_swap(half(m, 1 - core))])

    def blocks(m):
        return m.reshape((zs, 2, m.shape[0] // (2 * zs)) + m.shape[1:])

    act_all = both_halves(saved_mlp[2])
    a_mlp_all = both_halves(saved_mlp[1])
    o_all = both_halves(saved_attn[3])
    a_attn_all = both_halves(saved_attn[1])

    d_down = weight_grad(act_all, both_rows(g_mlp))
    down_a = sum_z_first(blocks(d_down[:, : d // 2]), y, z)
    down_b = sum_y_first(blocks(d_down[:, d // 2 :]), y, z)
    g_attn, dgain_mlp, dshift_mlp, du = mlp_backward(g_mlp, saved_mlp, w_mlp)
    d_up = weight_grad(a_mlp_all, both_rows(du))
    up_a = sum_y_first(blocks(d_up[:, : ff // 2]), y, z)
    up_b = sum_y_first(blocks(d_up[:, ff // 2 :]), y, z)
    d_out = weight_grad(o_all, both_rows(g_attn))
    g_in, dgain_attn, dshift_attn, dqkv = attention_backward(g_attn, seg, saved_attn, w_attn)
    d_qkv = weight_grad(a_attn_all, both_rows(dqkv))
    qkv_a = sum_y_first(blocks(d_qkv[:, : 2 * d]), y, z)
    qkv_b = sum_y_first(blocks(jnp.concatenate([d_qkv[:, 2 * d :], d_out], axis=1)), y, z)

    total = lambda m: jnp.sum(m.astype(F32), axis=0)
    dq_sum = total(dqkv)
    pieces = [
        jnp.concatenate([dq_sum[:d], dq_sum[2 * d :]]),
        total(g_attn),
        total(du),
        total(g_mlp),
        jnp.concatenate([dgain_attn, dgain_mlp]),
        jnp.concatenate([dshift_attn, dshift_mlp]),
    ]
    n_dp = 2 * zs
    small = jnp.concatenate([m.reshape(2, n_dp, -1) for m in pieces], axis=2)
    small = pick(small, core) + core_swap(pick(small, 1 - core))
    small = lax.psum_scatter(small.reshape(-1), "dp", scatter_dimension=0, tiled=True)
    vectors, at = [], 0
    for m in pieces:
        width = m.shape[0] // (2 * n_dp)
        vectors.append(small[at : at + width])
        at += width
    g_qv, g_out_b, g_up_b, g_down_b, g_gain, g_shift = vectors

    def columns(here, there, keep_side):
        mine = jnp.where(keep_side, here, there)
        own, other = half(mine, core), core_swap(half(mine, 1 - core))
        return jnp.where(core == 0, jnp.concatenate([own, other]), jnp.concatenate([other, own]))

    crossing = jnp.where(later, r2[:, : d // 2], g_in[:, d // 2 :])
    crossed = x_hop(crossing, fwd_pairs + bwd_pairs)
    block_output = columns(r2[:, d // 2 :], crossed, later)
    input_gradient = columns(g_in[:, : d // 2], crossed, jnp.logical_not(later))
    return (
        block_output,
        input_gradient,
        jnp.concatenate([qkv_a, qkv_b[:, :d]], axis=1),
        g_qv,
        qkv_b[:, d:],
        g_out_b,
        jnp.concatenate([up_a, up_b], axis=1),
        g_up_b,
        jnp.concatenate([down_a, down_b], axis=1),
        g_down_b,
        g_gain[None],
        g_shift[None],
    )


def solution(mesh):
    placed = (
        P("dp", None), P("dp", None), P("section", None), P("section"), P("section", None), P("section"),
        P("section", None), P("section"), P("section", None), P("section"), P("section", None), P("section", None),
        P("dp", None),
    )
    both = ("section", "dp")
    return jax.shard_map(
        per_device,
        mesh=mesh,
        in_specs=placed,
        out_specs=(
            P("dp", "section"), P("dp", "section"), P(both, None), P(both), P(both, None), P(both), P(both, None),
            P(both), P(both, None), P(both), P("section", "dp"), P("section", "dp"),
        ),
        check_vma=False,
    )
```

```python
import jax
import jax.numpy as jnp
from jax import lax
from jax.experimental import pallas as pl
from jax.experimental.pallas import tpu as pltpu
from jax.sharding import PartitionSpec as P

HEADS = 16
EPSILON = 1e-06
BF = jnp.bfloat16
F32 = jnp.float32
VMEM_BYTES = 60 * 1024 * 1024


def dot(a, b):
    return jnp.dot(a, b, preferred_element_type=F32)


def dot_t(a, b):
    return lax.dot_general(a, b, (((1,), (1,)), ((), ())), preferred_element_type=F32)


def t_dot(a, b):
    return lax.dot_general(a, b, (((0,), (0,)), ((), ())), preferred_element_type=F32)


def centered(x):
    r = x.astype(F32)
    center = r - jnp.mean(r, axis=-1, keepdims=True)
    spread = jnp.mean(center * center, axis=-1, keepdims=True)
    scale = lax.rsqrt(spread + EPSILON)
    return center * scale, scale


def call(kernel, steps, core, ins, in_specs, outs, out_specs, scratch, flops, bytes_, name, vmem=VMEM_BYTES):
    return pl.pallas_call(
        kernel,
        grid_spec=pltpu.PrefetchScalarGridSpec(
            num_scalar_prefetch=1, grid=(steps,), in_specs=in_specs, out_specs=out_specs, scratch_shapes=scratch
        ),
        out_shape=outs,
        compiler_params=pltpu.CompilerParams(vmem_limit_bytes=vmem, dimension_semantics=("arbitrary",)),
        cost_estimate=pl.CostEstimate(flops=0, bytes_accessed=0, transcendentals=0),
        name=name,
    )(core.reshape(-1).astype(jnp.int32), *ins)


def whole(a):
    return pl.BlockSpec(a.shape, lambda j, c, n=a.ndim: (0,) * n)


HBM = pl.BlockSpec(memory_space=pl.ANY)


class Fetch:
    def __init__(self, core, sems):
        self.core, self.sems, self.used = core, sems, 0

    def start(self, source, target):
        copy = pltpu.make_async_copy(source, target, self.sems.at[self.used])
        self.used += 1
        copy.start()
        return [copy]

    def columns(self, own, got, target, first, width):
        half = own.shape[0]
        cols = pl.ds(first, width)
        out = []
        for source, at in ((own, self.core), (got, 1 - self.core)):
            rows = pl.ds(pl.multiple_of(at * half, half), half)
            out += self.start(source.at[:, cols], target.at[rows, cols])
        return out

    def rows(self, own, got, target, first, count):
        half = own.shape[0]
        there = target.at[pl.ds(first, count)]
        here = pl.ds(first % half, count)
        sem = self.sems.at[self.used]
        self.used += 1
        mine = self.core == first // half

        @pl.when(mine)
        def _():
            pltpu.make_async_copy(own.at[here], there, sem).start()

        @pl.when(jnp.logical_not(mine))
        def _():
            pltpu.make_async_copy(got.at[here], there, sem).start()

        return [pltpu.make_async_copy(own.at[here], there, sem)]


def wait(copies):
    for copy in copies:
        copy.wait()


def kept_or_sent(core, index, value, keep, send):
    @pl.when(core == index)
    def _():
        keep[...] = value

    @pl.when(core != index)
    def _():
        send[...] = value


def shapes(*pairs):
    return [jax.ShapeDtypeStruct(shape, dtype) for shape, dtype in pairs]


def attention_forward(core, x, seg, w, save):
    (qkv_own, qkv_got), bias, (out_own, out_got), b_out, gain, shift = w
    t, d = x.shape
    groups = 4
    gw = d // groups
    dh = d // HEADS
    per = HEADS // groups

    def kernel(core_ref, x_ref, seg_r, seg_c, qo, qg, oo, og, bqv, bo, gain_ref, shift_ref, *refs):
        outs, (w_qkv, w_out, sems) = refs[:-3], refs[-3:]
        y_ref = outs[0]
        c = core_ref[0]
        fetch = Fetch(c, sems)
        need = []
        for j in range(groups):
            need.append([])
            for i in range(3):
                need[j] += fetch.columns(qo, qg, w_qkv, i * d + j * gw, gw)
        need_out = []
        for j in range(2):
            need_out += fetch.rows(oo, og, w_out, j * (d // 2), d // 2)
        xhat, _ = centered(x_ref[...])
        a = (xhat * gain_ref[...] + shift_ref[...]).astype(BF)
        if save:
            _, a_keep, a_send, qkv_ref, p_ref, o_keep, o_send = outs
            for i in range(2):
                kept_or_sent(c, i, a[:, i * (d // 2) : (i + 1) * (d // 2)], a_keep, a_send)
        mask = jnp.where(seg_r[...] == seg_c[...], 0.0, -1e30)
        head = lax.broadcasted_iota(jnp.int32, (1, gw), 1) // dh
        zero = jnp.zeros((), BF)
        o_all = []
        for j in range(groups):
            wait(need[j])
            cols = [slice(i * d + j * gw, i * d + (j + 1) * gw) for i in range(3)]
            q, k, v = (dot(a, w_qkv[:, s]) for s in cols)
            q = (q + bqv[:, j * gw : (j + 1) * gw]).astype(BF)
            k = k.astype(BF)
            v = (v + bqv[:, d + j * gw : d + (j + 1) * gw]).astype(BF)
            if save:
                for i, m in enumerate((q, k, v)):
                    qkv_ref[:, cols[i]] = m
            q = q * jnp.asarray(dh**-0.5, BF)
            o = None
            for h in range(per):
                s = dot_t(k, jnp.where(head == h, q, zero)) + mask
                e = jnp.exp(s - jnp.max(s, axis=0, keepdims=True))
                p = (e * (1.0 / jnp.sum(e, axis=0, keepdims=True))).astype(BF)
                if save:
                    p_ref[j * per + h] = p
                part = t_dot(p, jnp.where(head == h, v, zero))
                o = part if o is None else o + part
            o_all.append(o.astype(BF))
        o = jnp.concatenate(o_all, axis=1)
        if save:
            for i in range(2):
                kept_or_sent(c, i, o[:, i * (d // 2) : (i + 1) * (d // 2)], o_keep, o_send)
        wait(need_out)
        y_ref[...] = (x_ref[...].astype(F32) + bo[...] + dot(o, w_out[...])).astype(BF)

    ins = [x, seg[:, None], seg[None, :], qkv_own, qkv_got, out_own, out_got]
    ins += [bias[None], b_out[None], gain[None], shift[None]]
    in_specs = [whole(m) for m in ins[:3]] + [HBM] * 4 + [whole(m) for m in ins[7:]]
    half = ((t, d // 2), BF)
    outs = shapes(((t, d), BF))
    if save:
        outs = shapes(((t, d), BF), half, half, ((t, 3 * d), BF), ((HEADS, t, t), BF), half, half)
    scratch = [pltpu.VMEM((d, 3 * d), BF), pltpu.VMEM((d, d), BF), pltpu.SemaphoreType.DMA((6 * groups + 2,))]
    out = call(kernel, 1, core, ins, in_specs, outs, [whole(m) for m in outs], scratch, 0, 0, "attention_forward")
    return out[0], (x, *out[1:])


def norm_backward(da, x, gain, g):
    xhat, scale = centered(x)
    dx = da * gain
    dr = scale * (
        dx - jnp.mean(dx, axis=-1, keepdims=True) - xhat * jnp.mean(dx * xhat, axis=-1, keepdims=True)
    )
    return (
        (g.astype(F32) + dr).astype(BF),
        jnp.sum(da * xhat, axis=0, keepdims=True),
        jnp.sum(da, axis=0, keepdims=True),
    )


PIECE = 512


def pieces_of(t, width):
    return shapes(*[((t, PIECE), BF)] * (width // PIECE))


def attention_backward(core, g, saved, w, save):
    (qkv_own, qkv_got), bias, (out_own, out_got), b_out, gain, shift = w
    x, qkv, p = saved[0], saved[3], saved[4]
    t, d = x.shape
    groups = 4
    gw = d // groups
    dh = d // HEADS
    per = HEADS // groups

    def kernel(core_ref, g_ref, x_ref, qkv_ref, p_ref, qo, qg, oo, og, gain_ref, *refs):
        outs, (w_qkv, w_out, sems) = refs[:-3], refs[-3:]
        c = core_ref[0]
        fetch = Fetch(c, sems)
        need_out = []
        for j in range(2):
            need_out += fetch.rows(oo, og, w_out, j * (d // 2), d // 2)
        need = []
        for i in range(3):
            need += fetch.columns(qo, qg, w_qkv, i * d, d)
        head = lax.broadcasted_iota(jnp.int32, (1, gw), 1) // dh
        zero = jnp.zeros((), BF)
        g_now = g_ref[...]
        add = lambda a, b: b if a is None else a + b
        wait(need_out)
        parts = [[], [], []]
        for j in range(groups):
            do = dot_t(g_now, w_out[j * gw : (j + 1) * gw, :]).astype(BF)
            q, k, v = (qkv_ref[:, i * d + j * gw : i * d + (j + 1) * gw] for i in range(3))
            dq = dk = dv = None
            for h in range(per):
                ph = p_ref[j * per + h]
                pf = ph.astype(F32)
                doh = jnp.where(head == h, do, zero)
                w_ = pf * dot_t(v, doh)
                ds = (w_ - pf * jnp.sum(w_, axis=0, keepdims=True)).astype(BF)
                dv = add(dv, dot(ph, doh))
                dk = add(dk, dot(ds, jnp.where(head == h, q, zero)))
                dq = add(dq, t_dot(ds, jnp.where(head == h, k, zero)))
            scale = dh**-0.5
            for i, m in enumerate((dq * scale, dk * scale, dv)):
                parts[i].append(m.astype(BF))
        parts = [jnp.concatenate(m, axis=1) for m in parts]
        wait(need)
        da = sum(dot_t(m, w_qkv[:, i * d : (i + 1) * d]) for i, m in enumerate(parts))
        gi, dgain, dshift = norm_backward(da, x_ref[...], gain_ref[...], g_now)
        outs[0][...] = gi
        if save:
            for ref, value in zip(outs[1:4], (dgain, dshift, jnp.sum(g_now.astype(F32), axis=0, keepdims=True))):
                ref[...] = value
            for i, m in enumerate(parts):
                outs[4][i : i + 1, :] = jnp.sum(m.astype(F32), axis=0, keepdims=True)
            n = d // PIECE
            for i in range(3 * n):
                at = i % n * PIECE
                outs[5 + i][...] = parts[i // n][:, at : at + PIECE]

    ins = [g, x, qkv, p, qkv_own, qkv_got, out_own, out_got, gain[None]]
    in_specs = [whole(m) for m in ins[:4]] + [HBM] * 4 + [whole(ins[8])]
    outs = shapes(((t, d), BF))
    if save:
        row = ((1, d), F32)
        outs += shapes(row, row, row, ((3, d), F32)) + pieces_of(t, 3 * d)
    scratch = [pltpu.VMEM((d, 3 * d), BF), pltpu.VMEM((d, d), BF), pltpu.SemaphoreType.DMA((8,))]
    return call(kernel, 1, core, ins, in_specs, outs, [whole(m) for m in outs], scratch, 0, 0, "attention_backward")


def mlp_forward(core, x, w, save):
    (up_own, up_got), b_up, (down_own, down_got), b_down, gain, shift = w
    t, d = x.shape
    ff = up_own.shape[1]
    steps = 4
    tw = ff // steps

    def kernel(core_ref, x_ref, uo, ug, do, dg, bu, bd, gain_ref, shift_ref, *refs):
        outs, (w_up, w_down, sems) = refs[:-3], refs[-3:]
        c = core_ref[0]
        fetch = Fetch(c, sems)
        need_up, need_down = [], []
        for j in range(steps):
            need_up.append(fetch.columns(uo, ug, w_up, j * tw, tw))
            need_down.append(fetch.rows(do, dg, w_down, j * tw, tw))
        xhat, _ = centered(x_ref[...])
        a = (xhat * gain_ref[...] + shift_ref[...]).astype(BF)
        if save:
            _, a_keep, a_send, act_keep, act_send, slope_ref = outs
            for i in range(2):
                kept_or_sent(c, i, a[:, i * (d // 2) : (i + 1) * (d // 2)], a_keep, a_send)
        up = lambda j: dot(a, w_up[:, j * tw : (j + 1) * tw]) + bu[:, j * tw : (j + 1) * tw]
        total = x_ref[...].astype(F32) + bd[...]
        wait(need_up[0])
        u = up(0)
        for j in range(steps):
            if j + 1 < steps:
                wait(need_up[j + 1])
            wait(need_down[j])
            later = up(j + 1) if j + 1 < steps else None
            phi = 0.5 + 0.5 * lax.erf(u * 0.5**0.5)
            act = (u * phi).astype(BF)
            if save:
                at = j % (steps // 2) * tw
                kept_or_sent(c, j // (steps // 2), act, act_keep.at[:, pl.ds(at, tw)], act_send.at[:, pl.ds(at, tw)])
                slope = phi + u * (jnp.exp(-0.5 * u * u) * (2 * jnp.pi) ** -0.5)
                slope_ref[:, j * tw : (j + 1) * tw] = slope.astype(BF)
            total += dot(act, w_down[j * tw : (j + 1) * tw, :])
            u = later
        outs[0][...] = total.astype(BF)

    ins = [x, up_own, up_got, down_own, down_got, b_up[None], b_down[None], gain[None], shift[None]]
    in_specs = [whole(x)] + [HBM] * 4 + [whole(m) for m in ins[5:]]
    outs = shapes(((t, d), BF))
    if save:
        half, wide = ((t, d // 2), BF), ((t, ff // 2), BF)
        outs = shapes(((t, d), BF), half, half, wide, wide, ((t, ff), BF))
    scratch = [pltpu.VMEM((d, ff), BF), pltpu.VMEM((ff, d), BF), pltpu.SemaphoreType.DMA((3 * steps,))]
    out = call(kernel, 1, core, ins, in_specs, outs, [whole(m) for m in outs], scratch, 0, 0, "mlp_forward")
    return out[0], (x, *out[1:])


def mlp_backward(core, g, saved, w, save):
    (up_own, up_got), b_up, (down_own, down_got), b_down, gain, shift = w
    x, slope = saved[0], saved[5]
    t, d = x.shape
    ff = up_own.shape[1]
    steps = 4
    tw = ff // steps

    def kernel(core_ref, g_ref, x_ref, s_ref, uo, ug, do, dg, gain_ref, *refs):
        outs, (w_up, w_down, sems) = refs[:-3], refs[-3:]
        c = core_ref[0]
        fetch = Fetch(c, sems)
        need_up, need_down = [], []
        for j in range(steps):
            need_down.append(fetch.rows(do, dg, w_down, j * tw, tw))
            need_up.append(fetch.columns(uo, ug, w_up, j * tw, tw))
        g_now = g_ref[...]
        da = None
        for j in range(steps):
            wait(need_down[j])
            wait(need_up[j])
            du = dot_t(g_now, w_down[j * tw : (j + 1) * tw, :]) * s_ref[:, j * tw : (j + 1) * tw].astype(F32)
            du = du.astype(BF)
            part = dot_t(du, w_up[:, j * tw : (j + 1) * tw])
            da = part if da is None else da + part
            if save:
                outs[4][:, j * tw : (j + 1) * tw] = jnp.sum(du.astype(F32), axis=0, keepdims=True)
                n = tw // PIECE
                for i in range(n):
                    outs[7 + j * n + i][...] = du[:, i * PIECE : (i + 1) * PIECE]
        gi, dgain, dshift = norm_backward(da, x_ref[...], gain_ref[...], g_now)
        outs[0][...] = gi
        if save:
            for ref, value in zip(outs[1:4], (dgain, dshift, jnp.sum(g_now.astype(F32), axis=0, keepdims=True))):
                ref[...] = value
            for i in range(2):
                outs[5 + i][...] = gi[:, i * PIECE : (i + 1) * PIECE]

    ins = [g, x, slope, up_own, up_got, down_own, down_got, gain[None]]
    in_specs = [whole(m) for m in ins[:3]] + [HBM] * 4 + [whole(ins[7])]
    outs = shapes(((t, d), BF))
    if save:
        row = ((1, d), F32)
        outs += shapes(row, row, row, ((1, ff), F32)) + pieces_of(t, d) + pieces_of(t, ff)
    scratch = [pltpu.VMEM((d, ff), BF), pltpu.VMEM((ff, d), BF), pltpu.SemaphoreType.DMA((3 * steps,))]
    return call(kernel, 1, core, ins, in_specs, outs, [whole(m) for m in outs], scratch, 0, 0, "mlp_backward")


def store_split(bit, lo, value, keep, send, cols=None):
    value = value.reshape((-1, 2, lo) + value.shape[1:])
    for at in range(2):

        @pl.when(bit == at)
        def _():
            for ref, side in ((keep, at), (send, 1 - at)):
                part = value[:, side].reshape((-1,) + value.shape[3:]).astype(ref.dtype)
                if cols is None:
                    ref[...] = part
                else:
                    ref[:, :, cols] = part


def weight_grad(dp, left, rights, blocks, bit, lo):
    l_own, l_got = left
    m = l_own.shape[1]
    widths = [r.shape[1] for r, _ in rights]
    n = sum(widths)
    count = len(rights)

    def kernel(s_ref, lo_, lg, *refs):
        ro, rg = refs[:count], refs[count : 2 * count]
        keep, send = refs[2 * count :]
        mine = (s_ref[0] >> bit) & 1
        at = 0
        left_now, left_other = lo_[...], lg[...]
        for i, width in enumerate(widths):
            out = (t_dot(left_now, ro[i][...]) + t_dot(left_other, rg[i][...])).astype(BF)
            store_split(mine, lo, out.reshape(blocks, m // blocks, width), keep, send, pl.ds(at, width))
            at += width

    outs = shapes(*[((blocks // 2, m // blocks, n), BF)] * 2)
    ins = [l_own, l_got] + [r for r, _ in rights] + [r for _, r in rights]
    return call(
        kernel, 1, dp, ins, [whole(r) for r in ins], outs, [whole(r) for r in outs], [], 0, 0, "weight_grad",
        32 * 1024 * 1024,
    )


def folded(dp, mine, got, bit, lo):
    def kernel(s_ref, a, b, *outs):
        total = a[...].astype(F32) + b[...].astype(F32)
        if bit is None:
            outs[0][...] = total[0]
        else:
            store_split((s_ref[0] >> bit) & 1, lo, total, *outs)

    shape = mine.shape
    if bit is None:
        outs = shapes((shape[1:], F32))
    else:
        outs = shapes(*[((shape[0] // 2,) + shape[1:], mine.dtype)] * 2)
    ins = [mine, got]
    return call(
        kernel, 1, dp, ins, [whole(r) for r in ins], outs, [whole(r) for r in outs], [], 0, 0, "folded",
        16 * 1024 * 1024,
    )


def core_swap(x):
    return lax.ppermute(x, "section", [(i, i ^ 1) for i in range(lax.axis_size("section"))])


def x_hop(x, pairs):
    return lax.ppermute(x, "section", pairs)


def dp_swap(x, bit):
    return lax.ppermute(x, "dp", [(i, i ^ 1 << bit) for i in range(lax.axis_size("dp"))])


def pick(x, index, axis=0):
    return lax.dynamic_index_in_dim(x, index, axis, keepdims=False)


def lower(bits, k):
    return 1 << sum(b < bits[k] for b in bits[k:])


def scatter_steps(dp, bits, make):
    mine, send = make(bits[0], lower(bits, 0))
    for k, bit in enumerate(bits):
        got = yield dp_swap(send, bit), send
        if k + 1 < len(bits):
            mine, send = folded(dp, mine, got, bits[k + 1], lower(bits, k + 1))
    return folded(dp, mine, got, None, None)[0]


def all_sum_steps(x):
    x = x + (yield core_swap(x), x)
    for bit in range(lax.axis_size("dp").bit_length() - 1):
        x = x + (yield dp_swap(x, bit), x)
    return x


class Order:
    def __init__(self):
        self.last = None
        self.running = {}
        self.results = {}

    def after(self, x):
        if self.last is None:
            return x
        return lax.optimization_barrier((x, self.last))[0]

    def done(self, x):
        self.last = jax.tree.leaves(x)[0]
        return x

    def begin(self, name, steps):
        self.running[name] = (steps, next(steps)[0])

    def drain(self):
        while self.running:
            self.advance(*self.running)

    def advance(self, *names):
        for name in names:
            steps, arriving = self.running.pop(name)
            try:
                arriving, out = steps.send(self.after(arriving))
                self.running[name] = (steps, arriving)
                self.done(out)
            except StopIteration as stop:
                self.results[name] = self.done(stop.value)


def per_device(
    tokens, segments, qkv_weight, qv_bias, out_weight, out_bias, up_weight, up_bias, down_weight, down_bias,
    norm_gain, norm_shift, cotangent,
):
    d = tokens.shape[1]
    ff = up_weight.shape[1]
    t = segments.shape[1]
    section = lax.axis_index("section")
    core, x = section % 2, section // 2
    dp = lax.axis_index("dp")
    later = x == 1
    fwd_pairs, bwd_pairs = [(0, 2), (1, 3)], [(2, 0), (3, 1)]

    vec = jnp.concatenate(
        [m.astype(F32).reshape(-1) for m in (qv_bias, out_bias, up_bias, down_bias, norm_gain, norm_shift)]
    )
    vec_got = core_swap(vec)
    qkv_got = core_swap(qkv_weight)
    out_got = core_swap(out_weight)
    up_got = core_swap(up_weight)
    down_got = core_swap(down_weight)

    def natural(own, got):
        return jnp.where(core == 0, jnp.concatenate([own, got]), jnp.concatenate([got, own]))

    sizes = [qv_bias.shape[0], out_bias.shape[0], up_bias.shape[0], down_bias.shape[0], d, d]
    parts, at = [], 0
    for size in sizes:
        parts.append(natural(vec[at : at + size], vec_got[at : at + size]))
        at += size
    b_qv, b_out, b_up, b_down, gains, shifts = parts
    w_attn = ((qkv_weight, qkv_got), b_qv, (out_weight, out_got), b_out, gains[:d], shifts[:d])
    w_mlp = ((up_weight, up_got), b_up, (down_weight, down_got), b_down, gains[d:], shifts[d:])

    rows = lambda m: pick(m.reshape(2, t, d), core)
    own_tokens, own_cot = rows(tokens), rows(cotangent)
    seg = pick(segments, core)

    r1, _ = attention_forward(core, own_tokens, seg, w_attn, False)
    r2, _ = mlp_forward(core, r1, w_mlp, False)
    hopped = x_hop(r2, fwd_pairs)
    entering = jnp.where(later, hopped, own_tokens)
    r1, saved_attn = attention_forward(core, entering, seg, w_attn, True)
    r2, saved_mlp = mlp_forward(core, r1, w_mlp, True)

    a_attn_all = saved_attn[1], core_swap(saved_attn[2])
    o_all = saved_attn[5], core_swap(saved_attn[6])
    a_mlp_all = saved_mlp[1], core_swap(saved_mlp[2])
    act_all = saved_mlp[3], core_swap(saved_mlp[4])

    g1 = mlp_backward(core, own_cot, saved_mlp, w_mlp, False)[0]
    g1, act_all, a_mlp_all, o_all, a_attn_all = lax.optimization_barrier((g1, act_all, a_mlp_all, o_all, a_attn_all))
    g0 = attention_backward(core, g1, saved_attn, w_attn, False)[0]
    hopped = x_hop(g0, bwd_pairs)
    g_mlp = jnp.where(later, own_cot, hopped)

    def half(m, index):
        return lax.dynamic_slice_in_dim(m, index * (m.shape[1] // 2), m.shape[1] // 2, 1)

    def swapped(parts):
        return [(part, core_swap(part)) for part in parts]

    order = Order()
    n_dp = lax.axis_size("dp")
    y_first = list(range(n_dp.bit_length() - 1))
    z_first = y_first[1:] + y_first[:1]

    def begin(name, left, rights, bits=y_first):
        rights = order.after(rights)
        make = lambda bit, lo: order.done(weight_grad(dp, left, rights, n_dp, bit, lo))
        order.begin(name, scatter_steps(dp, bits, make))

    g_all = swapped([g_mlp[:, i : i + PIECE] for i in range(0, d, PIECE)])
    begin("down1", act_all, g_all[1:])
    begin("down0", act_all, g_all[:1], z_first)
    g_attn, dgain_mlp, dshift_mlp, g_mlp_sum, du_sum, *rest = order.done(
        mlp_backward(core, order.after(g_mlp), saved_mlp, w_mlp, True)
    )
    n = d // PIECE
    g_attn_all, du_all = swapped(rest[:n]), swapped(rest[n:])
    n = len(du_all) // 2
    begin("up0", a_mlp_all, du_all[:n])
    begin("up1", a_mlp_all, du_all[n:])
    g_in, dgain_attn, dshift_attn, g_attn_sum, dqkv_sum, *rest = order.done(
        attention_backward(core, order.after(g_attn), saved_attn, w_attn, True)
    )
    dqkv_all = swapped(rest)
    n = 2 * d // PIECE
    crossing = x_hop(jnp.where(later, r2[:, : d // 2], g_in[:, d // 2 :]), fwd_pairs + bwd_pairs)
    order.advance("down0", "down1")
    begin("qk", a_attn_all, dqkv_all[:n])
    begin("out", o_all, g_attn_all)
    begin("v", a_attn_all, dqkv_all[n:])
    order.advance("up0")
    pieces = [
        dqkv_sum[::2].reshape(-1),
        g_attn_sum[0],
        du_sum[0],
        g_mlp_sum[0],
        jnp.concatenate([dgain_attn[0], dgain_mlp[0]]),
        jnp.concatenate([dshift_attn[0], dshift_mlp[0]]),
    ]
    small = jnp.concatenate(order.after(pieces))
    order.begin("small", all_sum_steps(order.done(small)))
    order.advance("down0", "down1", "up0", "up1")
    crossing = order.after(crossing)

    def columns(here, there, keep_side):
        mine = jnp.where(keep_side, here, there)
        own, other = half(mine, core), core_swap(half(mine, 1 - core))
        return jnp.where(core == 0, jnp.concatenate([own, other]), jnp.concatenate([other, own]))

    block_output = columns(r2[:, d // 2 :], crossing, later)
    input_gradient = columns(g_in[:, : d // 2], crossing, jnp.logical_not(later))
    order.advance("small", "down1", "up0", "qk")
    block_output, input_gradient = order.done(order.after((block_output, input_gradient)))
    order.advance("up1", "small", "out", "qk", "v", "small", "down0", "out", "up1", "v", "small", "qk", "out", "v")
    order.drain()
    done = order.results
    vectors, at = [], 0
    for m in pieces:
        width = m.shape[0] // (2 * n_dp)
        vectors.append(lax.dynamic_slice_in_dim(done["small"], at + (core * n_dp + dp) * width, width))
        at += m.shape[0]
    g_qv, g_out_b, g_up_b, g_down_b, g_gain, g_shift = vectors
    return (
        block_output,
        input_gradient,
        jnp.concatenate([done["qk"], done["v"]], axis=1),
        g_qv,
        done["out"],
        g_out_b,
        jnp.concatenate([done["up0"], done["up1"]], axis=1),
        g_up_b,
        jnp.concatenate([done["down0"], done["down1"]], axis=1),
        g_down_b,
        g_gain[None],
        g_shift[None],
    )


def solution(mesh):
    placed = (
        P("dp", None), P("dp", None), P("section", None), P("section"), P("section", None), P("section"),
        P("section", None), P("section"), P("section", None), P("section"), P("section", None), P("section", None),
        P("dp", None),
    )
    both = ("section", "dp")
    return jax.shard_map(
        per_device,
        mesh=mesh,
        in_specs=placed,
        out_specs=(
            P("dp", "section"), P("dp", "section"), P(both, None), P(both), P(both, None), P(both), P(both, None),
            P(both), P(both, None), P(both), P("section", "dp"), P("section", "dp"),
        ),
        check_vma=False,
    )
```

```python
import jax
import jax.numpy as jnp
from jax import lax
from jax.experimental import pallas as pl
from jax.experimental.pallas import tpu as pltpu
from jax.sharding import PartitionSpec as P

HEADS = 16
EPSILON = 1e-06
BF = jnp.bfloat16
F32 = jnp.float32
MIB = 1024 * 1024
PIECE = 512
HBM = pl.BlockSpec(memory_space=pl.ANY)


def dot(a, b):
    return jnp.dot(a, b, preferred_element_type=F32)


def dot_t(a, b):
    return lax.dot_general(a, b, (((1,), (1,)), ((), ())), preferred_element_type=F32)


def t_dot(a, b):
    return lax.dot_general(a, b, (((0,), (0,)), ((), ())), preferred_element_type=F32)


def whole(a):
    return pl.BlockSpec(a.shape, lambda j, c, n=a.ndim: (0,) * n)


def shapes(*pairs):
    return [jax.ShapeDtypeStruct(shape, dtype) for shape, dtype in pairs]


def call(kernel, scalars, ins, in_specs, outs, out_specs, scratch, name, mib=60):
    return pl.pallas_call(
        kernel,
        grid_spec=pltpu.PrefetchScalarGridSpec(
            num_scalar_prefetch=1, grid=(1,), in_specs=in_specs, out_specs=out_specs, scratch_shapes=scratch
        ),
        out_shape=outs,
        compiler_params=pltpu.CompilerParams(vmem_limit_bytes=mib * MIB, dimension_semantics=("arbitrary",)),
        cost_estimate=pl.CostEstimate(flops=0, bytes_accessed=0, transcendentals=0),
        name=name,
    )(scalars, *ins)


class Copies:
    def __init__(self, core, sems):
        self.core, self.sems, self.used, self.leaving = core, sems, 0, []

    def start(self, source, target):
        copy = pltpu.make_async_copy(source, target, self.sems.at[self.used])
        self.used += 1
        copy.start()
        return [copy]

    def columns(self, own, got, target, first, width):
        half = own.shape[0]
        cols = pl.ds(first, width)
        out = []
        for source, at in ((own, self.core), (got, 1 - self.core)):
            rows = pl.ds(pl.multiple_of(at * half, half), half)
            out += self.start(source.at[:, cols], target.at[rows, cols])
        return out

    def either(self, first, source, other, target):
        sem = self.sems.at[self.used]
        self.used += 1

        @pl.when(first)
        def _():
            pltpu.make_async_copy(source, target, sem).start()

        @pl.when(jnp.logical_not(first))
        def _():
            pltpu.make_async_copy(other, target, sem).start()

        return [pltpu.make_async_copy(source, target, sem)]

    def rows(self, own, got, target, first, count):
        half = own.shape[0]
        here = pl.ds(first % half, count)
        return self.either(self.core == first // half, own.at[here], got.at[here], target.at[pl.ds(first, count)])

    def leave(self, source, target):
        self.leaving += self.start(source, target)

    def leave_halves(self, source, keep, send):
        half = source.shape[1] // 2
        for target, at in ((keep, self.core), (send, 1 - self.core)):
            self.leave(source.at[:, pl.ds(pl.multiple_of(at * half, half), half)], target)

    def finish(self):
        wait(self.leaving)


def wait(copies):
    for copy in copies:
        copy.wait()


def natural(core, own, got):
    return jnp.concatenate([jnp.where(core == 0, own, got), jnp.where(core == 0, got, own)], axis=-1).astype(F32)


def first_of(core, own, got):
    return jnp.where(core == 0, own, got).astype(F32)


class Chosen:
    def __init__(self, array=None, rows=None, other=None, at=1):
        self.arrays = [m for m in (array, rows, other) if m is not None]
        self.by_core, self.at = rows is not None, at

    def shape(self):
        return self.arrays[0].shape[-2:]

    def fetch(self, copies, scalars, refs, target):
        here = refs[0].at[scalars[0]] if self.by_core else refs[0]
        if len(self.arrays) == 1:
            return copies.start(here, target), refs[1:]
        return copies.either(scalars[1] == self.at, refs[1], here, target), refs[2:]


def centered(x):
    r = x.astype(F32)
    center = r - jnp.mean(r, axis=-1, keepdims=True)
    spread = jnp.mean(center * center, axis=-1, keepdims=True)
    scale = lax.rsqrt(spread + EPSILON)
    return center * scale, scale


def norm_backward(da, x, gain, g):
    xhat, scale = centered(x)
    dx = da * gain
    dr = scale * (
        dx - jnp.mean(dx, axis=-1, keepdims=True) - xhat * jnp.mean(dx * xhat, axis=-1, keepdims=True)
    )
    return (
        (g.astype(F32) + dr).astype(BF),
        jnp.sum(da * xhat, axis=0, keepdims=True),
        jnp.sum(da, axis=0, keepdims=True),
    )


GROUPS = 4


def head_blocks(m, dh):
    head = lax.broadcasted_iota(jnp.int32, (1, m.shape[1]), 1) // dh
    zero = jnp.zeros((), m.dtype)
    return jnp.concatenate([jnp.where(head == h, m, zero) for h in range(m.shape[1] // dh)], axis=0)


def stacked(m, t):
    return jnp.concatenate([m[:, i : i + t] for i in range(0, m.shape[1], t)], axis=0)


class Attention:
    def __init__(self, core, vectors):
        (q0, q1), (o0, o1), (gain0, gain1), (shift0, shift1) = vectors
        self.b_q, self.b_v = first_of(core, q0, q1), first_of(core, q1, q0)
        self.b_out = natural(core, o0, o1)
        self.gain, self.shift = first_of(core, gain0, gain1), first_of(core, shift0, shift1)

    @staticmethod
    def fetch(copies, qkv, out, w_qkv, w_out, out_first=False):
        d = w_out.shape[0]
        gw = d // GROUPS
        need, need_out = [], []

        def fetch_out():
            for j in range(2):
                need_out.extend(copies.rows(*out, w_out, j * (d // 2), d // 2))

        if out_first:
            fetch_out()
        for j in range(GROUPS):
            need.append([])
            for i in range(3):
                need[j] += copies.columns(*qkv, w_qkv, i * d + j * gw, gw)
        if not out_first:
            fetch_out()
        return need, need_out

    def normed(self, x):
        xhat, _ = centered(x)
        return (xhat * self.gain + self.shift).astype(BF)

    def forward(self, x, a, seg_r, seg_c, w_qkv, w_out, need, need_out, o_s, qkv_s=None, p_s=None, left=None):
        t, d = x.shape
        gw, dh = d // GROUPS, d // HEADS
        mask = jnp.where(seg_r == seg_c, 0.0, -1e30)
        mask = jnp.concatenate([mask] * (gw // dh), axis=1)

        def project(j):
            wait(need[j])
            cols = [slice(i * d + j * gw, i * d + (j + 1) * gw) for i in range(3)]
            q, k, v = (dot(a, w_qkv[:, s]) for s in cols)
            q = (q + self.b_q[:, j * gw : (j + 1) * gw]).astype(BF)
            k = k.astype(BF)
            v = (v + self.b_v[:, j * gw : (j + 1) * gw]).astype(BF)
            if qkv_s is not None:
                for i, m in enumerate((q, k, v)):
                    qkv_s[:, cols[i]] = m
            return q, k, v

        now = project(0)
        for j in range(GROUPS):
            q, k, v = now
            s = dot_t(k, head_blocks(q * jnp.asarray(dh**-0.5, BF), dh)) + mask
            if j + 1 < GROUPS:
                now = project(j + 1)
            e = jnp.exp(s - jnp.max(s, axis=0, keepdims=True))
            p = (e * (1.0 / jnp.sum(e, axis=0, keepdims=True))).astype(BF)
            if p_s is not None:
                p_s[j] = p
                left(j)
            o_s[:, j * gw : (j + 1) * gw] = t_dot(stacked(p, t), head_blocks(v, dh)).astype(BF)
        wait(need_out)
        return (x.astype(F32) + self.b_out + dot(o_s[...], w_out[...])).astype(BF)

    def backward(self, g, x, qkv_s, p_s, w_qkv, w_out, need, need_out, need_p=None):
        t, d = g.shape
        gw, dh = d // GROUPS, d // HEADS
        wait(need_out)
        parts = [[], [], []]
        for j in range(GROUPS):
            if need_p is not None:
                wait(need_p[j])
            do = dot_t(g, w_out[j * gw : (j + 1) * gw, :]).astype(BF)
            q, k, v = (qkv_s[:, i * d + j * gw : i * d + (j + 1) * gw] for i in range(3))
            do = head_blocks(do, dh)
            p = p_s[j]
            pf = p.astype(F32)
            w_ = pf * dot_t(v, do)
            ds = (w_ - pf * jnp.sum(w_, axis=0, keepdims=True)).astype(BF)
            dv = dot(p, do)
            dk = dot(ds, head_blocks(q, dh))
            dq = t_dot(stacked(ds, t), head_blocks(k, dh))
            scale = dh**-0.5
            for i, m in enumerate((dq * scale, dk * scale, dv)):
                parts[i].append(m.astype(BF))
        parts = [jnp.concatenate(m, axis=1) for m in parts]
        for m in need:
            wait(m)
        da = sum(dot_t(m, w_qkv[:, i * d : (i + 1) * d]) for i, m in enumerate(parts))
        return norm_backward(da, x[...], self.gain, g), parts


class Mlp:
    steps = 4

    def __init__(self, core, vectors):
        (u0, u1), (d0, d1), (gain0, gain1), (shift0, shift1) = vectors
        self.b_up, self.b_down = natural(core, u0, u1), natural(core, d0, d1)
        self.gain, self.shift = first_of(core, gain1, gain0), first_of(core, shift1, shift0)

    @classmethod
    def fetch(cls, copies, up, down, w_up, w_down, down_first=False):
        tw = w_up.shape[1] // cls.steps
        need_up, need_down = [], []
        for j in range(cls.steps):
            if down_first:
                need_down.append(copies.rows(*down, w_down, j * tw, tw))
            need_up.append(copies.columns(*up, w_up, j * tw, tw))
            if not down_first:
                need_down.append(copies.rows(*down, w_down, j * tw, tw))
        return need_up, need_down

    def normed(self, x):
        xhat, _ = centered(x)
        return (xhat * self.gain + self.shift).astype(BF)

    def forward(self, x, a, w_up, w_down, need_up, need_down, act_s=None, slope_s=None):
        tw = w_up.shape[1] // self.steps

        def hidden(j):
            wait(need_up[j])
            return dot(a, w_up[:, j * tw : (j + 1) * tw]) + self.b_up[:, j * tw : (j + 1) * tw]

        total = x.astype(F32) + self.b_down
        u = hidden(0)
        for j in range(self.steps):
            cols = slice(j * tw, (j + 1) * tw)
            later = hidden(j + 1) if j + 1 < self.steps else None
            phi = 0.5 + 0.5 * lax.erf(u * 0.5**0.5)
            act = (u * phi).astype(BF)
            if act_s is not None:
                act_s[:, cols] = act
                slope_s[:, cols] = (phi + u * (jnp.exp(-0.5 * u * u) * (2 * jnp.pi) ** -0.5)).astype(BF)
            wait(need_down[j])
            total += dot(act, w_down[cols, :])
            u = later
        return total.astype(BF)

    def backward(self, g, x, slope_s, w_up, w_down, need_up, need_down, emit=None, need_slope=None):
        tw = w_up.shape[1] // self.steps

        def incoming(j):
            wait(need_down[j])
            return dot_t(g, w_down[j * tw : (j + 1) * tw, :])

        da = None
        dg = incoming(0)
        if need_slope is not None:
            wait(need_slope)
        for j in range(self.steps):
            cols = slice(j * tw, (j + 1) * tw)
            du = (dg * slope_s[:, cols].astype(F32)).astype(BF)
            dg = incoming(j + 1) if j + 1 < self.steps else None
            if emit is not None:
                emit(j, cols, du)
            wait(need_up[j])
            part = dot_t(du, w_up[:, cols])
            da = part if da is None else da + part
        return norm_backward(da, x[...], self.gain, g)


def paired(refs):
    return [(refs[i][...], refs[i + 1][...]) for i in range(0, len(refs), 2)]


def attention_forward(scalars, x, seg, w):
    t, d = x.shape()
    vectors = [m for pair in w["attention_vectors"] for m in pair]

    def kernel(s_ref, *refs):
        w_qkv, w_out, o_s, x_s, sems = refs[-5:]
        copies = Copies(s_ref[0], sems)
        need_x, refs = x.fetch(copies, s_ref, refs[:-5], x_s)
        seg_r, seg_c, qo, qg, oo, og, *refs = refs
        sub = Attention(s_ref[0], paired(refs[: len(vectors)]))
        need, need_out = sub.fetch(copies, (qo, qg), (oo, og), w_qkv, w_out)
        wait(need_x)
        x_now = x_s[...]
        y = sub.forward(x_now, sub.normed(x_now), seg_r[...], seg_c[...], w_qkv, w_out, need, need_out, o_s)
        refs[len(vectors)][...] = y

    segs = [seg[:, None], seg[None, :]]
    ins = x.arrays + segs + [*w["qkv"], *w["out"], *vectors]
    in_specs = [HBM] * len(x.arrays) + [whole(m) for m in segs] + [HBM] * 4 + [whole(m) for m in vectors]
    outs = shapes(((t, d), BF))
    scratch = [pltpu.VMEM(s, BF) for s in ((d, 3 * d), (d, d), (t, d), (t, d))]
    scratch += [pltpu.SemaphoreType.DMA((6 * GROUPS + 3,))]
    return call(kernel, scalars, ins, in_specs, outs, [whole(m) for m in outs], scratch, "attention_forward")[0]


def mlp_forward(scalars, x, w):
    t, d = x.shape()
    ff = w["up"][0].shape[1]
    vectors = [m for pair in w["mlp_vectors"] for m in pair]

    def kernel(s_ref, *refs):
        w_up, w_down, x_s, sems = refs[-4:]
        copies = Copies(s_ref[0], sems)
        need_x, refs = x.fetch(copies, s_ref, refs[:-4], x_s)
        uo, ug, do, dg, *refs = refs
        sub = Mlp(s_ref[0], paired(refs[: len(vectors)]))
        need_up, need_down = sub.fetch(copies, (uo, ug), (do, dg), w_up, w_down)
        wait(need_x)
        x_now = x_s[...]
        refs[len(vectors)][...] = sub.forward(x_now, sub.normed(x_now), w_up, w_down, need_up, need_down)

    ins = x.arrays + [*w["up"], *w["down"], *vectors]
    in_specs = [HBM] * (len(x.arrays) + 4) + [whole(m) for m in vectors]
    outs = shapes(((t, d), BF))
    scratch = [pltpu.VMEM(s, BF) for s in ((d, ff), (ff, d), (t, d))] + [pltpu.SemaphoreType.DMA((3 * Mlp.steps + 1,))]
    return call(kernel, scalars, ins, in_specs, outs, [whole(m) for m in outs], scratch, "mlp_forward")[0]


def layer(scalars, x, seg, g, w):
    t, d = x.shape()
    ff = w["up"][0].shape[1]
    vectors = [m for key in ("attention_vectors", "mlp_vectors") for pair in w[key] for m in pair]

    def kernel(s_ref, *refs):
        c = s_ref[0]
        x_s, g_s, sems = refs[-3:]
        copies = Copies(c, sems)
        need_x, refs = x.fetch(copies, s_ref, refs[:-3], x_s)
        g_refs, refs = refs[: len(g.arrays)], refs[len(g.arrays) :]
        seg_r, seg_c, qo, qg, oo, og, uo, ug, do, dg, *refs = refs
        pairs = paired(refs[: len(vectors)])
        attention, mlp = Attention(c, pairs[: len(pairs) // 2]), Mlp(c, pairs[len(pairs) // 2 :])
        refs = refs[len(vectors) :]
        y_ref, gi_ref, *refs = refs
        outs, (w_qkv, w_out, w_up, w_down, a1, qkv_s, p_s, o_s, r1, a2, act_s, slope_s) = refs[:-12], refs[-12:]
        need, need_out = attention.fetch(copies, (qo, qg), (oo, og), w_qkv, w_out)
        need_up, need_down = mlp.fetch(copies, (uo, ug), (do, dg), w_up, w_down)
        need_g, _ = g.fetch(copies, s_ref, g_refs, g_s)
        wait(need_x)
        x_now = x_s[...]
        a = attention.normed(x_now)
        a1[...] = a
        copies.leave_halves(a1, outs[0], outs[1])
        left = lambda j: copies.leave(p_s.at[j], outs[3].at[j])
        r = attention.forward(x_now, a, seg_r[...], seg_c[...], w_qkv, w_out, need, need_out, o_s, qkv_s, p_s, left)
        r1[...] = r
        copies.leave(qkv_s, outs[2])
        copies.leave_halves(o_s, outs[4], outs[5])
        copies.leave(r1, outs[6])
        a = mlp.normed(r)
        a2[...] = a
        copies.leave_halves(a2, outs[7], outs[8])
        y_ref[...] = mlp.forward(r, a, w_up, w_down, need_up, need_down, act_s, slope_s)
        copies.leave_halves(act_s, outs[9], outs[10])
        copies.leave(slope_s, outs[11])
        none = [[]] * Mlp.steps
        wait(need_g)
        g_mid, _, _ = mlp.backward(g_s[...], r1, slope_s, w_up, w_down, none, none)
        (g_in, _, _), _ = attention.backward(g_mid, x_s, qkv_s, p_s, w_qkv, w_out, [], [])
        gi_ref[...] = g_in
        copies.finish()

    segs = [seg[:, None], seg[None, :]]
    ins = x.arrays + g.arrays + segs + [*w["qkv"], *w["out"], *w["up"], *w["down"], *vectors]
    in_specs = [HBM] * len(x.arrays + g.arrays) + [whole(m) for m in segs] + [HBM] * 8 + [whole(m) for m in vectors]
    half, row, wide = ((t, d // 2), BF), ((t, d), BF), ((t, ff // 2), BF)
    probs = ((GROUPS, t, t * HEADS // GROUPS), BF)
    outs = shapes(row, row)
    saved = shapes(half, half, ((t, 3 * d), BF), probs, half, half, row, half, half, wide, wide, ((t, ff), BF))
    scratch = [pltpu.VMEM(s, BF) for s in ((d, 3 * d), (d, d), (d, ff), (ff, d))]
    scratch += [pltpu.VMEM(s, BF) for s in ((t, d), (t, 3 * d), probs[0], (t, d), (t, d), (t, d), (t, ff), (t, ff))]
    scratch += [pltpu.VMEM((t, d), BF)] * 2
    scratch += [pltpu.SemaphoreType.DMA((6 * GROUPS + 2 + 3 * Mlp.steps + 13 + GROUPS,))]
    out = call(
        kernel, scalars, ins, in_specs, outs + saved, [whole(m) for m in outs] + [HBM] * len(saved), scratch, "layer"
    )
    return out[0], out[1], out[2:]


def layer_backward(scalars, g, x, saved, w):
    t, d = x.shape()
    ff = w["up"][0].shape[1]
    vectors = [m for key in ("attention_vectors", "mlp_vectors") for pair in w[key] for m in pair]
    qkv, p, r1, slope = saved

    def kernel(s_ref, *refs):
        c = s_ref[0]
        x_s, r_s, sems = refs[-3:]
        copies = Copies(c, sems)
        x_refs, refs = refs[: len(x.arrays)], refs[len(x.arrays) : -3]
        need_g, refs = g.fetch(copies, s_ref, refs, refs[-4])
        r1_ref, qkv_ref, p_ref, slope_ref, qo, qg, oo, og, uo, ug, do, dg, *refs = refs
        pairs = paired(refs[: len(vectors)])
        attention, mlp = Attention(c, pairs[: len(pairs) // 2]), Mlp(c, pairs[len(pairs) // 2 :])
        refs = refs[len(vectors) :]
        outs, (w_qkv, w_out, w_up, w_down, qkv_s, p_s, slope_s, g_s, mid_s, du_s, dqkv_s) = refs[:-11], refs[-11:]
        g_out, mid_out, gi_ref, du_out, dqkv_out, sums = outs
        need_slope = copies.start(slope_ref, slope_s)
        need_up, need_down = mlp.fetch(copies, (uo, ug), (do, dg), w_up, w_down, True)
        need_r = copies.start(r1_ref, r_s)
        need_x, _ = x.fetch(copies, s_ref, x_refs, x_s)
        wait(need_g)
        g_now = g_s[...]
        copies.leave(g_s, g_out)
        need_p = [copies.start(qkv_ref, qkv_s)] + [[]] * (GROUPS - 1)
        need_p = [m + copies.start(p_ref.at[j], p_s.at[j]) for j, m in enumerate(need_p)]
        need, need_out = attention.fetch(copies, (qo, qg), (oo, og), w_qkv, w_out, True)
        at = 3 * d
        col_sum = lambda m: jnp.sum(m.astype(F32), axis=0, keepdims=True)

        def emit(j, cols, du):
            du_s[:, cols] = du
            part = pl.ds(cols.start, cols.stop - cols.start)
            copies.leave(du_s.at[:, part], du_out.at[:, part])
            sums[:, at + cols.start : at + cols.stop] = col_sum(du)

        wait(need_r)
        mid, gain_mlp, shift_mlp = mlp.backward(
            g_now, r_s, slope_s, w_up, w_down, need_up, need_down, emit, need_slope
        )
        mid_s[...] = mid
        copies.leave(mid_s, mid_out)
        wait(need_x)
        (gi, gain, shift), parts = attention.backward(mid, x_s, qkv_s, p_s, w_qkv, w_out, need, need_out, need_p)
        gi_ref[...] = gi
        for i, m in enumerate(parts):
            dqkv_s[:, i * d : (i + 1) * d] = m
        copies.leave(dqkv_s, dqkv_out)
        ends = at + ff
        rows = (col_sum(parts[0]), col_sum(parts[2]), col_sum(mid))
        for i, m in enumerate(rows):
            sums[:, i * d : (i + 1) * d] = m
        for i, m in enumerate((col_sum(g_now), gain, gain_mlp, shift, shift_mlp)):
            sums[:, ends + i * d : ends + (i + 1) * d] = m
        copies.finish()

    ins = x.arrays + g.arrays + [r1, qkv, p, slope, *w["qkv"], *w["out"], *w["up"], *w["down"], *vectors]
    in_specs = [HBM] * (len(x.arrays + g.arrays) + 12) + [whole(m) for m in vectors]
    row = ((t, d), BF)
    outs = shapes(row, row, row, ((t, ff), BF), ((t, 3 * d), BF), ((1, 8 * d + ff), F32))
    out_specs = [HBM, HBM, whole(outs[2]), HBM, HBM, whole(outs[5])]
    scratch = [pltpu.VMEM(s, BF) for s in ((d, 3 * d), (d, d), (d, ff), (ff, d), qkv.shape, p.shape, slope.shape)]
    scratch += [pltpu.VMEM(s, BF) for s in ((t, d), (t, d), (t, ff), (t, 3 * d), (t, d), (t, d))]
    scratch += [pltpu.SemaphoreType.DMA((7 * GROUPS + 2 + 4 * Mlp.steps + 8,))]
    return call(kernel, scalars, ins, in_specs, outs, out_specs, scratch, "layer_backward")


def weight_grads(scalars, tasks, blocks):
    arrays, specs, outs, scratch = [], [], [], []

    def index_of(m):
        for i, known in enumerate(arrays):
            if known is m:
                return i
        arrays.append(m)
        return len(arrays) - 1

    tasks = [(tuple(map(index_of, left)), tuple(map(index_of, right)), *rest) for left, right, *rest in tasks]
    lefts = sorted({i for left, *_ in tasks for i in left})
    columns = sorted({(i, c) for _, right, first, n, *_ in tasks for i in right for c in range(first, first + n, PIECE)})
    t = arrays[0].shape[0]
    for left, _, _, n, _, _ in tasks:
        rows = arrays[left[0]].shape[1] // blocks
        outs += shapes(*[((blocks // 2, rows, n), BF)] * 2)
        scratch.append(pltpu.VMEM((n // PIECE, blocks, rows, PIECE), BF))
    scratch += [pltpu.VMEM(arrays[i].shape, BF) for i in lefts] + [pltpu.VMEM((t, PIECE), BF) for _ in columns]
    leaving = sum(n // PIECE * blocks for _, _, _, n, _, _ in tasks)
    scratch += [pltpu.SemaphoreType.DMA((len(lefts) + len(columns) + leaving,))]

    def kernel(s_ref, *refs):
        refs, sems = refs[:-1], refs[-1]
        ins, refs = refs[: len(arrays)], refs[len(arrays) :]
        targets, refs = refs[: len(outs)], refs[len(outs) :]
        out_s, refs = refs[: len(tasks)], refs[len(tasks) :]
        left_s = dict(zip(lefts, refs))
        right_s = dict(zip(columns, refs[len(lefts) :]))
        copies = Copies(None, sems)
        need = {}

        def fetched(key, source, target):
            if key not in need:
                need[key] = copies.start(source, target)

        def ready(key):
            wait(need[key])
            need[key] = []

        for left, right, first, n, _, _ in tasks:
            for i in left:
                fetched(i, ins[i], left_s[i])
            for c in range(first, first + n, PIECE):
                for i in right:
                    fetched((i, c), ins[i].at[:, pl.ds(c, PIECE)], right_s[i, c])
        for k, (left, right, first, n, bit, lo) in enumerate(tasks):
            side = (s_ref[2] >> bit) & 1
            keep, send = targets[2 * k : 2 * k + 2]
            for piece in range(n // PIECE):
                c = first + piece * PIECE
                for i, j in zip(left, right):
                    ready(i)
                    ready((j, c))
                out = sum(t_dot(left_s[i][...], right_s[j, c][...]) for i, j in zip(left, right))
                out_s[k][piece] = out.astype(BF).reshape(out_s[k].shape[1:])
                for m in range(blocks // 2):
                    base = m // lo * 2 * lo + m % lo
                    for target, at in ((send, base + (1 - side) * lo), (keep, base + side * lo)):
                        copies.leave(out_s[k].at[piece, at], target.at[m, :, pl.ds(piece * PIECE, PIECE)])
        copies.finish()

    out = call(kernel, scalars, arrays, [HBM] * len(arrays), outs, [HBM] * len(outs), scratch, "weight_grads")
    return [(out[2 * k], out[2 * k + 1]) for k in range(len(tasks))]


def folded(scalars, mine, got, bit, lo):
    def kernel(s_ref, a, b, *outs):
        if bit is None:
            outs[0][...] = a[0].astype(F32) + b[0].astype(F32)
            return
        side = (s_ref[2] >> bit) & 1
        for k in range(outs[0].shape[0]):
            base = k // lo * 2 * lo + k % lo
            for ref, at in ((outs[0], base + side * lo), (outs[1], base + (1 - side) * lo)):
                ref[k] = (a[at].astype(F32) + b[at].astype(F32)).astype(ref.dtype)

    shape = mine.shape
    if bit is None:
        outs = shapes((shape[1:], F32))
    else:
        outs = shapes(*[((shape[0] // 2,) + shape[1:], mine.dtype)] * 2)
    ins = [mine, got]
    return call(kernel, scalars, ins, [whole(r) for r in ins], outs, [whole(r) for r in outs], [], "folded", 16)


def core_swap(x):
    return lax.ppermute(x, "section", [(i, i ^ 1) for i in range(lax.axis_size("section"))])


def x_hop(x, pairs):
    return lax.ppermute(x, "section", pairs)


def dp_swap(x, bit):
    return lax.ppermute(x, "dp", [(i, i ^ 1 << bit) for i in range(lax.axis_size("dp"))])


def lower(bits, k):
    return 1 << sum(b < bits[k] for b in bits[k:])


def scatter_steps(scalars, bits, mine, send):
    for k, bit in enumerate(bits):
        got = yield dp_swap(send, bit), send
        if k + 1 < len(bits):
            mine, send = folded(scalars, mine, got, bits[k + 1], lower(bits, k + 1))
    return folded(scalars, mine, got, None, None)[0]


def all_sum_steps(x):
    x = x + (yield core_swap(x), x)
    for bit in range(lax.axis_size("dp").bit_length() - 1):
        x = x + (yield dp_swap(x, bit), x)
    return x


class Order:
    def __init__(self):
        self.last = None
        self.running = {}
        self.results = {}

    def after(self, x):
        if self.last is None:
            return x
        return lax.optimization_barrier((x, self.last))[0]

    def done(self, x):
        self.last = jax.tree.leaves(x)[0]
        return x

    def begin(self, name, steps):
        self.running[name] = (steps, next(steps)[0])

    def drain(self):
        while self.running:
            self.advance(*self.running)

    def advance(self, *names):
        for name in names:
            steps, arriving = self.running.pop(name)
            try:
                arriving, out = steps.send(self.after(arriving))
                self.running[name] = (steps, arriving)
                self.done(out)
            except StopIteration as stop:
                self.results[name] = self.done(stop.value)


def per_device(
    tokens, segments, qkv_weight, qv_bias, out_weight, out_bias, up_weight, up_bias, down_weight, down_bias,
    norm_gain, norm_shift, cotangent,
):
    d = tokens.shape[1]
    t = segments.shape[1]
    section = lax.axis_index("section")
    core, x = section % 2, section // 2
    dp = lax.axis_index("dp")
    n_dp = lax.axis_size("dp")
    later = x == 1
    fwd_pairs, bwd_pairs = [(0, 2), (1, 3)], [(2, 0), (3, 1)]
    scalars = jnp.stack([core, x, dp]).astype(jnp.int32)

    both = lambda m: (m, core_swap(m))
    vec = lambda m: both(m.reshape(1, -1))
    w = {"qkv": both(qkv_weight), "out": both(out_weight)}
    gain, shift = vec(norm_gain), vec(norm_shift)
    w["attention_vectors"] = (vec(qv_bias), vec(out_bias), gain, shift)
    w["mlp_vectors"] = (vec(up_bias), vec(down_bias), gain, shift)
    (up_weight, down_weight), _ = lax.optimization_barrier(((up_weight, down_weight), w))
    w["up"], w["down"] = both(up_weight), both(down_weight)

    token_rows, cot_rows = tokens.reshape(2, t, d), cotangent.reshape(2, t, d)
    seg = lax.dynamic_index_in_dim(segments, core, 0, False)

    r1 = attention_forward(scalars, Chosen(rows=token_rows), seg, w)
    entering = Chosen(rows=token_rows, other=x_hop(mlp_forward(scalars, Chosen(r1), w), fwd_pairs))
    r2, g0, saved = layer(scalars, entering, seg, Chosen(rows=cot_rows), w)
    a1_keep, a1_send, qkv, p, o_keep, o_send, r1, a2_keep, a2_send, act_keep, act_send, slope = saved

    a1, o, a2, act = ((k, core_swap(s)) for k, s in ((a1_keep, a1_send), (o_keep, o_send), (a2_keep, a2_send), (act_keep, act_send)))

    hopped, a1, o, a2, act = lax.optimization_barrier((x_hop(g0, bwd_pairs), a1, o, a2, act))
    leaving = Chosen(rows=cot_rows, other=hopped, at=0)
    g_mlp, g_attn, g_in, du, dqkv, small = layer_backward(scalars, leaving, entering, (qkv, p, r1, slope), w)
    g_mlp = both(g_mlp)
    (g_attn, du, dqkv), _ = lax.optimization_barrier(((g_attn, du, dqkv), g_mlp))
    du, dqkv, g_attn = both(du), both(dqkv), both(g_attn)

    order = Order()
    bits = list(range(n_dp.bit_length() - 1))
    y_first, z_first, y_second = bits, bits[1:] + bits[:1], bits[1:2] + bits[:1] + bits[2:]

    def begin(*tasks):
        names, kinds, lefts, rights, firsts, widths = zip(*tasks)
        rights = order.after(rights)
        halves = [(kind[0], lower(kind, 0)) for kind in kinds]
        args = [(left, right, first, n, *h) for left, right, first, n, h in zip(lefts, rights, firsts, widths, halves)]
        for name, kind, pair in zip(names, kinds, order.done(weight_grads(scalars, args, n_dp))):
            order.begin(name, scatter_steps(scalars, kind, *pair))

    hf = up_weight.shape[1] // 2
    begin(("d1", y_first, act, g_mlp, d // 2, d // 2), ("d0", z_first, act, g_mlp, 0, d // 2))
    begin(("u0", y_first, a2, du, 0, hf), ("u1", y_first, a2, du, hf, hf))
    begin(("qk", y_first, a1, dqkv, 0, 2 * d), ("o", z_first, o, g_attn, 0, d), ("v", y_first, a1, dqkv, 2 * d, d))
    order.advance("d0", "d1", "o", "u0", "d0", "d1", "u1")
    order.begin("small", all_sum_steps(order.done(order.after(small))))

    crossed = x_hop(jnp.where(later, r2[:, : d // 2], g_in[:, d // 2 :]), fwd_pairs + bwd_pairs)

    def columns(here, there, keep_side):
        mine = jnp.where(keep_side, here, there)
        half = mine.shape[1] // 2
        part = lambda index: lax.dynamic_slice_in_dim(mine, index * half, half, 1)
        own, other = part(core), core_swap(part(1 - core))
        return jnp.where(core == 0, jnp.concatenate([own, other]), jnp.concatenate([other, own]))

    crossed = order.after(crossed)
    block_output = columns(r2[:, d // 2 :], crossed, later)
    input_gradient = columns(g_in[:, : d // 2], crossed, jnp.logical_not(later))
    order.advance("o", "u0", "d1", "qk", "small")
    block_output, input_gradient = order.done(order.after((block_output, input_gradient)))
    order.advance("u1", "v", "small", "u0", "d0", "qk", "o", "small", "v", "u1", "qk", "small", "v")
    order.drain()
    done = order.results
    vectors, at = [], 0
    small = done["small"][0]
    for width in (2 * d, d, hf * 2, d, 2 * d, 2 * d):
        part = width // (2 * n_dp)
        vectors.append(lax.dynamic_slice_in_dim(small, at + (core * n_dp + dp) * part, part))
        at += width
    g_qv, g_out_b, g_up_b, g_down_b, g_gain, g_shift = vectors
    return (
        block_output,
        input_gradient,
        jnp.concatenate([done["qk"], done["v"]], axis=1),
        g_qv,
        done["o"],
        g_out_b,
        jnp.concatenate([done["u0"], done["u1"]], axis=1),
        g_up_b,
        jnp.concatenate([done["d0"], done["d1"]], axis=1),
        g_down_b,
        g_gain[None],
        g_shift[None],
    )


def solution(mesh):
    placed = (
        P("dp", None), P("dp", None), P("section", None), P("section"), P("section", None), P("section"),
        P("section", None), P("section"), P("section", None), P("section"), P("section", None), P("section", None),
        P("dp", None),
    )
    both = ("section", "dp")
    return jax.shard_map(
        per_device,
        mesh=mesh,
        in_specs=placed,
        out_specs=(
            P("dp", "section"), P("dp", "section"), P(both, None), P(both), P(both, None), P(both), P(both, None),
            P(both), P(both, None), P(both), P("section", "dp"), P("section", "dp"),
        ),
        check_vma=False,
    )
```

```python
import jax
import jax.numpy as jnp
from jax import lax
from jax.experimental import pallas as pl
from jax.experimental.pallas import tpu as pltpu
from jax.sharding import PartitionSpec as P

HEADS = 16
EPSILON = 1e-06
BF = jnp.bfloat16
F32 = jnp.float32
MIB = 1024 * 1024
PIECE = 512
ANYWHERE = pl.BlockSpec(memory_space=pl.ANY)
IN_VMEM = pl.BlockSpec(memory_space=pltpu.VMEM)


def dot(a, b):
    return jnp.dot(a, b, preferred_element_type=F32)


def dot_t(a, b):
    return lax.dot_general(a, b, (((1,), (1,)), ((), ())), preferred_element_type=F32)


def t_dot(a, b):
    return lax.dot_general(a, b, (((0,), (0,)), ((), ())), preferred_element_type=F32)


def call(kernel, scalars, held, ins, outs, scratch, name, mib):
    return pl.pallas_call(
        kernel,
        in_specs=[pl.BlockSpec(memory_space=pltpu.SMEM)] + [IN_VMEM] * len(held) + [ANYWHERE] * len(ins),
        out_specs=[IN_VMEM] * len(outs),
        out_shape=[pltpu.VMEM(shape, dtype) for shape, dtype in outs],
        scratch_shapes=scratch,
        compiler_params=pltpu.CompilerParams(vmem_limit_bytes=mib * MIB),
        cost_estimate=pl.CostEstimate(flops=0, bytes_accessed=0, transcendentals=0),
        name=name,
    )(scalars, *held, *ins)


def rooms(*pairs):
    return [pltpu.VMEM(shape, dtype) for shape, dtype in pairs]


class Copies:
    def __init__(self, core, sems):
        self.core, self.sems, self.used = core, sems, 0

    def start(self, source, target):
        copy = pltpu.make_async_copy(source, target, self.sems.at[self.used])
        self.used += 1
        copy.start()
        return [copy]

    def columns(self, own, got, target, first, width):
        half = own.shape[0]
        cols = pl.ds(first, width)
        out = []
        for source, at in ((own, self.core), (got, 1 - self.core)):
            rows = pl.ds(pl.multiple_of(at * half, half), half)
            out += self.start(source.at[:, cols], target.at[rows, cols])
        return out

    def either(self, first, source, other, target):
        sem = self.sems.at[self.used]
        self.used += 1

        @pl.when(first)
        def _():
            pltpu.make_async_copy(source, target, sem).start()

        @pl.when(jnp.logical_not(first))
        def _():
            pltpu.make_async_copy(other, target, sem).start()

        return [pltpu.make_async_copy(source, target, sem)]

    def rows(self, own, got, target, first, count):
        half = own.shape[0]
        here = pl.ds(first % half, count)
        return self.either(self.core == first // half, own.at[here], got.at[here], target.at[pl.ds(first, count)])


def wait(copies):
    for copy in copies:
        copy.wait()


def split_halves(core, value, keep, send):
    half = value.shape[1] // 2
    low, high = value[:, :half], value[:, half:]
    keep[...] = jnp.where(core == 0, low, high)
    send[...] = jnp.where(core == 0, high, low)


def split_blocks(side, lo, value, first, keep, send, cols):
    for k in range(value.shape[0]):
        at = first + k
        if at // lo % 2 == 0:
            to, a, b = at // (2 * lo) * lo + at % lo, value[k], value[k + lo]
            keep[to, :, cols] = jnp.where(side == 0, a, b)
            send[to, :, cols] = jnp.where(side == 0, b, a)


class Chosen:
    def __init__(self, array=None, rows=None, other=None, at=1, flip=False):
        self.arrays = [m for m in (array, rows, other) if m is not None]
        self.by_core, self.at, self.flip = rows is not None, at, flip

    def shape(self):
        return self.arrays[0].shape[-2:]

    def fetch(self, copies, scalars, refs, target):
        row = 1 - scalars[0] if self.flip else scalars[0]
        here = refs[0].at[row] if self.by_core else refs[0]
        if len(self.arrays) == 1:
            return copies.start(here, target), refs[1:]
        return copies.either(scalars[1] == self.at, refs[1], here, target), refs[2:]


def centered(x):
    r = x.astype(F32)
    center = r - jnp.mean(r, axis=-1, keepdims=True)
    spread = jnp.mean(center * center, axis=-1, keepdims=True)
    scale = lax.rsqrt(spread + EPSILON)
    return center * scale, scale


def norm_backward(da, x, gain, g):
    xhat, scale = centered(x)
    dx = da * gain
    dr = scale * (
        dx - jnp.mean(dx, axis=-1, keepdims=True) - xhat * jnp.mean(dx * xhat, axis=-1, keepdims=True)
    )
    return (
        (g.astype(F32) + dr).astype(BF),
        jnp.sum(da * xhat, axis=0, keepdims=True),
        jnp.sum(da, axis=0, keepdims=True),
    )


GROUPS = 4


def head_blocks(m, dh):
    head = lax.broadcasted_iota(jnp.int32, (1, m.shape[1]), 1) // dh
    zero = jnp.zeros((), m.dtype)
    return jnp.concatenate([jnp.where(head == h, m, zero) for h in range(m.shape[1] // dh)], axis=0)


def stacked(m, t):
    return jnp.concatenate([m[:, i : i + t] for i in range(0, m.shape[1], t)], axis=0)


def vector_places(d, ff):
    names = ("q", "v", "out", "down", "gain0", "gain1", "shift0", "shift1")
    places = {name: slice(i * d, (i + 1) * d) for i, name in enumerate(names)}
    places["up"] = slice(8 * d, 8 * d + ff)
    return places


class Attention:
    def __init__(self, vectors, d, ff):
        at = vector_places(d, ff)
        self.b_q, self.b_v, self.b_out = (vectors[:, at[name]] for name in ("q", "v", "out"))
        self.gain, self.shift = vectors[:, at["gain0"]], vectors[:, at["shift0"]]

    @staticmethod
    def fetch(copies, qkv, out, w_qkv, w_out, out_first=False):
        d = w_out.shape[0]
        gw = d // GROUPS
        need, need_out = [], []

        def fetch_out():
            for j in range(2):
                need_out.extend(copies.rows(*out, w_out, j * (d // 2), d // 2))

        if out_first:
            fetch_out()
        for j in range(GROUPS):
            need.append([])
            for i in range(3):
                need[j] += copies.columns(*qkv, w_qkv, i * d + j * gw, gw)
        if not out_first:
            fetch_out()
        return need, need_out

    def normed(self, x):
        xhat, _ = centered(x)
        return (xhat * self.gain + self.shift).astype(BF)

    def forward(self, x, a, mask, w_qkv, w_out, need, need_out, o_s, qkv_s=None, p_s=None):
        t, d = x.shape
        gw, dh = d // GROUPS, d // HEADS
        mask = jnp.concatenate([mask] * (gw // dh), axis=1)

        def project(j):
            wait(need[j])
            cols = [slice(i * d + j * gw, i * d + (j + 1) * gw) for i in range(3)]
            q, k, v = (dot(a, w_qkv[:, s]) for s in cols)
            q = (q + self.b_q[:, j * gw : (j + 1) * gw]).astype(BF)
            k = k.astype(BF)
            v = (v + self.b_v[:, j * gw : (j + 1) * gw]).astype(BF)
            if qkv_s is not None:
                for i, m in enumerate((q, k, v)):
                    qkv_s[:, cols[i]] = m
            return q, k, v

        now = project(0)
        for j in range(GROUPS):
            q, k, v = now
            s = dot_t(k, head_blocks(q * jnp.asarray(dh**-0.5, BF), dh)) + mask
            if j + 1 < GROUPS:
                now = project(j + 1)
            e = jnp.exp(s - jnp.max(s, axis=0, keepdims=True))
            p = (e * (1.0 / jnp.sum(e, axis=0, keepdims=True))).astype(BF)
            if p_s is not None:
                p_s[j] = p
            o_s[:, j * gw : (j + 1) * gw] = t_dot(stacked(p, t), head_blocks(v, dh)).astype(BF)
        wait(need_out)
        return (x.astype(F32) + self.b_out + dot(o_s[...], w_out[...])).astype(BF)

    def backward(self, g, x, qkv_s, p_s, w_qkv, w_out, need, need_out, need_p=None, need_x=()):
        t, d = g.shape
        gw, dh = d // GROUPS, d // HEADS
        wait(need_out)
        parts = [[], [], []]
        for j in range(GROUPS):
            if need_p is not None:
                wait(need_p[j])
            do = dot_t(g, w_out[j * gw : (j + 1) * gw, :]).astype(BF)
            q, k, v = (qkv_s[:, i * d + j * gw : i * d + (j + 1) * gw] for i in range(3))
            do = head_blocks(do, dh)
            p = p_s[j]
            pf = p.astype(F32)
            w_ = pf * dot_t(v, do)
            ds = (w_ - pf * jnp.sum(w_, axis=0, keepdims=True)).astype(BF)
            dv = dot(p, do)
            dk = dot(ds, head_blocks(q, dh))
            dq = t_dot(stacked(ds, t), head_blocks(k, dh))
            scale = dh**-0.5
            for i, m in enumerate((dq * scale, dk * scale, dv)):
                parts[i].append(m.astype(BF))
        parts = [jnp.concatenate(m, axis=1) for m in parts]
        for m in need:
            wait(m)
        da = sum(dot_t(m, w_qkv[:, i * d : (i + 1) * d]) for i, m in enumerate(parts))
        wait(need_x)
        return norm_backward(da, x[...], self.gain, g), parts


class Mlp:
    steps = 4

    def __init__(self, vectors, d, ff):
        at = vector_places(d, ff)
        self.b_up, self.b_down = vectors[:, at["up"]], vectors[:, at["down"]]
        self.gain, self.shift = vectors[:, at["gain1"]], vectors[:, at["shift1"]]

    @classmethod
    def fetch(cls, copies, up, down, w_up, w_down, down_first=False):
        tw = w_up.shape[1] // cls.steps
        need_up, need_down = [], []
        for j in range(cls.steps):
            if down_first:
                need_down.append(copies.rows(*down, w_down, j * tw, tw))
            need_up.append(copies.columns(*up, w_up, j * tw, tw))
            if not down_first:
                need_down.append(copies.rows(*down, w_down, j * tw, tw))
        return need_up, need_down

    def normed(self, x):
        xhat, _ = centered(x)
        return (xhat * self.gain + self.shift).astype(BF)

    def forward(self, x, a, w_up, w_down, need_up, need_down, act_s=None, slope_s=None):
        tw = w_up.shape[1] // self.steps

        def hidden(j):
            wait(need_up[j])
            return dot(a, w_up[:, j * tw : (j + 1) * tw]) + self.b_up[:, j * tw : (j + 1) * tw]

        total = x.astype(F32) + self.b_down
        u = hidden(0)
        for j in range(self.steps):
            cols = slice(j * tw, (j + 1) * tw)
            later = hidden(j + 1) if j + 1 < self.steps else None
            phi = 0.5 + 0.5 * lax.erf(u * 0.5**0.5)
            act = (u * phi).astype(BF)
            if act_s is not None:
                act_s[:, cols] = act
                slope_s[:, cols] = (phi + u * (jnp.exp(-0.5 * u * u) * (2 * jnp.pi) ** -0.5)).astype(BF)
            wait(need_down[j])
            total += dot(act, w_down[cols, :])
            u = later
        return total.astype(BF)

    def backward(self, g, x, slope_s, w_up, w_down, need_up, need_down, emit=None, need_slope=(), need_x=()):
        tw = w_up.shape[1] // self.steps

        def incoming(j):
            wait(need_down[j])
            return dot_t(g, w_down[j * tw : (j + 1) * tw, :])

        da = None
        dg = incoming(0)
        wait(need_slope)
        for j in range(self.steps):
            cols = slice(j * tw, (j + 1) * tw)
            du = (dg * slope_s[:, cols].astype(F32)).astype(BF)
            dg = incoming(j + 1) if j + 1 < self.steps else None
            if emit is not None:
                emit(j, cols, du)
            wait(need_up[j])
            part = dot_t(du, w_up[:, cols])
            da = part if da is None else da + part
        wait(need_x)
        return norm_backward(da, x[...], self.gain, g)


def col_sum(m):
    return jnp.sum(m.astype(F32), axis=0, keepdims=True)


def attention_forward(scalars, x, segs, own, got, qkv, out):
    t, d = x.shape()
    ff = 2 * own.shape[1] - 8 * d

    def kernel(s_ref, *refs):
        c = s_ref[0]
        y_out, w_qkv, w_out, vectors, mask, o_s, x_s, own_s, got_s, r_s, c_s, sems = refs[-12:]
        copies = Copies(c, sems)
        need_x, refs = x.fetch(copies, s_ref, refs[:-12], x_s)
        seg_r, seg_c, own_ref, got_ref, qo, qg, oo, og = refs
        need_v = copies.start(own_ref, own_s) + copies.start(got_ref, got_s)
        need_m = copies.start(seg_r, r_s) + copies.start(seg_c, c_s)
        need, need_out = Attention.fetch(copies, (qo, qg), (oo, og), w_qkv, w_out)
        wait(need_v)
        at = vector_places(d, ff)
        low, high = jnp.where(c == 0, own_s[...], got_s[...]), jnp.where(c == 0, got_s[...], own_s[...])
        first = 0
        for names, width in (
            (("q", "v"), d), (("out",), d // 2), (("up",), ff // 2), (("down",), d // 2),
            (("gain0", "gain1"), d), (("shift0", "shift1"), d),
        ):
            places = [at[name] for name in names]
            if len(places) == 1:
                start = places[0].start
                places = [slice(start, start + width), slice(start + width, start + 2 * width)]
            for place, half in zip(places, (low, high)):
                vectors[:, place] = half[:, first : first + width]
            first += width
        wait(need_m)
        mask[...] = jnp.where(r_s[...] == c_s[...], 0.0, -1e30)
        sub = Attention(vectors, d, ff)
        wait(need_x)
        x_now = x_s[...]
        y_out[...] = sub.forward(x_now, sub.normed(x_now), mask[...], w_qkv, w_out, need, need_out, o_s)

    row = ((t, d), BF)
    ins = x.arrays + [*segs, own, got, *qkv, *out]
    outs = (row, ((d, 3 * d), BF), ((d, d), BF), ((1, 8 * d + ff), F32), ((t, t), F32))
    scratch = rooms(row, row, (own.shape, F32), (own.shape, F32), ((t, 1), jnp.int32), ((1, t), jnp.int32))
    scratch += [pltpu.SemaphoreType.DMA((6 * GROUPS + 7,))]
    return call(kernel, scalars, [], ins, outs, scratch, "attention_forward", 44)


def mlp_forward(scalars, x, vectors, up, down):
    t, d = x.shape
    ff = up[0].shape[1]

    def kernel(s_ref, vec, x_ref, uo, ug, do, dg, y_out, w_up, w_down, sems):
        need_up, need_down = Mlp.fetch(Copies(s_ref[0], sems), (uo, ug), (do, dg), w_up, w_down)
        sub = Mlp(vec, d, ff)
        x_now = x_ref[...]
        y_out[...] = sub.forward(x_now, sub.normed(x_now), w_up, w_down, need_up, need_down)

    outs = (((t, d), BF), ((d, ff), BF), ((ff, d), BF))
    scratch = [pltpu.SemaphoreType.DMA((3 * Mlp.steps,))]
    return call(kernel, scalars, [vectors, x], [*up, *down], outs, scratch, "mlp_forward", 8)


def layer(scalars, x, g, vectors, mask, weights):
    t, d = x.shape()
    ff = weights[2].shape[1]

    def kernel(s_ref, vec, mask_ref, w_qkv, w_out, w_up, w_down, *refs):
        *refs, g_s, o_s, act_s, sems = refs
        x_s, qkv_s, p_s, r1, slope_s = refs[-5:]
        c = s_ref[0]
        copies = Copies(c, sems)
        need_x, refs = x.fetch(copies, s_ref, refs[:-5], x_s)
        need_g, outs = g.fetch(copies, s_ref, refs, g_s)
        y_out, gi_out, a1_keep, a1_send, o_keep, o_send, a2_keep, a2_send, act_keep, act_send = outs
        attention, mlp = Attention(vec, d, ff), Mlp(vec, d, ff)
        none = [[]] * max(GROUPS, Mlp.steps)
        wait(need_x)
        x_now = x_s[...]
        a = attention.normed(x_now)
        split_halves(c, a, a1_keep, a1_send)
        r = attention.forward(x_now, a, mask_ref[...], w_qkv, w_out, none, [], o_s, qkv_s, p_s)
        r1[...] = r
        split_halves(c, o_s[...], o_keep, o_send)
        a = mlp.normed(r)
        split_halves(c, a, a2_keep, a2_send)
        y_out[...] = mlp.forward(r, a, w_up, w_down, none, none, act_s, slope_s)
        split_halves(c, act_s[...], act_keep, act_send)
        wait(need_g)
        mid, _, _ = mlp.backward(g_s[...], r1, slope_s, w_up, w_down, none, none)
        (gi, _, _), _ = attention.backward(mid, x_s, qkv_s, p_s, w_qkv, w_out, [], [])
        gi_out[...] = gi

    row, half = ((t, d), BF), ((t, d // 2), BF)
    outs = (row, row, half, half, half, half, half, half, ((t, ff // 2), BF), ((t, ff // 2), BF))
    outs += (row, ((t, 3 * d), BF), ((GROUPS, t, t * HEADS // GROUPS), BF), row, ((t, ff), BF))
    scratch = rooms(row, row, ((t, ff), BF)) + [pltpu.SemaphoreType.DMA((2,))]
    out = call(kernel, scalars, [vectors, mask, *weights], x.arrays + g.arrays, outs, scratch, "layer", 14)
    return out[:10], out[10:]


def mlp_backward(scalars, g, g_other, act, vectors, r1, slope, weights, blocks, splits):
    t, d = r1.shape
    ff = weights[0].shape[1]

    def kernel(s_ref, vec, x_s, slope_s, w_up, w_down, act_keep, act_got, *refs):
        *refs, g_s, other_s, sems = refs
        copies = Copies(s_ref[0], sems)
        need_g, refs = g.fetch(copies, s_ref, refs, g_s)
        need_other, refs = g_other.fetch(copies, s_ref, refs, other_s)
        mid_out, du_out, sums, *halves = refs
        sub = Mlp(vec, d, ff)
        wait(need_g)
        wait(need_other)
        g_now = g_s[...]
        rows = ff // 2 // blocks
        for piece, (bit, lo) in enumerate(splits):
            cols = slice(piece * PIECE, (piece + 1) * PIECE)
            group = max(2 * lo, blocks // 4)
            for first in range(0, blocks, group):
                part = slice(first * rows, (first + group) * rows)
                out = t_dot(act_keep[:, part], g_s[:, cols]) + t_dot(act_got[:, part], other_s[:, cols])
                out = out.astype(BF).reshape(group, rows, PIECE)
                split_blocks((s_ref[2] >> bit) & 1, lo, out, first, *halves[2 * piece : 2 * piece + 2], slice(None))

        def emit(j, cols, du):
            du_out[:, cols] = du
            sums[:, cols] = col_sum(du)

        none = [[]] * Mlp.steps
        mid, gain, shift = sub.backward(g_now, x_s, slope_s, w_up, w_down, none, none, emit)
        mid_out[...] = mid
        for i, m in enumerate((col_sum(g_now), gain, shift, col_sum(mid))):
            sums[:, ff + i * d : ff + (i + 1) * d] = m

    row = ((t, d), BF)
    outs = [row, ((t, ff), BF), ((1, ff + 4 * d), F32)]
    outs += [((blocks // 2, ff // 2 // blocks, PIECE), BF)] * 2 * len(splits)
    scratch = rooms(row, row) + [pltpu.SemaphoreType.DMA((2,))]
    held = [vectors, r1, slope, *weights, *act]
    out = call(kernel, scalars, held, g.arrays + g_other.arrays, outs, scratch, "mlp_backward", 12)
    return (*out[:3], [out[3 + 2 * i : 5 + 2 * i] for i in range(len(splits))])


def attention_backward(scalars, g, vectors, x, qkv, p, weights):
    t, d = x.shape
    ff = vectors.shape[1] - 8 * d

    def kernel(s_ref, vec, x_s, qkv_s, p_s, w_qkv, w_out, g_ref, gi_out, dqkv_out, sums):
        sub = Attention(vec, d, ff)
        (gi, gain, shift), parts = sub.backward(g_ref[...], x_s, qkv_s, p_s, w_qkv, w_out, [], [])
        for i, m in enumerate(parts):
            dqkv_out[:, i * d : (i + 1) * d] = m
        gi_out[...] = gi
        for i, m in enumerate((col_sum(parts[0]), col_sum(parts[2]), gain, shift)):
            sums[:, i * d : (i + 1) * d] = m

    outs = (((t, d), BF), ((t, 3 * d), BF), ((1, 4 * d), F32))
    return call(kernel, scalars, [vectors, x, qkv, p, *weights, g], [], outs, [], "attention_backward", 10)


def weight_grads(scalars, tasks, blocks):
    arrays, outs = [], []

    def index_of(m):
        for i, known in enumerate(arrays):
            if known is m:
                return i
        arrays.append(m)
        return len(arrays) - 1

    tasks = [(tuple(map(index_of, left)), tuple(map(index_of, right)), *rest) for left, right, *rest in tasks]
    for left, _, _, n, _, _ in tasks:
        outs += [((blocks // 2, arrays[left[0]].shape[1] // blocks, n), BF)] * 2

    def kernel(s_ref, *refs):
        ins, targets = refs[: len(arrays)], refs[len(arrays) :]
        for k, (left, right, first, n, bit, lo) in enumerate(tasks):
            for at in range(0, n, PIECE):
                cols = slice(first + at, first + at + PIECE)
                out = sum(t_dot(ins[i][...], ins[j][:, cols]) for i, j in zip(left, right))
                out = out.astype(BF).reshape(blocks, -1, PIECE)
                split_blocks((s_ref[2] >> bit) & 1, lo, out, 0, *targets[2 * k : 2 * k + 2], slice(at, at + PIECE))

    out = call(kernel, scalars, arrays, [], outs, [], "weight_grads", 8)
    return [(out[2 * k], out[2 * k + 1]) for k in range(len(tasks))]


def folded(scalars, mine, got, bit, lo):
    shape = mine.shape

    def kernel(s_ref, a, b, *outs):
        if bit is None:
            outs[0][...] = a[0].astype(F32) + b[0].astype(F32)
            return
        side = (s_ref[2] >> bit) & 1
        for k in range(shape[0] // 2):
            base = k // lo * 2 * lo + k % lo
            for ref, at in ((outs[0], base + side * lo), (outs[1], base + (1 - side) * lo)):
                ref[k] = (a[at].astype(F32) + b[at].astype(F32)).astype(ref.dtype)

    outs = [(shape[1:], F32)] if bit is None else [((shape[0] // 2,) + shape[1:], mine.dtype)] * 2
    return call(kernel, scalars, [mine, got], [], outs, [], "folded", 6)


def core_swap(x):
    return lax.ppermute(x, "section", [(i, i ^ 1) for i in range(lax.axis_size("section"))])


def x_hop(x, pairs):
    return lax.ppermute(x, "section", pairs)


def dp_swap(x, bit):
    return lax.ppermute(x, "dp", [(i, i ^ 1 << bit) for i in range(lax.axis_size("dp"))])


def lower(bits, k):
    return 1 << sum(b < bits[k] for b in bits[k:])


def scatter_steps(scalars, bits, mine, send):
    for k, bit in enumerate(bits):
        got = yield dp_swap(send, bit), send
        if k + 1 < len(bits):
            mine, send = folded(scalars, mine, got, bits[k + 1], lower(bits, k + 1))
    return folded(scalars, mine, got, None, None)[0]


def all_sum_steps(x):
    x = x + (yield core_swap(x), x)
    for bit in range(lax.axis_size("dp").bit_length() - 1):
        x = x + (yield dp_swap(x, bit), x)
    return x


class Order:
    def __init__(self):
        self.last = None
        self.running = {}
        self.results = {}

    def after(self, x):
        if self.last is None:
            return x
        return lax.optimization_barrier((x, self.last))[0]

    def done(self, x):
        self.last = jax.tree.leaves(x)[0]
        return x

    def begin(self, name, steps):
        self.running[name] = (steps, next(steps)[0])

    def drain(self):
        while self.running:
            self.advance(*self.running)

    def advance(self, *names):
        for name in names:
            steps, arriving = self.running.pop(name)
            try:
                arriving, out = steps.send(self.after(arriving))
                self.running[name] = (steps, arriving)
                self.done(out)
            except StopIteration as stop:
                self.results[name] = self.done(stop.value)


def per_device(
    tokens, segments, qkv_weight, qv_bias, out_weight, out_bias, up_weight, up_bias, down_weight, down_bias,
    norm_gain, norm_shift, cotangent,
):
    d = tokens.shape[1]
    t = segments.shape[1]
    section = lax.axis_index("section")
    core, x = section % 2, section // 2
    dp = lax.axis_index("dp")
    n_dp = lax.axis_size("dp")
    later = x == 1
    fwd_pairs, bwd_pairs = [(0, 2), (1, 3)], [(2, 0), (3, 1)]
    scalars = jnp.stack([core, x, dp]).astype(jnp.int32)

    both = lambda m: (m, core_swap(m))
    qkv, out = both(qkv_weight), both(out_weight)
    vectors = [qv_bias, out_bias, up_bias, down_bias, norm_gain, norm_shift]
    vectors = both(jnp.concatenate([m.reshape(1, -1).astype(F32) for m in vectors], axis=1))
    token_rows, cot_rows = tokens.reshape(2, t, d), cotangent.reshape(2, t, d)
    seg = lax.dynamic_index_in_dim(segments, core, 0, False)
    segs = [seg[:, None], seg[None, :]]
    (up_weight, down_weight), qkv, out, vectors, scalars, segs = lax.optimization_barrier(
        ((up_weight, down_weight), qkv, out, vectors, scalars, segs)
    )
    up, down = both(up_weight), both(down_weight)

    r1, w_qkv, w_out, vec, mask = attention_forward(scalars, Chosen(rows=token_rows), segs, *vectors, qkv, out)
    r2, w_up, w_down = mlp_forward(scalars, r1, vec, up, down)
    entering = Chosen(rows=token_rows, other=x_hop(r2, fwd_pairs))
    outs, held = layer(scalars, entering, Chosen(rows=cot_rows), vec, mask, (w_qkv, w_out, w_up, w_down))
    r2, g0, a1_keep, a1_send, o_keep, o_send, a2_keep, a2_send, act_keep, act_send = outs
    x_held, qkv, p, r1, slope = held

    swaps = ((a1_keep, a1_send), (o_keep, o_send), (a2_keep, a2_send), (act_keep, act_send))
    a1, o, a2, act = ((keep, core_swap(send)) for keep, send in swaps)

    hopped = x_hop(g0, bwd_pairs)
    hopped, hopped_other, a1, o, a2, act = lax.optimization_barrier((hopped, core_swap(hopped), a1, o, a2, act))
    g_own = Chosen(rows=cot_rows, other=hopped, at=0)
    g_other = Chosen(rows=cot_rows, other=hopped_other, at=0, flip=True)
    bits = list(range(n_dp.bit_length() - 1))
    y_first, z_first, y_second = bits, bits[1:] + bits[:1], bits[1:2] + bits[:1] + bits[2:]
    first_half = lambda kind: (kind[0], lower(kind, 0))
    down_kinds = {"d0": z_first, "d1": y_first}
    splits = [first_half(kind) for kind in down_kinds.values()]
    g_attn, du, mlp_sums, downs = mlp_backward(
        scalars, g_own, g_other, act, vec, r1, slope, (w_up, w_down), n_dp, splits
    )
    du, g_attn_all = both(du), both(g_attn)

    order = Order()

    def begin(*tasks):
        names, kinds, lefts, rights, firsts, widths = zip(*tasks)
        rights = order.after(rights)
        halves = [first_half(kind) for kind in kinds]
        args = [(left, right, first, n, *h) for left, right, first, n, h in zip(lefts, rights, firsts, widths, halves)]
        for name, kind, pair in zip(names, kinds, order.done(weight_grads(scalars, args, n_dp))):
            order.begin(name, scatter_steps(scalars, kind, *pair))

    hf = up_weight.shape[1] // 2
    for name, pair in zip(down_kinds, downs):
        order.begin(name, scatter_steps(scalars, down_kinds[name], *order.done(pair)))
    begin(("u0", y_first, a2, du, 0, hf), ("u1", y_first, a2, du, hf, hf))
    g_in, dqkv, attn_sums = order.done(
        attention_backward(scalars, order.after(g_attn), vec, x_held, qkv, p, (w_qkv, w_out))
    )
    dqkv = both(dqkv)
    order.advance("d0", "d1")
    small = jnp.concatenate(order.after([mlp_sums, attn_sums]), axis=1)
    order.begin("small", all_sum_steps(order.done(small)))
    order.advance("small")
    begin(("qk", y_first, a1, dqkv, 0, 2 * d), ("o", z_first, o, g_attn_all, 0, d), ("v", y_first, a1, dqkv, 2 * d, d))
    order.advance("d0", "u0", "d1", "o", "u0")

    crossed = x_hop(jnp.where(later, r2[:, : d // 2], g_in[:, d // 2 :]), fwd_pairs + bwd_pairs)

    def columns(here, there, keep_side):
        mine = jnp.where(keep_side, here, there)
        half = mine.shape[1] // 2
        part = lambda index: lax.dynamic_slice_in_dim(mine, index * half, half, 1)
        own, other = part(core), core_swap(part(1 - core))
        return jnp.where(core == 0, jnp.concatenate([own, other]), jnp.concatenate([other, own]))

    crossed = order.after(crossed)
    block_output = columns(r2[:, d // 2 :], crossed, later)
    input_gradient = columns(g_in[:, : d // 2], crossed, jnp.logical_not(later))
    order.advance("u1", "d1", "o", "qk")
    block_output, input_gradient = order.done(order.after((block_output, input_gradient)))
    order.advance("u1", "u0", "small", "v", "d0", "o", "qk", "small", "v", "u1", "qk", "small", "v")
    order.drain()
    done = order.results
    vectors = []
    small = done["small"][0]
    ff, at, parts = 2 * hf, 0, {}
    for name, width in zip(("up", "down", "gain1", "shift1", "out", "q", "v", "gain0", "shift0"), (ff,) + (d,) * 8):
        parts[name] = small[at : at + width]
        at += width
    for names in (("q", "v"), ("out",), ("up",), ("down",), ("gain0", "gain1"), ("shift0", "shift1")):
        vector = jnp.concatenate([parts[name] for name in names])
        part = vector.shape[0] // (2 * n_dp)
        vectors.append(lax.dynamic_slice_in_dim(vector, (core * n_dp + dp) * part, part))
    g_qv, g_out_b, g_up_b, g_down_b, g_gain, g_shift = vectors
    return (
        block_output,
        input_gradient,
        jnp.concatenate([done["qk"], done["v"]], axis=1),
        g_qv,
        done["o"],
        g_out_b,
        jnp.concatenate([done["u0"], done["u1"]], axis=1),
        g_up_b,
        jnp.concatenate([done["d0"], done["d1"]], axis=1),
        g_down_b,
        g_gain[None],
        g_shift[None],
    )


def solution(mesh):
    placed = (
        P("dp", None), P("dp", None), P("section", None), P("section"), P("section", None), P("section"),
        P("section", None), P("section"), P("section", None), P("section"), P("section", None), P("section", None),
        P("dp", None),
    )
    both = ("section", "dp")
    return jax.shard_map(
        per_device,
        mesh=mesh,
        in_specs=placed,
        out_specs=(
            P("dp", "section"), P("dp", "section"), P(both, None), P(both), P(both, None), P(both), P(both, None),
            P(both), P(both, None), P(both), P("section", "dp"), P("section", "dp"),
        ),
        check_vma=False,
    )
```

```python
import jax
import jax.numpy as jnp
from jax import lax
from jax.experimental import pallas as pl
from jax.experimental.pallas import tpu as pltpu
from jax.sharding import PartitionSpec as P

HEADS = 16
EPSILON = 1e-06
BF = jnp.bfloat16
F32 = jnp.float32
MIB = 1024 * 1024
PIECE = 512
ANYWHERE = pl.BlockSpec(memory_space=pl.ANY)
IN_VMEM = pl.BlockSpec(memory_space=pltpu.VMEM)


def dot(a, b):
    return jnp.dot(a, b, preferred_element_type=F32)


def dot_t(a, b):
    return lax.dot_general(a, b, (((1,), (1,)), ((), ())), preferred_element_type=F32)


def t_dot(a, b):
    return lax.dot_general(a, b, (((0,), (0,)), ((), ())), preferred_element_type=F32)


def call(kernel, scalars, held, ins, outs, scratch, name, mib):
    return pl.pallas_call(
        kernel,
        in_specs=[pl.BlockSpec(memory_space=pltpu.SMEM)] + [IN_VMEM] * len(held) + [ANYWHERE] * len(ins),
        out_specs=[IN_VMEM] * len(outs),
        out_shape=[pltpu.VMEM(shape, dtype) for shape, dtype in outs],
        scratch_shapes=scratch,
        compiler_params=pltpu.CompilerParams(vmem_limit_bytes=mib * MIB),
        cost_estimate=pl.CostEstimate(flops=0, bytes_accessed=0, transcendentals=0),
        name=name,
    )(scalars, *held, *ins)


def rooms(*pairs):
    return [pltpu.VMEM(shape, dtype) for shape, dtype in pairs]


class Copies:
    def __init__(self, core, sems):
        self.core, self.sems, self.used = core, sems, 0

    def start(self, source, target):
        copy = pltpu.make_async_copy(source, target, self.sems.at[self.used])
        self.used += 1
        copy.start()
        return [copy]

    def columns(self, own, got, target, first, width):
        half = own.shape[0]
        cols = pl.ds(first, width)
        out = []
        for source, at in ((own, self.core), (got, 1 - self.core)):
            rows = pl.ds(pl.multiple_of(at * half, half), half)
            out += self.start(source.at[:, cols], target.at[rows, cols])
        return out

    def either(self, first, source, other, target):
        sem = self.sems.at[self.used]
        self.used += 1

        @pl.when(first)
        def _():
            pltpu.make_async_copy(source, target, sem).start()

        @pl.when(jnp.logical_not(first))
        def _():
            pltpu.make_async_copy(other, target, sem).start()

        return [pltpu.make_async_copy(source, target, sem)]

    def rows(self, own, got, target, first, count):
        half = own.shape[0]
        here = pl.ds(first % half, count)
        return self.either(self.core == first // half, own.at[here], got.at[here], target.at[pl.ds(first, count)])


def wait(copies):
    for copy in copies:
        copy.wait()


def split_halves(core, value, keep, send):
    half = value.shape[1] // 2
    low, high = value[:, :half], value[:, half:]
    keep[...] = jnp.where(core == 0, low, high)
    send[...] = jnp.where(core == 0, high, low)


def split_blocks(side, lo, value, first, keep, send, cols):
    for k in range(value.shape[0]):
        at = first + k
        if at // lo % 2 == 0:
            to, a, b = at // (2 * lo) * lo + at % lo, value[k], value[k + lo]
            keep[to, :, cols] = jnp.where(side == 0, a, b)
            send[to, :, cols] = jnp.where(side == 0, b, a)


class Chosen:
    def __init__(self, array=None, rows=None, other=None, at=1, flip=False):
        self.arrays = [m for m in (array, rows, other) if m is not None]
        self.by_core, self.at, self.flip = rows is not None, at, flip

    def shape(self):
        return self.arrays[0].shape[-2:]

    def fetch(self, copies, scalars, refs, target):
        row = 1 - scalars[0] if self.flip else scalars[0]
        here = refs[0].at[row] if self.by_core else refs[0]
        if len(self.arrays) == 1:
            return copies.start(here, target), refs[1:]
        return copies.either(scalars[1] == self.at, refs[1], here, target), refs[2:]


def centered(x):
    r = x.astype(F32)
    center = r - jnp.mean(r, axis=-1, keepdims=True)
    spread = jnp.mean(center * center, axis=-1, keepdims=True)
    scale = lax.rsqrt(spread + EPSILON)
    return center * scale, scale


def norm_backward(da, x, gain, g):
    xhat, scale = centered(x)
    dx = da * gain
    dr = scale * (
        dx - jnp.mean(dx, axis=-1, keepdims=True) - xhat * jnp.mean(dx * xhat, axis=-1, keepdims=True)
    )
    return (
        (g.astype(F32) + dr).astype(BF),
        jnp.sum(da * xhat, axis=0, keepdims=True),
        jnp.sum(da, axis=0, keepdims=True),
    )


GROUPS = 4


def head_blocks(m, dh):
    head = lax.broadcasted_iota(jnp.int32, (1, m.shape[1]), 1) // dh
    zero = jnp.zeros((), m.dtype)
    return jnp.concatenate([jnp.where(head == h, m, zero) for h in range(m.shape[1] // dh)], axis=0)


def stacked(m, t):
    return jnp.concatenate([m[:, i : i + t] for i in range(0, m.shape[1], t)], axis=0)


def vector_places(d, ff):
    names = ("q", "v", "out", "down", "gain0", "gain1", "shift0", "shift1")
    places = {name: slice(i * d, (i + 1) * d) for i, name in enumerate(names)}
    places["up"] = slice(8 * d, 8 * d + ff)
    return places


class Attention:
    def __init__(self, vectors, d, ff):
        at = vector_places(d, ff)
        self.b_q, self.b_v, self.b_out = (vectors[:, at[name]] for name in ("q", "v", "out"))
        self.gain, self.shift = vectors[:, at["gain0"]], vectors[:, at["shift0"]]

    @staticmethod
    def fetch(copies, qkv, out, w_qkv, w_out, out_first=False):
        d = w_out.shape[0]
        gw = d // GROUPS
        need, need_out = [], []

        def fetch_out():
            for j in range(2):
                need_out.extend(copies.rows(*out, w_out, j * (d // 2), d // 2))

        if out_first:
            fetch_out()
        for j in range(GROUPS):
            need.append([])
            for i in range(3):
                need[j] += copies.columns(*qkv, w_qkv, i * d + j * gw, gw)
        if not out_first:
            fetch_out()
        return need, need_out

    def normed(self, x):
        xhat, _ = centered(x)
        return (xhat * self.gain + self.shift).astype(BF)

    def forward(self, x, a, mask, w_qkv, w_out, need, need_out, o_s, qkv_s=None, p_s=None):
        t, d = x.shape
        gw, dh = d // GROUPS, d // HEADS
        mask = jnp.concatenate([mask] * (gw // dh), axis=1)

        def project(j):
            wait(need[j])
            cols = [slice(i * d + j * gw, i * d + (j + 1) * gw) for i in range(3)]
            q, k, v = (dot(a, w_qkv[:, s]) for s in cols)
            q = (q + self.b_q[:, j * gw : (j + 1) * gw]).astype(BF)
            k = k.astype(BF)
            v = (v + self.b_v[:, j * gw : (j + 1) * gw]).astype(BF)
            if qkv_s is not None:
                for i, m in enumerate((q, k, v)):
                    qkv_s[:, cols[i]] = m
            return q, k, v

        now = project(0)
        for j in range(GROUPS):
            q, k, v = now
            s = dot_t(k, head_blocks(q * jnp.asarray(dh**-0.5, BF), dh)) + mask
            if j + 1 < GROUPS:
                now = project(j + 1)
            e = jnp.exp(s - jnp.max(s, axis=0, keepdims=True))
            p = (e * (1.0 / jnp.sum(e, axis=0, keepdims=True))).astype(BF)
            if p_s is not None:
                p_s[j] = p
            o_s[:, j * gw : (j + 1) * gw] = t_dot(stacked(p, t), head_blocks(v, dh)).astype(BF)
        wait(need_out)
        return (x.astype(F32) + self.b_out + dot(o_s[...], w_out[...])).astype(BF)

    def backward(self, g, x, qkv_s, p_s, w_qkv, w_out, need, need_out, need_p=None, need_x=()):
        t, d = g.shape
        gw, dh = d // GROUPS, d // HEADS
        wait(need_out)
        parts = [[], [], []]
        for j in range(GROUPS):
            if need_p is not None:
                wait(need_p[j])
            do = dot_t(g, w_out[j * gw : (j + 1) * gw, :]).astype(BF)
            q, k, v = (qkv_s[:, i * d + j * gw : i * d + (j + 1) * gw] for i in range(3))
            do = head_blocks(do, dh)
            p = p_s[j]
            pf = p.astype(F32)
            w_ = pf * dot_t(v, do)
            ds = (w_ - pf * jnp.sum(w_, axis=0, keepdims=True)).astype(BF)
            dv = dot(p, do)
            dk = dot(ds, head_blocks(q, dh))
            dq = t_dot(stacked(ds, t), head_blocks(k, dh))
            scale = dh**-0.5
            for i, m in enumerate((dq * scale, dk * scale, dv)):
                parts[i].append(m.astype(BF))
        parts = [jnp.concatenate(m, axis=1) for m in parts]
        for m in need:
            wait(m)
        da = sum(dot_t(m, w_qkv[:, i * d : (i + 1) * d]) for i, m in enumerate(parts))
        wait(need_x)
        return norm_backward(da, x[...], self.gain, g), parts


class Mlp:
    steps = 4

    def __init__(self, vectors, d, ff):
        at = vector_places(d, ff)
        self.b_up, self.b_down = vectors[:, at["up"]], vectors[:, at["down"]]
        self.gain, self.shift = vectors[:, at["gain1"]], vectors[:, at["shift1"]]

    @classmethod
    def fetch(cls, copies, up, down, w_up, w_down, down_first=False):
        tw = w_up.shape[1] // cls.steps
        need_up, need_down = [], []
        for j in range(cls.steps):
            if down_first:
                need_down.append(copies.rows(*down, w_down, j * tw, tw))
            need_up.append(copies.columns(*up, w_up, j * tw, tw))
            if not down_first:
                need_down.append(copies.rows(*down, w_down, j * tw, tw))
        return need_up, need_down

    def normed(self, x):
        xhat, _ = centered(x)
        return (xhat * self.gain + self.shift).astype(BF)

    def forward(self, x, a, w_up, w_down, need_up, need_down, act_s=None, slope_s=None):
        tw = w_up.shape[1] // self.steps

        def hidden(j):
            wait(need_up[j])
            return dot(a, w_up[:, j * tw : (j + 1) * tw]) + self.b_up[:, j * tw : (j + 1) * tw]

        total = x.astype(F32) + self.b_down
        u = hidden(0)
        for j in range(self.steps):
            cols = slice(j * tw, (j + 1) * tw)
            later = hidden(j + 1) if j + 1 < self.steps else None
            phi = 0.5 + 0.5 * lax.erf(u * 0.5**0.5)
            act = (u * phi).astype(BF)
            if act_s is not None:
                act_s[:, cols] = act
                slope_s[:, cols] = (phi + u * (jnp.exp(-0.5 * u * u) * (2 * jnp.pi) ** -0.5)).astype(BF)
            wait(need_down[j])
            total += dot(act, w_down[cols, :])
            u = later
        return total.astype(BF)

    def backward(self, g, x, slope_s, w_up, w_down, need_up, need_down, emit=None, need_slope=(), need_x=()):
        tw = w_up.shape[1] // self.steps

        def incoming(j):
            wait(need_down[j])
            return dot_t(g, w_down[j * tw : (j + 1) * tw, :])

        da = None
        dg = incoming(0)
        wait(need_slope)
        for j in range(self.steps):
            cols = slice(j * tw, (j + 1) * tw)
            du = (dg * slope_s[:, cols].astype(F32)).astype(BF)
            dg = incoming(j + 1) if j + 1 < self.steps else None
            if emit is not None:
                emit(j, cols, du)
            wait(need_up[j])
            part = dot_t(du, w_up[:, cols])
            da = part if da is None else da + part
        wait(need_x)
        return norm_backward(da, x[...], self.gain, g)


def col_sum(m):
    return jnp.sum(m.astype(F32), axis=0, keepdims=True)


def attention_forward(scalars, x, segs, own, got, qkv, out):
    t, d = x.shape()
    ff = 2 * own.shape[1] - 8 * d

    def kernel(s_ref, *refs):
        c = s_ref[0]
        y_out, w_qkv, w_out, vectors, mask, o_s, x_s, own_s, got_s, r_s, c_s, sems = refs[-12:]
        copies = Copies(c, sems)
        need_x, refs = x.fetch(copies, s_ref, refs[:-12], x_s)
        seg_r, seg_c, own_ref, got_ref, qo, qg, oo, og = refs
        need_v = copies.start(own_ref, own_s) + copies.start(got_ref, got_s)
        need_m = copies.start(seg_r, r_s) + copies.start(seg_c, c_s)
        need, need_out = Attention.fetch(copies, (qo, qg), (oo, og), w_qkv, w_out)
        wait(need_v)
        at = vector_places(d, ff)
        low, high = jnp.where(c == 0, own_s[...], got_s[...]), jnp.where(c == 0, got_s[...], own_s[...])
        first = 0
        for names, width in (
            (("q", "v"), d), (("out",), d // 2), (("up",), ff // 2), (("down",), d // 2),
            (("gain0", "gain1"), d), (("shift0", "shift1"), d),
        ):
            places = [at[name] for name in names]
            if len(places) == 1:
                start = places[0].start
                places = [slice(start, start + width), slice(start + width, start + 2 * width)]
            for place, half in zip(places, (low, high)):
                vectors[:, place] = half[:, first : first + width]
            first += width
        wait(need_m)
        mask[...] = jnp.where(r_s[...] == c_s[...], 0.0, -1e30)
        sub = Attention(vectors, d, ff)
        wait(need_x)
        x_now = x_s[...]
        y_out[...] = sub.forward(x_now, sub.normed(x_now), mask[...], w_qkv, w_out, need, need_out, o_s)

    row = ((t, d), BF)
    ins = x.arrays + [*segs, own, got, *qkv, *out]
    outs = (row, ((d, 3 * d), BF), ((d, d), BF), ((1, 8 * d + ff), F32), ((t, t), F32))
    scratch = rooms(row, row, (own.shape, F32), (own.shape, F32), ((t, 1), jnp.int32), ((1, t), jnp.int32))
    scratch += [pltpu.SemaphoreType.DMA((6 * GROUPS + 7,))]
    return call(kernel, scalars, [], ins, outs, scratch, "attention_forward", 44)


def mlp_forward(scalars, x, vectors, up, down):
    t, d = x.shape
    ff = up[0].shape[1]

    def kernel(s_ref, vec, x_ref, uo, ug, do, dg, y_out, w_up, w_down, sems):
        need_up, need_down = Mlp.fetch(Copies(s_ref[0], sems), (uo, ug), (do, dg), w_up, w_down)
        sub = Mlp(vec, d, ff)
        x_now = x_ref[...]
        y_out[...] = sub.forward(x_now, sub.normed(x_now), w_up, w_down, need_up, need_down)

    outs = (((t, d), BF), ((d, ff), BF), ((ff, d), BF))
    scratch = [pltpu.SemaphoreType.DMA((3 * Mlp.steps,))]
    return call(kernel, scalars, [vectors, x], [*up, *down], outs, scratch, "mlp_forward", 8)


def layer(scalars, x, g, vectors, mask, weights):
    t, d = x.shape()
    ff = weights[2].shape[1]

    def kernel(s_ref, vec, mask_ref, w_qkv, w_out, w_up, w_down, *refs):
        *refs, g_s, o_s, act_s, sems = refs
        x_s, qkv_s, p_s, r1, slope_s = refs[-5:]
        c = s_ref[0]
        copies = Copies(c, sems)
        need_x, refs = x.fetch(copies, s_ref, refs[:-5], x_s)
        need_g, outs = g.fetch(copies, s_ref, refs, g_s)
        y_out, gi_out, a1_keep, a1_send, o_keep, o_send, a2_keep, a2_send, act_keep, act_send = outs
        attention, mlp = Attention(vec, d, ff), Mlp(vec, d, ff)
        none = [[]] * max(GROUPS, Mlp.steps)
        wait(need_x)
        x_now = x_s[...]
        a = attention.normed(x_now)
        split_halves(c, a, a1_keep, a1_send)
        r = attention.forward(x_now, a, mask_ref[...], w_qkv, w_out, none, [], o_s, qkv_s, p_s)
        r1[...] = r
        split_halves(c, o_s[...], o_keep, o_send)
        a = mlp.normed(r)
        split_halves(c, a, a2_keep, a2_send)
        y_out[...] = mlp.forward(r, a, w_up, w_down, none, none, act_s, slope_s)
        split_halves(c, act_s[...], act_keep, act_send)
        wait(need_g)
        mid, _, _ = mlp.backward(g_s[...], r1, slope_s, w_up, w_down, none, none)
        (gi, _, _), _ = attention.backward(mid, x_s, qkv_s, p_s, w_qkv, w_out, [], [])
        gi_out[...] = gi

    row, half = ((t, d), BF), ((t, d // 2), BF)
    outs = (row, row, half, half, half, half, half, half, ((t, ff // 2), BF), ((t, ff // 2), BF))
    outs += (row, ((t, 3 * d), BF), ((GROUPS, t, t * HEADS // GROUPS), BF), row, ((t, ff), BF))
    scratch = rooms(row, row, ((t, ff), BF)) + [pltpu.SemaphoreType.DMA((2,))]
    out = call(kernel, scalars, [vectors, mask, *weights], x.arrays + g.arrays, outs, scratch, "layer", 12)
    return out[:10], out[10:]


def mlp_backward(scalars, g, g_other, act, vectors, r1, slope, weights, blocks, splits):
    t, d = r1.shape
    ff = weights[0].shape[1]

    def kernel(s_ref, vec, x_s, slope_s, w_up, w_down, act_keep, act_got, *refs):
        *refs, g_s, other_s, sems = refs
        copies = Copies(s_ref[0], sems)
        need_g, refs = g.fetch(copies, s_ref, refs, g_s)
        need_other, refs = g_other.fetch(copies, s_ref, refs, other_s)
        mid_out, du_out, sums, *halves = refs
        sub = Mlp(vec, d, ff)
        wait(need_g)
        wait(need_other)
        g_now = g_s[...]
        rows = ff // 2 // blocks
        for piece, (bit, lo) in enumerate(splits):
            cols = slice(piece * PIECE, (piece + 1) * PIECE)
            group = max(2 * lo, blocks // 4)
            for first in range(0, blocks, group):
                part = slice(first * rows, (first + group) * rows)
                out = t_dot(act_keep[:, part], g_s[:, cols]) + t_dot(act_got[:, part], other_s[:, cols])
                out = out.astype(BF).reshape(group, rows, PIECE)
                split_blocks((s_ref[2] >> bit) & 1, lo, out, first, *halves[2 * piece : 2 * piece + 2], slice(None))

        def emit(j, cols, du):
            du_out[:, cols] = du
            sums[:, cols] = col_sum(du)

        none = [[]] * Mlp.steps
        mid, gain, shift = sub.backward(g_now, x_s, slope_s, w_up, w_down, none, none, emit)
        mid_out[...] = mid
        for i, m in enumerate((col_sum(g_now), gain, shift, col_sum(mid))):
            sums[:, ff + i * d : ff + (i + 1) * d] = m

    row = ((t, d), BF)
    outs = [row, ((t, ff), BF), ((1, ff + 4 * d), F32)]
    outs += [((blocks // 2, ff // 2 // blocks, PIECE), BF)] * 2 * len(splits)
    scratch = rooms(row, row) + [pltpu.SemaphoreType.DMA((2,))]
    held = [vectors, r1, slope, *weights, *act]
    out = call(kernel, scalars, held, g.arrays + g_other.arrays, outs, scratch, "mlp_backward", 12)
    return (*out[:3], [out[3 + 2 * i : 5 + 2 * i] for i in range(len(splits))])


def attention_backward(scalars, g, vectors, x, qkv, p, weights):
    t, d = x.shape
    ff = vectors.shape[1] - 8 * d

    def kernel(s_ref, vec, x_s, qkv_s, p_s, w_qkv, w_out, g_ref, gi_out, dqkv_out, sums):
        sub = Attention(vec, d, ff)
        (gi, gain, shift), parts = sub.backward(g_ref[...], x_s, qkv_s, p_s, w_qkv, w_out, [], [])
        for i, m in enumerate(parts):
            dqkv_out[:, i * d : (i + 1) * d] = m
        gi_out[...] = gi
        for i, m in enumerate((col_sum(parts[0]), col_sum(parts[2]), gain, shift)):
            sums[:, i * d : (i + 1) * d] = m

    outs = (((t, d), BF), ((t, 3 * d), BF), ((1, 4 * d), F32))
    return call(kernel, scalars, [vectors, x, qkv, p, *weights, g], [], outs, [], "attention_backward", 10)


def weight_grads(scalars, tasks, blocks):
    arrays, outs = [], []

    def index_of(m):
        for i, known in enumerate(arrays):
            if known is m:
                return i
        arrays.append(m)
        return len(arrays) - 1

    tasks = [(tuple(map(index_of, left)), tuple(map(index_of, right)), *rest) for left, right, *rest in tasks]
    for left, _, _, n, _, _ in tasks:
        outs += [((blocks // 2, arrays[left[0]].shape[1] // blocks, n), BF)] * 2

    def kernel(s_ref, *refs):
        ins, targets = refs[: len(arrays)], refs[len(arrays) :]
        for k, (left, right, first, n, bit, lo) in enumerate(tasks):
            for at in range(0, n, PIECE):
                cols = slice(first + at, first + at + PIECE)
                out = sum(t_dot(ins[i][...], ins[j][:, cols]) for i, j in zip(left, right))
                out = out.astype(BF).reshape(blocks, -1, PIECE)
                split_blocks((s_ref[2] >> bit) & 1, lo, out, 0, *targets[2 * k : 2 * k + 2], slice(at, at + PIECE))

    out = call(kernel, scalars, arrays, [], outs, [], "weight_grads", 8)
    return [(out[2 * k], out[2 * k + 1]) for k in range(len(tasks))]


def folded(scalars, mine, got, bit, lo):
    shape = mine.shape

    def kernel(s_ref, a, b, *outs):
        if bit is None:
            outs[0][...] = a[0].astype(F32) + b[0].astype(F32)
            return
        side = (s_ref[2] >> bit) & 1
        for k in range(shape[0] // 2):
            base = k // lo * 2 * lo + k % lo
            for ref, at in ((outs[0], base + side * lo), (outs[1], base + (1 - side) * lo)):
                ref[k] = (a[at].astype(F32) + b[at].astype(F32)).astype(ref.dtype)

    outs = [(shape[1:], F32)] if bit is None else [((shape[0] // 2,) + shape[1:], mine.dtype)] * 2
    return call(kernel, scalars, [mine, got], [], outs, [], "folded", 6)


def core_swap(x):
    return lax.ppermute(x, "section", [(i, i ^ 1) for i in range(lax.axis_size("section"))])


def x_hop(x, pairs):
    return lax.ppermute(x, "section", pairs)


def dp_swap(x, bit):
    return lax.ppermute(x, "dp", [(i, i ^ 1 << bit) for i in range(lax.axis_size("dp"))])


def lower(bits, k):
    return 1 << sum(b < bits[k] for b in bits[k:])


def scatter_steps(scalars, bits, mine, send):
    for k, bit in enumerate(bits):
        got = yield dp_swap(send, bit), send
        if k + 1 < len(bits):
            mine, send = folded(scalars, mine, got, bits[k + 1], lower(bits, k + 1))
    return folded(scalars, mine, got, None, None)[0]


def all_sum_steps(x):
    x = x + (yield core_swap(x), x)
    for bit in range(lax.axis_size("dp").bit_length() - 1):
        x = x + (yield dp_swap(x, bit), x)
    return x


class Order:
    def __init__(self):
        self.last = None
        self.running = {}
        self.results = {}

    def after(self, x):
        if self.last is None:
            return x
        return lax.optimization_barrier((x, self.last))[0]

    def done(self, x):
        self.last = jax.tree.leaves(x)[0]
        return x

    def begin(self, name, steps):
        self.running[name] = (steps, next(steps)[0])

    def drain(self):
        while self.running:
            self.advance(*self.running)

    def advance(self, *names):
        for name in names:
            steps, arriving = self.running.pop(name)
            try:
                arriving, out = steps.send(self.after(arriving))
                self.running[name] = (steps, arriving)
                self.done(out)
            except StopIteration as stop:
                self.results[name] = self.done(stop.value)


KINDS = {"d0": "z", "d1": "y", "u0": "y", "u1": "y", "q": "y", "k": "y", "o": "z", "v": "y"}
STEPS = (
    "sums", "d0", "d1", "grads", "d0", "d1", "u0", "o", "small", "columns", "u0", "u1", "o", "d1", "columns end", "q",
    "small", "k", "u1", "q", "u0", "k", "v", "d0", "small", "u1", "k", "v", "q", "small", "o", "v",
)


def per_device(
    tokens, segments, qkv_weight, qv_bias, out_weight, out_bias, up_weight, up_bias, down_weight, down_bias,
    norm_gain, norm_shift, cotangent,
):
    d = tokens.shape[1]
    t = segments.shape[1]
    section = lax.axis_index("section")
    core, x = section % 2, section // 2
    dp = lax.axis_index("dp")
    n_dp = lax.axis_size("dp")
    later = x == 1
    fwd_pairs, bwd_pairs = [(0, 2), (1, 3)], [(2, 0), (3, 1)]
    scalars = jnp.stack([core, x, dp]).astype(jnp.int32)

    both = lambda m: (m, core_swap(m))
    qkv, out = both(qkv_weight), both(out_weight)
    vectors = [qv_bias, out_bias, up_bias, down_bias, norm_gain, norm_shift]
    vectors = both(jnp.concatenate([m.reshape(1, -1).astype(F32) for m in vectors], axis=1))
    first_hop = x_hop(norm_gain, fwd_pairs + bwd_pairs)
    token_rows, cot_rows = tokens.reshape(2, t, d), cotangent.reshape(2, t, d)
    seg = lax.dynamic_index_in_dim(segments, core, 0, False)
    segs = [seg[:, None], seg[None, :]]
    (up_weight, down_weight), qkv, out, vectors, scalars, segs, _ = lax.optimization_barrier(
        ((up_weight, down_weight), qkv, out, vectors, scalars, segs, first_hop)
    )
    up, down = both(up_weight), both(down_weight)

    r1, w_qkv, w_out, vec, mask = attention_forward(scalars, Chosen(rows=token_rows), segs, *vectors, qkv, out)
    r2, w_up, w_down = mlp_forward(scalars, r1, vec, up, down)
    entering = Chosen(rows=token_rows, other=x_hop(r2, fwd_pairs))
    outs, held = layer(scalars, entering, Chosen(rows=cot_rows), vec, mask, (w_qkv, w_out, w_up, w_down))
    r2, g0, a1_keep, a1_send, o_keep, o_send, a2_keep, a2_send, act_keep, act_send = outs
    x_held, qkv, p, r1, slope = held

    swaps = ((a1_keep, a1_send), (o_keep, o_send), (a2_keep, a2_send), (act_keep, act_send))
    a1, o, a2, act = ((keep, core_swap(send)) for keep, send in swaps)

    hopped = x_hop(g0, bwd_pairs)
    hopped, hopped_other, a1, o, a2, act = lax.optimization_barrier((hopped, core_swap(hopped), a1, o, a2, act))
    g_own = Chosen(rows=cot_rows, other=hopped, at=0)
    g_other = Chosen(rows=cot_rows, other=hopped_other, at=0, flip=True)
    bits = list(range(n_dp.bit_length() - 1))
    kinds = {"y": bits, "z": bits[1:] + bits[:1], "c": bits[1:2] + bits[:1] + bits[2:]}
    kinds = {name: kinds[kind] for name, kind in KINDS.items()}
    first_half = lambda name: (kinds[name][0], lower(kinds[name], 0))
    g_attn, du, mlp_sums, downs = mlp_backward(
        scalars, g_own, g_other, act, vec, r1, slope, (w_up, w_down), n_dp, [first_half(n) for n in ("d0", "d1")]
    )
    du, g_attn_all = both(du), both(g_attn)
    order = Order()

    def begin(names, rights):
        rights = order.after(rights)
        tasks = []
        for name in names:
            left, right, first, n = sources[name]
            tasks.append((left, rights[right], first, n, *first_half(name)))
        for name, pair in zip(names, order.done(weight_grads(scalars, tasks, n_dp))):
            order.begin(name, scatter_steps(scalars, kinds[name], *pair))

    for name, pair in zip(("d0", "d1"), downs):
        order.begin(name, scatter_steps(scalars, kinds[name], *order.done(pair)))
    ff = up_weight.shape[1]
    sources = {"u0": (a2, "du", 0, ff // 2), "u1": (a2, "du", ff // 2, ff // 2), "o": (o, "g", 0, d)}
    for i, name in enumerate("qkv"):
        sources[name] = (a1, "dqkv", i * d, d)
    sources["qk"] = (a1, "dqkv", 0, 2 * d)
    begin([n for n in kinds if n in ("u0", "u1")], {"du": du})
    g_in, dqkv, attn_sums = order.done(
        attention_backward(scalars, order.after(g_attn), vec, x_held, qkv, p, (w_qkv, w_out))
    )
    dqkv = both(dqkv)
    crossed = x_hop(jnp.where(later, r2[:, : d // 2], g_in[:, d // 2 :]), fwd_pairs + bwd_pairs)

    def columns(here, there, keep_side):
        mine = jnp.where(keep_side, here, there)
        half = mine.shape[1] // 2
        part = lambda index: lax.dynamic_slice_in_dim(mine, index * half, half, 1)
        own, other = part(core), core_swap(part(1 - core))
        return jnp.where(core == 0, jnp.concatenate([own, other]), jnp.concatenate([other, own]))

    for name in STEPS:
        if name == "sums":
            small = jnp.concatenate(order.after([mlp_sums, attn_sums]), axis=1)
            order.begin("small", all_sum_steps(order.done(small)))
        elif name == "grads":
            begin([n for n in kinds if n in ("q", "k", "v", "qk", "o")], {"g": g_attn_all, "dqkv": dqkv})
        elif name == "columns":
            crossed = order.after(crossed)
            block_output = columns(r2[:, d // 2 :], crossed, later)
            input_gradient = columns(g_in[:, : d // 2], crossed, jnp.logical_not(later))
        elif name == "columns end":
            block_output, input_gradient = order.done(order.after((block_output, input_gradient)))
        else:
            order.advance(name)
    order.drain()
    done = order.results
    vectors = []
    small = done["small"][0]
    at, parts = 0, {}
    for name, width in zip(("up", "down", "gain1", "shift1", "out", "q", "v", "gain0", "shift0"), (ff,) + (d,) * 8):
        parts[name] = small[at : at + width]
        at += width
    for names in (("q", "v"), ("out",), ("up",), ("down",), ("gain0", "gain1"), ("shift0", "shift1")):
        vector = jnp.concatenate([parts[name] for name in names])
        part = vector.shape[0] // (2 * n_dp)
        vectors.append(lax.dynamic_slice_in_dim(vector, (core * n_dp + dp) * part, part))
    g_qv, g_out_b, g_up_b, g_down_b, g_gain, g_shift = vectors
    return (
        block_output,
        input_gradient,
        jnp.concatenate([done[n] for n in ("q", "k", "qk", "v") if n in done], axis=1),
        g_qv,
        done["o"],
        g_out_b,
        jnp.concatenate([done["u0"], done["u1"]], axis=1),
        g_up_b,
        jnp.concatenate([done["d0"], done["d1"]], axis=1),
        g_down_b,
        g_gain[None],
        g_shift[None],
    )


def solution(mesh):
    placed = (
        P("dp", None), P("dp", None), P("section", None), P("section"), P("section", None), P("section"),
        P("section", None), P("section"), P("section", None), P("section"), P("section", None), P("section", None),
        P("dp", None),
    )
    both = ("section", "dp")
    return jax.shard_map(
        per_device,
        mesh=mesh,
        in_specs=placed,
        out_specs=(
            P("dp", "section"), P("dp", "section"), P(both, None), P(both), P(both, None), P(both), P(both, None),
            P(both), P(both, None), P(both), P("section", "dp"), P("section", "dp"),
        ),
        check_vma=False,
    )
```

```python
import jax
import jax.numpy as jnp
from jax import lax
from jax.experimental import pallas as pl
from jax.experimental.pallas import tpu as pltpu
from jax.sharding import PartitionSpec as P

HEADS = 16
EPSILON = 1e-06
BF = jnp.bfloat16
F32 = jnp.float32
MIB = 1024 * 1024
PIECE = 512
ANYWHERE = pl.BlockSpec(memory_space=pl.ANY)
IN_VMEM = pl.BlockSpec(memory_space=pltpu.VMEM)


def dot(a, b):
    return jnp.dot(a, b, preferred_element_type=F32)


def dot_t(a, b):
    return lax.dot_general(a, b, (((1,), (1,)), ((), ())), preferred_element_type=F32)


def t_dot(a, b):
    return lax.dot_general(a, b, (((0,), (0,)), ((), ())), preferred_element_type=F32)


def call(kernel, scalars, held, ins, outs, scratch, name, mib):
    return pl.pallas_call(
        kernel,
        in_specs=[pl.BlockSpec(memory_space=pltpu.SMEM)] + [IN_VMEM] * len(held) + [ANYWHERE] * len(ins),
        out_specs=[IN_VMEM] * len(outs),
        out_shape=[pltpu.VMEM(shape, dtype) for shape, dtype in outs],
        scratch_shapes=scratch,
        compiler_params=pltpu.CompilerParams(vmem_limit_bytes=mib * MIB),
        cost_estimate=pl.CostEstimate(flops=0, bytes_accessed=0, transcendentals=0),
        name=name,
    )(scalars, *held, *ins)


def rooms(*pairs):
    return [pltpu.VMEM(shape, dtype) for shape, dtype in pairs]


class Copies:
    def __init__(self, core, sems):
        self.core, self.sems, self.used = core, sems, 0

    def start(self, source, target):
        copy = pltpu.make_async_copy(source, target, self.sems.at[self.used])
        self.used += 1
        copy.start()
        return [copy]

    def columns(self, own, got, target, first, width):
        half = own.shape[0]
        cols = pl.ds(first, width)
        out = []
        for source, at in ((own, self.core), (got, 1 - self.core)):
            rows = pl.ds(pl.multiple_of(at * half, half), half)
            out += self.start(source.at[:, cols], target.at[rows, cols])
        return out

    def either(self, first, source, other, target):
        sem = self.sems.at[self.used]
        self.used += 1

        @pl.when(first)
        def _():
            pltpu.make_async_copy(source, target, sem).start()

        @pl.when(jnp.logical_not(first))
        def _():
            pltpu.make_async_copy(other, target, sem).start()

        return [pltpu.make_async_copy(source, target, sem)]

    def rows(self, own, got, target, first, count):
        half = own.shape[0]
        here = pl.ds(first % half, count)
        return self.either(self.core == first // half, own.at[here], got.at[here], target.at[pl.ds(first, count)])


def wait(copies):
    for copy in copies:
        copy.wait()


def split_halves(core, value, keep, send):
    half = value.shape[1] // 2
    low, high = value[:, :half], value[:, half:]
    keep[...] = jnp.where(core == 0, low, high)
    send[...] = jnp.where(core == 0, high, low)


def split_blocks(side, lo, value, first, keep, send, cols):
    for k in range(value.shape[0]):
        at = first + k
        if at // lo % 2 == 0:
            to, a, b = at // (2 * lo) * lo + at % lo, value[k], value[k + lo]
            keep[to, :, cols] = jnp.where(side == 0, a, b)
            send[to, :, cols] = jnp.where(side == 0, b, a)


class Chosen:
    def __init__(self, array=None, rows=None, other=None, at=1, flip=False):
        self.arrays = [m for m in (array, rows, other) if m is not None]
        self.by_core, self.at, self.flip = rows is not None, at, flip

    def shape(self):
        return self.arrays[0].shape[-2:]

    def fetch(self, copies, scalars, refs, target):
        row = 1 - scalars[0] if self.flip else scalars[0]
        here = refs[0].at[row] if self.by_core else refs[0]
        if len(self.arrays) == 1:
            return copies.start(here, target), refs[1:]
        return copies.either(scalars[1] == self.at, refs[1], here, target), refs[2:]


def centered(x):
    r = x.astype(F32)
    center = r - jnp.mean(r, axis=-1, keepdims=True)
    spread = jnp.mean(center * center, axis=-1, keepdims=True)
    scale = lax.rsqrt(spread + EPSILON)
    return center * scale, scale


def norm_backward(da, x, gain, g):
    xhat, scale = centered(x)
    dx = da * gain
    dr = scale * (
        dx - jnp.mean(dx, axis=-1, keepdims=True) - xhat * jnp.mean(dx * xhat, axis=-1, keepdims=True)
    )
    return (
        (g.astype(F32) + dr).astype(BF),
        jnp.sum(da * xhat, axis=0, keepdims=True),
        jnp.sum(da, axis=0, keepdims=True),
    )


GROUPS = 4


def head_blocks(m, dh):
    head = lax.broadcasted_iota(jnp.int32, (1, m.shape[1]), 1) // dh
    zero = jnp.zeros((), m.dtype)
    return jnp.concatenate([jnp.where(head == h, m, zero) for h in range(m.shape[1] // dh)], axis=0)


def stacked(m, t):
    return jnp.concatenate([m[:, i : i + t] for i in range(0, m.shape[1], t)], axis=0)


def vector_places(d, ff):
    names = ("q", "v", "out", "down", "gain0", "gain1", "shift0", "shift1")
    places = {name: slice(i * d, (i + 1) * d) for i, name in enumerate(names)}
    places["up"] = slice(8 * d, 8 * d + ff)
    return places


class Attention:
    def __init__(self, vectors, d, ff):
        at = vector_places(d, ff)
        self.b_q, self.b_v, self.b_out = (vectors[:, at[name]] for name in ("q", "v", "out"))
        self.gain, self.shift = vectors[:, at["gain0"]], vectors[:, at["shift0"]]

    @staticmethod
    def fetch(copies, qkv, out, w_qkv, w_out, out_first=False):
        d = w_out.shape[0]
        gw = d // GROUPS
        need, need_out = [], []

        def fetch_out():
            for j in range(2):
                need_out.extend(copies.rows(*out, w_out, j * (d // 2), d // 2))

        if out_first:
            fetch_out()
        for j in range(GROUPS):
            need.append([])
            for i in range(3):
                need[j] += copies.columns(*qkv, w_qkv, i * d + j * gw, gw)
        if not out_first:
            fetch_out()
        return need, need_out

    def normed(self, x):
        xhat, _ = centered(x)
        return (xhat * self.gain + self.shift).astype(BF)

    def forward(self, x, a, mask, w_qkv, w_out, need, need_out, o_s, qkv_s=None, p_s=None):
        t, d = x.shape
        gw, dh = d // GROUPS, d // HEADS
        mask = jnp.concatenate([mask] * (gw // dh), axis=1)

        def project(j):
            wait(need[j])
            cols = [slice(i * d + j * gw, i * d + (j + 1) * gw) for i in range(3)]
            q, k, v = (dot(a, w_qkv[:, s]) for s in cols)
            q = (q + self.b_q[:, j * gw : (j + 1) * gw]).astype(BF)
            k = k.astype(BF)
            v = (v + self.b_v[:, j * gw : (j + 1) * gw]).astype(BF)
            if qkv_s is not None:
                for i, m in enumerate((q, k, v)):
                    qkv_s[:, cols[i]] = m
            return q, k, v

        now = project(0)
        for j in range(GROUPS):
            q, k, v = now
            s = dot_t(k, head_blocks(q * jnp.asarray(dh**-0.5, BF), dh)) + mask
            if j + 1 < GROUPS:
                now = project(j + 1)
            e = jnp.exp(s - jnp.max(s, axis=0, keepdims=True))
            p = (e * (1.0 / jnp.sum(e, axis=0, keepdims=True))).astype(BF)
            if p_s is not None:
                p_s[j] = p
            o_s[:, j * gw : (j + 1) * gw] = t_dot(stacked(p, t), head_blocks(v, dh)).astype(BF)
        wait(need_out)
        return (x.astype(F32) + self.b_out + dot(o_s[...], w_out[...])).astype(BF)

    def backward(self, g, x, qkv_s, p_s, w_qkv, w_out, need, need_out, need_p=None, need_x=()):
        t, d = g.shape
        gw, dh = d // GROUPS, d // HEADS
        wait(need_out)
        parts = [[], [], []]
        for j in range(GROUPS):
            if need_p is not None:
                wait(need_p[j])
            do = dot_t(g, w_out[j * gw : (j + 1) * gw, :]).astype(BF)
            q, k, v = (qkv_s[:, i * d + j * gw : i * d + (j + 1) * gw] for i in range(3))
            do = head_blocks(do, dh)
            p = p_s[j]
            pf = p.astype(F32)
            w_ = pf * dot_t(v, do)
            ds = (w_ - pf * jnp.sum(w_, axis=0, keepdims=True)).astype(BF)
            dv = dot(p, do)
            dk = dot(ds, head_blocks(q, dh))
            dq = t_dot(stacked(ds, t), head_blocks(k, dh))
            scale = dh**-0.5
            for i, m in enumerate((dq * scale, dk * scale, dv)):
                parts[i].append(m.astype(BF))
        parts = [jnp.concatenate(m, axis=1) for m in parts]
        for m in need:
            wait(m)
        da = sum(dot_t(m, w_qkv[:, i * d : (i + 1) * d]) for i, m in enumerate(parts))
        wait(need_x)
        return norm_backward(da, x[...], self.gain, g), parts


class Mlp:
    steps = 4

    def __init__(self, vectors, d, ff):
        at = vector_places(d, ff)
        self.b_up, self.b_down = vectors[:, at["up"]], vectors[:, at["down"]]
        self.gain, self.shift = vectors[:, at["gain1"]], vectors[:, at["shift1"]]

    @classmethod
    def fetch(cls, copies, up, down, w_up, w_down, down_first=False):
        tw = w_up.shape[1] // cls.steps
        need_up, need_down = [], []
        for j in range(cls.steps):
            if down_first:
                need_down.append(copies.rows(*down, w_down, j * tw, tw))
            need_up.append(copies.columns(*up, w_up, j * tw, tw))
            if not down_first:
                need_down.append(copies.rows(*down, w_down, j * tw, tw))
        return need_up, need_down

    def normed(self, x):
        xhat, _ = centered(x)
        return (xhat * self.gain + self.shift).astype(BF)

    def forward(self, x, a, w_up, w_down, need_up, need_down, act_s=None, slope_s=None):
        tw = w_up.shape[1] // self.steps

        def hidden(j):
            wait(need_up[j])
            return dot(a, w_up[:, j * tw : (j + 1) * tw]) + self.b_up[:, j * tw : (j + 1) * tw]

        total = x.astype(F32) + self.b_down
        u = hidden(0)
        for j in range(self.steps):
            cols = slice(j * tw, (j + 1) * tw)
            later = hidden(j + 1) if j + 1 < self.steps else None
            phi = 0.5 + 0.5 * lax.erf(u * 0.5**0.5)
            act = (u * phi).astype(BF)
            if act_s is not None:
                act_s[:, cols] = act
                slope_s[:, cols] = (phi + u * (jnp.exp(-0.5 * u * u) * (2 * jnp.pi) ** -0.5)).astype(BF)
            wait(need_down[j])
            total += dot(act, w_down[cols, :])
            u = later
        return total.astype(BF)

    def backward(self, g, x, slope_s, w_up, w_down, need_up, need_down, emit=None, need_slope=(), need_x=()):
        tw = w_up.shape[1] // self.steps

        def incoming(j):
            wait(need_down[j])
            return dot_t(g, w_down[j * tw : (j + 1) * tw, :])

        da = None
        dg = incoming(0)
        wait(need_slope)
        for j in range(self.steps):
            cols = slice(j * tw, (j + 1) * tw)
            du = (dg * slope_s[:, cols].astype(F32)).astype(BF)
            dg = incoming(j + 1) if j + 1 < self.steps else None
            if emit is not None:
                emit(j, cols, du)
            wait(need_up[j])
            part = dot_t(du, w_up[:, cols])
            da = part if da is None else da + part
        wait(need_x)
        return norm_backward(da, x[...], self.gain, g)


def col_sum(m):
    return jnp.sum(m.astype(F32), axis=0, keepdims=True)


def attention_forward(scalars, x, segs, own, got, qkv, out):
    t, d = x.shape()
    ff = 2 * own.shape[1] - 8 * d

    def kernel(s_ref, *refs):
        c = s_ref[0]
        y_out, w_qkv, w_out, vectors, mask, o_s, x_s, own_s, got_s, r_s, c_s, sems = refs[-12:]
        copies = Copies(c, sems)
        need_x, refs = x.fetch(copies, s_ref, refs[:-12], x_s)
        seg_r, seg_c, own_ref, got_ref, qo, qg, oo, og = refs
        need_v = copies.start(own_ref, own_s) + copies.start(got_ref, got_s)
        need_m = copies.start(seg_r, r_s) + copies.start(seg_c, c_s)
        need, need_out = Attention.fetch(copies, (qo, qg), (oo, og), w_qkv, w_out)
        wait(need_v)
        at = vector_places(d, ff)
        low, high = jnp.where(c == 0, own_s[...], got_s[...]), jnp.where(c == 0, got_s[...], own_s[...])
        first = 0
        for names, width in (
            (("q", "v"), d), (("out",), d // 2), (("up",), ff // 2), (("down",), d // 2),
            (("gain0", "gain1"), d), (("shift0", "shift1"), d),
        ):
            places = [at[name] for name in names]
            if len(places) == 1:
                start = places[0].start
                places = [slice(start, start + width), slice(start + width, start + 2 * width)]
            for place, half in zip(places, (low, high)):
                vectors[:, place] = half[:, first : first + width]
            first += width
        wait(need_m)
        mask[...] = jnp.where(r_s[...] == c_s[...], 0.0, -1e30)
        sub = Attention(vectors, d, ff)
        wait(need_x)
        x_now = x_s[...]
        y_out[...] = sub.forward(x_now, sub.normed(x_now), mask[...], w_qkv, w_out, need, need_out, o_s)

    row = ((t, d), BF)
    ins = x.arrays + [*segs, own, got, *qkv, *out]
    outs = (row, ((d, 3 * d), BF), ((d, d), BF), ((1, 8 * d + ff), F32), ((t, t), F32))
    scratch = rooms(row, row, (own.shape, F32), (own.shape, F32), ((t, 1), jnp.int32), ((1, t), jnp.int32))
    scratch += [pltpu.SemaphoreType.DMA((6 * GROUPS + 7,))]
    return call(kernel, scalars, [], ins, outs, scratch, "attention_forward", 44)


def mlp_forward(scalars, x, vectors, up, down, early):
    t, d = x.shape
    ff = up[0].shape[1]

    def kernel(s_ref, vec, x_ref, uo, ug, do, dg, _, y_out, w_up, w_down, sems):
        need_up, need_down = Mlp.fetch(Copies(s_ref[0], sems), (uo, ug), (do, dg), w_up, w_down)
        sub = Mlp(vec, d, ff)
        x_now = x_ref[...]
        y_out[...] = sub.forward(x_now, sub.normed(x_now), w_up, w_down, need_up, need_down)

    outs = (((t, d), BF), ((d, ff), BF), ((ff, d), BF))
    scratch = [pltpu.SemaphoreType.DMA((3 * Mlp.steps,))]
    return call(kernel, scalars, [vectors, x], [*up, *down, early], outs, scratch, "mlp_forward", 8)


def layer(scalars, x, g, vectors, mask, weights):
    t, d = x.shape()
    ff = weights[2].shape[1]

    def kernel(s_ref, vec, mask_ref, w_qkv, w_out, w_up, w_down, *refs):
        *refs, g_s, o_s, act_s, sems = refs
        x_s, qkv_s, p_s, r1, slope_s = refs[-5:]
        c = s_ref[0]
        copies = Copies(c, sems)
        need_x, refs = x.fetch(copies, s_ref, refs[:-5], x_s)
        need_g, outs = g.fetch(copies, s_ref, refs, g_s)
        y_out, gi_out, a1_keep, a1_send, o_keep, o_send, a2_keep, a2_send, act_keep, act_send = outs
        attention, mlp = Attention(vec, d, ff), Mlp(vec, d, ff)
        none = [[]] * max(GROUPS, Mlp.steps)
        wait(need_x)
        x_now = x_s[...]
        a = attention.normed(x_now)
        split_halves(c, a, a1_keep, a1_send)
        r = attention.forward(x_now, a, mask_ref[...], w_qkv, w_out, none, [], o_s, qkv_s, p_s)
        r1[...] = r
        split_halves(c, o_s[...], o_keep, o_send)
        a = mlp.normed(r)
        split_halves(c, a, a2_keep, a2_send)
        y_out[...] = mlp.forward(r, a, w_up, w_down, none, none, act_s, slope_s)
        split_halves(c, act_s[...], act_keep, act_send)
        wait(need_g)
        mid, _, _ = mlp.backward(g_s[...], r1, slope_s, w_up, w_down, none, none)
        (gi, _, _), _ = attention.backward(mid, x_s, qkv_s, p_s, w_qkv, w_out, [], [])
        gi_out[...] = gi

    row, half = ((t, d), BF), ((t, d // 2), BF)
    outs = (row, row, half, half, half, half, half, half, ((t, ff // 2), BF), ((t, ff // 2), BF))
    outs += (row, ((t, 3 * d), BF), ((GROUPS, t, t * HEADS // GROUPS), BF), row, ((t, ff), BF))
    scratch = rooms(row, row, ((t, ff), BF)) + [pltpu.SemaphoreType.DMA((2,))]
    out = call(kernel, scalars, [vectors, mask, *weights], x.arrays + g.arrays, outs, scratch, "layer", 11)
    return out[:10], out[10:]


def mlp_backward(scalars, g, g_other, act, vectors, r1, slope, weights, blocks, splits):
    t, d = r1.shape
    ff = weights[0].shape[1]

    def kernel(s_ref, vec, x_s, slope_s, w_up, act_keep, act_got, down_ref, *refs):
        *refs, g_s, other_s, w_down, sems = refs
        copies = Copies(s_ref[0], sems)
        need_g, refs = g.fetch(copies, s_ref, refs, g_s)
        need_other, refs = g_other.fetch(copies, s_ref, refs, other_s)
        mid_out, du_out, sums, *halves = refs
        chunks = [pl.ds(i * (ff // Mlp.steps), ff // Mlp.steps) for i in range(Mlp.steps)]
        need_down = [copies.start(down_ref.at[chunk], w_down.at[chunk]) for chunk in chunks]
        sub = Mlp(vec, d, ff)
        wait(need_g)
        wait(need_other)
        g_now = g_s[...]
        rows = ff // 2 // blocks
        for piece, (bit, lo) in enumerate(splits):
            cols = slice(piece * PIECE, (piece + 1) * PIECE)
            group = max(2 * lo, blocks // 4)
            for first in range(0, blocks, group):
                part = slice(first * rows, (first + group) * rows)
                out = t_dot(act_keep[:, part], g_s[:, cols]) + t_dot(act_got[:, part], other_s[:, cols])
                out = out.astype(BF).reshape(group, rows, PIECE)
                split_blocks((s_ref[2] >> bit) & 1, lo, out, first, *halves[2 * piece : 2 * piece + 2], slice(None))

        def emit(j, cols, du):
            du_out[:, cols] = du
            sums[:, cols] = col_sum(du)

        none = [[]] * Mlp.steps
        mid, gain, shift = sub.backward(g_now, x_s, slope_s, w_up, w_down, none, need_down, emit)
        mid_out[...] = mid
        for i, m in enumerate((col_sum(g_now), gain, shift, col_sum(mid))):
            sums[:, ff + i * d : ff + (i + 1) * d] = m

    row = ((t, d), BF)
    outs = [row, ((t, ff), BF), ((1, ff + 4 * d), F32)]
    outs += [((blocks // 2, ff // 2 // blocks, PIECE), BF)] * 2 * len(splits)
    scratch = rooms(row, row, ((ff, d), BF)) + [pltpu.SemaphoreType.DMA((2 + Mlp.steps,))]
    held = [vectors, r1, slope, weights[0], *act]
    ins = [weights[1]] + g.arrays + g_other.arrays
    out = call(kernel, scalars, held, ins, outs, scratch, "mlp_backward", 18)
    return (*out[:3], [out[3 + 2 * i : 5 + 2 * i] for i in range(len(splits))])


def attention_backward(scalars, g, vectors, x, qkv, p, weights):
    t, d = x.shape
    ff = vectors.shape[1] - 8 * d

    def kernel(s_ref, vec, x_s, qkv_s, p_s, w_qkv, w_out, g_ref, gi_out, dqkv_out, sums):
        sub = Attention(vec, d, ff)
        (gi, gain, shift), parts = sub.backward(g_ref[...], x_s, qkv_s, p_s, w_qkv, w_out, [], [])
        for i, m in enumerate(parts):
            dqkv_out[:, i * d : (i + 1) * d] = m
        gi_out[...] = gi
        for i, m in enumerate((col_sum(parts[0]), col_sum(parts[2]), gain, shift)):
            sums[:, i * d : (i + 1) * d] = m

    outs = (((t, d), BF), ((t, 3 * d), BF), ((1, 4 * d), F32))
    return call(kernel, scalars, [vectors, x, qkv, p, *weights, g], [], outs, [], "attention_backward", 10)


def weight_grads(scalars, tasks, blocks):
    arrays, outs = [], []

    def index_of(m):
        for i, known in enumerate(arrays):
            if known is m:
                return i
        arrays.append(m)
        return len(arrays) - 1

    tasks = [(tuple(map(index_of, left)), tuple(map(index_of, right)), *rest) for left, right, *rest in tasks]
    for left, _, _, n, _, _ in tasks:
        outs += [((blocks // 2, arrays[left[0]].shape[1] // blocks, n), BF)] * 2

    def kernel(s_ref, *refs):
        ins, targets = refs[: len(arrays)], refs[len(arrays) :]
        for k, (left, right, first, n, bit, lo) in enumerate(tasks):
            for at in range(0, n, PIECE):
                cols = slice(first + at, first + at + PIECE)
                out = sum(t_dot(ins[i][...], ins[j][:, cols]) for i, j in zip(left, right))
                out = out.astype(BF).reshape(blocks, -1, PIECE)
                split_blocks((s_ref[2] >> bit) & 1, lo, out, 0, *targets[2 * k : 2 * k + 2], slice(at, at + PIECE))

    out = call(kernel, scalars, arrays, [], outs, [], "weight_grads", 8)
    return [(out[2 * k], out[2 * k + 1]) for k in range(len(tasks))]


def folded(scalars, mine, got, bit, lo):
    shape = mine.shape

    def kernel(s_ref, a, b, *outs):
        if bit is None:
            outs[0][...] = a[0].astype(F32) + b[0].astype(F32)
            return
        side = (s_ref[2] >> bit) & 1
        for k in range(shape[0] // 2):
            base = k // lo * 2 * lo + k % lo
            for ref, at in ((outs[0], base + side * lo), (outs[1], base + (1 - side) * lo)):
                ref[k] = (a[at].astype(F32) + b[at].astype(F32)).astype(ref.dtype)

    outs = [(shape[1:], F32)] if bit is None else [((shape[0] // 2,) + shape[1:], mine.dtype)] * 2
    return call(kernel, scalars, [mine, got], [], outs, [], "folded", 6)


def core_swap(x):
    return lax.ppermute(x, "section", [(i, i ^ 1) for i in range(lax.axis_size("section"))])


def x_hop(x, pairs):
    return lax.ppermute(x, "section", pairs)


def dp_swap(x, bit):
    return lax.ppermute(x, "dp", [(i, i ^ 1 << bit) for i in range(lax.axis_size("dp"))])


def lower(bits, k):
    return 1 << sum(b < bits[k] for b in bits[k:])


def scatter_steps(scalars, bits, mine, send):
    for k, bit in enumerate(bits):
        got = yield dp_swap(send, bit), send
        if k + 1 < len(bits):
            mine, send = folded(scalars, mine, got, bits[k + 1], lower(bits, k + 1))
    return folded(scalars, mine, got, None, None)[0]


def all_sum_steps(x):
    x = x + (yield core_swap(x), x)
    for bit in range(lax.axis_size("dp").bit_length() - 1):
        x = x + (yield dp_swap(x, bit), x)
    return x


class Order:
    def __init__(self):
        self.last = None
        self.running = {}
        self.results = {}

    def after(self, x):
        if self.last is None:
            return x
        return lax.optimization_barrier((x, self.last))[0]

    def done(self, x):
        self.last = jax.tree.leaves(x)[0]
        return x

    def begin(self, name, steps):
        self.running[name] = (steps, next(steps)[0])

    def drain(self):
        while self.running:
            self.advance(*self.running)

    def advance(self, *names):
        for name in names:
            steps, arriving = self.running.pop(name)
            try:
                arriving, out = steps.send(self.after(arriving))
                self.running[name] = (steps, arriving)
                self.done(out)
            except StopIteration as stop:
                self.results[name] = self.done(stop.value)


KINDS = {"d0": "z", "d1": "y", "u0": "y", "u1": "y", "q": "y", "k": "y", "o": "z", "v": "y"}
STEPS = (
    "sums", "d0", "d1", "grads", "d0", "d1", "u0", "o", "small", "columns", "u0", "u1", "o", "q", "d1", "columns end",
    "k", "u1", "u0", "small", "q", "k", "v", "d0", "small", "q", "u1", "v", "small", "o", "k", "v",
)


def per_device(
    tokens, segments, qkv_weight, qv_bias, out_weight, out_bias, up_weight, up_bias, down_weight, down_bias,
    norm_gain, norm_shift, cotangent,
):
    d = tokens.shape[1]
    t = segments.shape[1]
    section = lax.axis_index("section")
    core, x = section % 2, section // 2
    dp = lax.axis_index("dp")
    n_dp = lax.axis_size("dp")
    later = x == 1
    fwd_pairs, bwd_pairs = [(0, 2), (1, 3)], [(2, 0), (3, 1)]
    scalars = jnp.stack([core, x, dp]).astype(jnp.int32)

    both = lambda m: (m, core_swap(m))
    qkv, out = both(qkv_weight), both(out_weight)
    vectors = [qv_bias, out_bias, up_bias, down_bias, norm_gain, norm_shift]
    vectors = both(jnp.concatenate([m.reshape(1, -1).astype(F32) for m in vectors], axis=1))
    token_rows, cot_rows = tokens.reshape(2, t, d), cotangent.reshape(2, t, d)
    seg = lax.dynamic_index_in_dim(segments, core, 0, False)
    segs = [seg[:, None], seg[None, :]]
    (up_weight, down_weight), qkv, out, vectors, scalars, segs = lax.optimization_barrier(
        ((up_weight, down_weight), qkv, out, vectors, scalars, segs)
    )
    up, down = both(up_weight), both(down_weight)

    r1, w_qkv, w_out, vec, mask = attention_forward(scalars, Chosen(rows=token_rows), segs, *vectors, qkv, out)
    early = x_hop(norm_gain, fwd_pairs + bwd_pairs)
    r2, w_up, w_down = mlp_forward(scalars, r1, vec, up, down, early)
    entering = Chosen(rows=token_rows, other=x_hop(r2, fwd_pairs))
    outs, held = layer(scalars, entering, Chosen(rows=cot_rows), vec, mask, (w_qkv, w_out, w_up, w_down))
    r2, g0, a1_keep, a1_send, o_keep, o_send, a2_keep, a2_send, act_keep, act_send = outs
    x_held, qkv, p, r1, slope = held

    swaps = ((a1_keep, a1_send), (o_keep, o_send), (a2_keep, a2_send), (act_keep, act_send))
    a1, o, a2, act = ((keep, core_swap(send)) for keep, send in swaps)

    hopped = x_hop(g0, bwd_pairs)
    hopped, hopped_other, a1, o, a2, act = lax.optimization_barrier((hopped, core_swap(hopped), a1, o, a2, act))
    g_own = Chosen(rows=cot_rows, other=hopped, at=0)
    g_other = Chosen(rows=cot_rows, other=hopped_other, at=0, flip=True)
    bits = list(range(n_dp.bit_length() - 1))
    kinds = {"y": bits, "z": bits[1:] + bits[:1], "c": bits[1:2] + bits[:1] + bits[2:]}
    kinds = {name: kinds[kind] for name, kind in KINDS.items()}
    first_half = lambda name: (kinds[name][0], lower(kinds[name], 0))
    g_attn, du, mlp_sums, downs = mlp_backward(
        scalars, g_own, g_other, act, vec, r1, slope, (w_up, w_down), n_dp, [first_half(n) for n in ("d0", "d1")]
    )
    du, g_attn_all = both(du), both(g_attn)
    order = Order()

    def begin(names, rights):
        rights = order.after(rights)
        tasks = []
        for name in names:
            left, right, first, n = sources[name]
            tasks.append((left, rights[right], first, n, *first_half(name)))
        for name, pair in zip(names, order.done(weight_grads(scalars, tasks, n_dp))):
            order.begin(name, scatter_steps(scalars, kinds[name], *pair))

    for name, pair in zip(("d0", "d1"), downs):
        order.begin(name, scatter_steps(scalars, kinds[name], *order.done(pair)))
    ff = up_weight.shape[1]
    named = lambda base: [name for name in kinds if name[0] == base]
    sources = {}
    for base, left, right, first, n in (
        ("u", a2, "du", 0, ff), ("q", a1, "dqkv", 0, d), ("k", a1, "dqkv", d, d), ("v", a1, "dqkv", 2 * d, d),
        ("o", o, "g", 0, d),
    ):
        width = n // len(named(base))
        for i, name in enumerate(named(base)):
            sources[name] = (left, right, first + i * width, width)
    begin(named("u"), {"du": du})
    g_in, dqkv, attn_sums = order.done(
        attention_backward(scalars, order.after(g_attn), vec, x_held, qkv, p, (w_qkv, w_out))
    )
    dqkv = both(dqkv)
    crossed = x_hop(jnp.where(later, r2[:, : d // 2], g_in[:, d // 2 :]), fwd_pairs + bwd_pairs)

    def columns(here, there, keep_side):
        mine = jnp.where(keep_side, here, there)
        half = mine.shape[1] // 2
        part = lambda index: lax.dynamic_slice_in_dim(mine, index * half, half, 1)
        own, other = part(core), core_swap(part(1 - core))
        return jnp.where(core == 0, jnp.concatenate([own, other]), jnp.concatenate([other, own]))

    for name in STEPS:
        if name == "sums":
            small = jnp.concatenate(order.after([mlp_sums, attn_sums]), axis=1)
            order.begin("small", all_sum_steps(order.done(small)))
        elif name == "grads":
            begin([n for n in kinds if n[0] in "qkvo"], {"g": g_attn_all, "dqkv": dqkv})
        elif name == "columns":
            crossed = order.after(crossed)
            block_output = columns(r2[:, d // 2 :], crossed, later)
            input_gradient = columns(g_in[:, : d // 2], crossed, jnp.logical_not(later))
        elif name == "columns end":
            block_output, input_gradient = order.done(order.after((block_output, input_gradient)))
        else:
            order.advance(name)
    order.drain()
    done = order.results
    vectors = []
    small = done["small"][0]
    at, parts = 0, {}
    for name, width in zip(("up", "down", "gain1", "shift1", "out", "q", "v", "gain0", "shift0"), (ff,) + (d,) * 8):
        parts[name] = small[at : at + width]
        at += width
    for names in (("q", "v"), ("out",), ("up",), ("down",), ("gain0", "gain1"), ("shift0", "shift1")):
        vector = jnp.concatenate([parts[name] for name in names])
        part = vector.shape[0] // (2 * n_dp)
        vectors.append(lax.dynamic_slice_in_dim(vector, (core * n_dp + dp) * part, part))
    g_qv, g_out_b, g_up_b, g_down_b, g_gain, g_shift = vectors
    joined = lambda bases: jnp.concatenate([done[name] for base in bases for name in named(base)], axis=1)
    return (
        block_output,
        input_gradient,
        joined("qkv"),
        g_qv,
        joined("o"),
        g_out_b,
        joined("u"),
        g_up_b,
        joined("d"),
        g_down_b,
        g_gain[None],
        g_shift[None],
    )


def solution(mesh):
    placed = (
        P("dp", None), P("dp", None), P("section", None), P("section"), P("section", None), P("section"),
        P("section", None), P("section"), P("section", None), P("section"), P("section", None), P("section", None),
        P("dp", None),
    )
    both = ("section", "dp")
    return jax.shard_map(
        per_device,
        mesh=mesh,
        in_specs=placed,
        out_specs=(
            P("dp", "section"), P("dp", "section"), P(both, None), P(both), P(both, None), P(both), P(both, None),
            P(both), P(both, None), P(both), P("section", "dp"), P("section", "dp"),
        ),
        check_vma=False,
    )
```

```python
import jax
import jax.numpy as jnp
from jax import lax
from jax.experimental import pallas as pl
from jax.experimental.pallas import tpu as pltpu
from jax.sharding import PartitionSpec as P

HEADS = 16
EPSILON = 1e-06
BF = jnp.bfloat16
F32 = jnp.float32
MIB = 1024 * 1024
PIECE = 512
ANYWHERE = pl.BlockSpec(memory_space=pl.ANY)
IN_VMEM = pl.BlockSpec(memory_space=pltpu.VMEM)


def dot(a, b):
    return jnp.dot(a, b, preferred_element_type=F32)


def dot_t(a, b):
    return lax.dot_general(a, b, (((1,), (1,)), ((), ())), preferred_element_type=F32)


def t_dot(a, b):
    return lax.dot_general(a, b, (((0,), (0,)), ((), ())), preferred_element_type=F32)


def call(kernel, scalars, held, ins, outs, scratch, name, mib):
    return pl.pallas_call(
        kernel,
        in_specs=[pl.BlockSpec(memory_space=pltpu.SMEM)] + [IN_VMEM] * len(held) + [ANYWHERE] * len(ins),
        out_specs=[IN_VMEM] * len(outs),
        out_shape=[pltpu.VMEM(shape, dtype) for shape, dtype in outs],
        scratch_shapes=scratch,
        compiler_params=pltpu.CompilerParams(vmem_limit_bytes=mib * MIB),
        cost_estimate=pl.CostEstimate(flops=0, bytes_accessed=0, transcendentals=0),
        name=name,
    )(scalars, *held, *ins)


def rooms(*pairs):
    return [pltpu.VMEM(shape, dtype) for shape, dtype in pairs]


class Copies:
    def __init__(self, core, sems):
        self.core, self.sems, self.used = core, sems, 0

    def start(self, source, target):
        copy = pltpu.make_async_copy(source, target, self.sems.at[self.used])
        self.used += 1
        copy.start()
        return [copy]

    def columns(self, own, got, target, first, width):
        half = own.shape[0]
        cols = pl.ds(first, width)
        out = []
        for source, at in ((own, self.core), (got, 1 - self.core)):
            rows = pl.ds(pl.multiple_of(at * half, half), half)
            out += self.start(source.at[:, cols], target.at[rows, cols])
        return out

    def either(self, first, source, other, target):
        sem = self.sems.at[self.used]
        self.used += 1

        @pl.when(first)
        def _():
            pltpu.make_async_copy(source, target, sem).start()

        @pl.when(jnp.logical_not(first))
        def _():
            pltpu.make_async_copy(other, target, sem).start()

        return [pltpu.make_async_copy(source, target, sem)]

    def rows(self, own, got, target, first, count):
        half = own.shape[0]
        here = pl.ds(first % half, count)
        return self.either(self.core == first // half, own.at[here], got.at[here], target.at[pl.ds(first, count)])


def wait(copies):
    for copy in copies:
        copy.wait()


def split_halves(core, value, keep, send):
    half = value.shape[1] // 2
    low, high = value[:, :half], value[:, half:]
    keep[...] = jnp.where(core == 0, low, high)
    send[...] = jnp.where(core == 0, high, low)


def split_blocks(side, lo, value, first, keep, send, cols):
    for k in range(value.shape[0]):
        at = first + k
        if at // lo % 2 == 0:
            to, a, b = at // (2 * lo) * lo + at % lo, value[k], value[k + lo]
            keep[to, :, cols] = jnp.where(side == 0, a, b)
            send[to, :, cols] = jnp.where(side == 0, b, a)


class Chosen:
    def __init__(self, array=None, rows=None, other=None, at=1, flip=False):
        self.arrays = [m for m in (array, rows, other) if m is not None]
        self.by_core, self.at, self.flip = rows is not None, at, flip

    def shape(self):
        return self.arrays[0].shape[-2:]

    def fetch(self, copies, scalars, refs, target):
        row = 1 - scalars[0] if self.flip else scalars[0]
        here = refs[0].at[row] if self.by_core else refs[0]
        if len(self.arrays) == 1:
            return copies.start(here, target), refs[1:]
        return copies.either(scalars[1] == self.at, refs[1], here, target), refs[2:]


def centered(x):
    r = x.astype(F32)
    center = r - jnp.mean(r, axis=-1, keepdims=True)
    spread = jnp.mean(center * center, axis=-1, keepdims=True)
    scale = lax.rsqrt(spread + EPSILON)
    return center * scale, scale


def norm_backward(da, x, gain, g):
    xhat, scale = centered(x)
    dx = da * gain
    dr = scale * (
        dx - jnp.mean(dx, axis=-1, keepdims=True) - xhat * jnp.mean(dx * xhat, axis=-1, keepdims=True)
    )
    return (
        (g.astype(F32) + dr).astype(BF),
        jnp.sum(da * xhat, axis=0, keepdims=True),
        jnp.sum(da, axis=0, keepdims=True),
    )


GROUPS = 4


def head_blocks(m, dh):
    head = lax.broadcasted_iota(jnp.int32, (1, m.shape[1]), 1) // dh
    zero = jnp.zeros((), m.dtype)
    return jnp.concatenate([jnp.where(head == h, m, zero) for h in range(m.shape[1] // dh)], axis=0)


def stacked(m, t):
    return jnp.concatenate([m[:, i : i + t] for i in range(0, m.shape[1], t)], axis=0)


def vector_places(d, ff):
    names = ("q", "v", "out", "down", "gain0", "gain1", "shift0", "shift1")
    places = {name: slice(i * d, (i + 1) * d) for i, name in enumerate(names)}
    places["up"] = slice(8 * d, 8 * d + ff)
    return places


class Attention:
    def __init__(self, vectors, d, ff):
        at = vector_places(d, ff)
        self.b_q, self.b_v, self.b_out = (vectors[:, at[name]] for name in ("q", "v", "out"))
        self.gain, self.shift = vectors[:, at["gain0"]], vectors[:, at["shift0"]]

    @staticmethod
    def fetch(copies, qkv, out, w_qkv, w_out, out_first=False):
        d = w_out.shape[0]
        gw = d // GROUPS
        need, need_out = [], []

        def fetch_out():
            for j in range(2):
                need_out.extend(copies.rows(*out, w_out, j * (d // 2), d // 2))

        if out_first:
            fetch_out()
        for j in range(GROUPS):
            need.append([])
            for i in range(3):
                need[j] += copies.columns(*qkv, w_qkv, i * d + j * gw, gw)
        if not out_first:
            fetch_out()
        return need, need_out

    def normed(self, x):
        xhat, _ = centered(x)
        return (xhat * self.gain + self.shift).astype(BF)

    def forward(self, x, a, mask, w_qkv, w_out, need, need_out, o_s, qkv_s=None, p_s=None):
        t, d = x.shape
        gw, dh = d // GROUPS, d // HEADS
        mask = jnp.concatenate([mask] * (gw // dh), axis=1)

        def project(j):
            wait(need[j])
            cols = [slice(i * d + j * gw, i * d + (j + 1) * gw) for i in range(3)]
            q, k, v = (dot(a, w_qkv[:, s]) for s in cols)
            q = (q + self.b_q[:, j * gw : (j + 1) * gw]).astype(BF)
            k = k.astype(BF)
            v = (v + self.b_v[:, j * gw : (j + 1) * gw]).astype(BF)
            if qkv_s is not None:
                for i, m in enumerate((q, k, v)):
                    qkv_s[:, cols[i]] = m
            return q, k, v

        now = project(0)
        for j in range(GROUPS):
            q, k, v = now
            s = dot_t(k, head_blocks(q * jnp.asarray(dh**-0.5, BF), dh)) + mask
            if j + 1 < GROUPS:
                now = project(j + 1)
            e = jnp.exp(s - jnp.max(s, axis=0, keepdims=True))
            p = (e * (1.0 / jnp.sum(e, axis=0, keepdims=True))).astype(BF)
            if p_s is not None:
                p_s[j] = p
            o_s[:, j * gw : (j + 1) * gw] = t_dot(stacked(p, t), head_blocks(v, dh)).astype(BF)
        wait(need_out)
        return (x.astype(F32) + self.b_out + dot(o_s[...], w_out[...])).astype(BF)

    def backward(self, g, x, qkv_s, p_s, w_qkv, w_out, need, need_out, need_p=None, need_x=()):
        t, d = g.shape
        gw, dh = d // GROUPS, d // HEADS
        wait(need_out)
        parts = [[], [], []]
        for j in range(GROUPS):
            if need_p is not None:
                wait(need_p[j])
            do = dot_t(g, w_out[j * gw : (j + 1) * gw, :]).astype(BF)
            q, k, v = (qkv_s[:, i * d + j * gw : i * d + (j + 1) * gw] for i in range(3))
            do = head_blocks(do, dh)
            p = p_s[j]
            pf = p.astype(F32)
            w_ = pf * dot_t(v, do)
            ds = (w_ - pf * jnp.sum(w_, axis=0, keepdims=True)).astype(BF)
            dv = dot(p, do)
            dk = dot(ds, head_blocks(q, dh))
            dq = t_dot(stacked(ds, t), head_blocks(k, dh))
            scale = dh**-0.5
            for i, m in enumerate((dq * scale, dk * scale, dv)):
                parts[i].append(m.astype(BF))
        parts = [jnp.concatenate(m, axis=1) for m in parts]
        for m in need:
            wait(m)
        da = sum(dot_t(m, w_qkv[:, i * d : (i + 1) * d]) for i, m in enumerate(parts))
        wait(need_x)
        return norm_backward(da, x[...], self.gain, g), parts


class Mlp:
    steps = 4

    def __init__(self, vectors, d, ff):
        at = vector_places(d, ff)
        self.b_up, self.b_down = vectors[:, at["up"]], vectors[:, at["down"]]
        self.gain, self.shift = vectors[:, at["gain1"]], vectors[:, at["shift1"]]

    @classmethod
    def fetch(cls, copies, up, down, w_up, w_down, down_first=False):
        tw = w_up.shape[1] // cls.steps
        need_up, need_down = [], []
        for j in range(cls.steps):
            if down_first:
                need_down.append(copies.rows(*down, w_down, j * tw, tw))
            need_up.append(copies.columns(*up, w_up, j * tw, tw))
            if not down_first:
                need_down.append(copies.rows(*down, w_down, j * tw, tw))
        return need_up, need_down

    def normed(self, x):
        xhat, _ = centered(x)
        return (xhat * self.gain + self.shift).astype(BF)

    def forward(self, x, a, w_up, w_down, need_up, need_down, act_s=None, slope_s=None):
        tw = w_up.shape[1] // self.steps

        def hidden(j):
            wait(need_up[j])
            return dot(a, w_up[:, j * tw : (j + 1) * tw]) + self.b_up[:, j * tw : (j + 1) * tw]

        total = x.astype(F32) + self.b_down
        u = hidden(0)
        for j in range(self.steps):
            cols = slice(j * tw, (j + 1) * tw)
            later = hidden(j + 1) if j + 1 < self.steps else None
            phi = 0.5 + 0.5 * lax.erf(u * 0.5**0.5)
            act = (u * phi).astype(BF)
            if act_s is not None:
                act_s[:, cols] = act
                slope_s[:, cols] = (phi + u * (jnp.exp(-0.5 * u * u) * (2 * jnp.pi) ** -0.5)).astype(BF)
            wait(need_down[j])
            total += dot(act, w_down[cols, :])
            u = later
        return total.astype(BF)

    def backward(self, g, x, slope_s, w_up, w_down, need_up, need_down, emit=None, need_slope=(), need_x=()):
        tw = w_up.shape[1] // self.steps

        def incoming(j):
            wait(need_down[j])
            return dot_t(g, w_down[j * tw : (j + 1) * tw, :])

        da = None
        dg = incoming(0)
        wait(need_slope)
        for j in range(self.steps):
            cols = slice(j * tw, (j + 1) * tw)
            du = (dg * slope_s[:, cols].astype(F32)).astype(BF)
            dg = incoming(j + 1) if j + 1 < self.steps else None
            if emit is not None:
                emit(j, cols, du)
            wait(need_up[j])
            part = dot_t(du, w_up[:, cols])
            da = part if da is None else da + part
        wait(need_x)
        return norm_backward(da, x[...], self.gain, g)


def col_sum(m):
    return jnp.sum(m.astype(F32), axis=0, keepdims=True)


def attention_forward(scalars, x, segs, own, got, qkv, out):
    t, d = x.shape()
    ff = 2 * own.shape[1] - 8 * d

    def kernel(s_ref, *refs):
        c = s_ref[0]
        y_out, w_qkv, w_out, vectors, mask, o_s, x_s, own_s, got_s, r_s, c_s, sems = refs[-12:]
        copies = Copies(c, sems)
        need_x, refs = x.fetch(copies, s_ref, refs[:-12], x_s)
        seg_r, seg_c, own_ref, got_ref, qo, qg, oo, og = refs
        need_v = copies.start(own_ref, own_s) + copies.start(got_ref, got_s)
        need_m = copies.start(seg_r, r_s) + copies.start(seg_c, c_s)
        need, need_out = Attention.fetch(copies, (qo, qg), (oo, og), w_qkv, w_out)
        wait(need_v)
        at = vector_places(d, ff)
        low, high = jnp.where(c == 0, own_s[...], got_s[...]), jnp.where(c == 0, got_s[...], own_s[...])
        first = 0
        for names, width in (
            (("q", "v"), d), (("out",), d // 2), (("up",), ff // 2), (("down",), d // 2),
            (("gain0", "gain1"), d), (("shift0", "shift1"), d),
        ):
            places = [at[name] for name in names]
            if len(places) == 1:
                start = places[0].start
                places = [slice(start, start + width), slice(start + width, start + 2 * width)]
            for place, half in zip(places, (low, high)):
                vectors[:, place] = half[:, first : first + width]
            first += width
        wait(need_m)
        mask[...] = jnp.where(r_s[...] == c_s[...], 0.0, -1e30)
        sub = Attention(vectors, d, ff)
        wait(need_x)
        x_now = x_s[...]
        y_out[...] = sub.forward(x_now, sub.normed(x_now), mask[...], w_qkv, w_out, need, need_out, o_s)

    row = ((t, d), BF)
    ins = x.arrays + [*segs, own, got, *qkv, *out]
    outs = (row, ((d, 3 * d), BF), ((d, d), BF), ((1, 8 * d + ff), F32), ((t, t), F32))
    scratch = rooms(row, row, (own.shape, F32), (own.shape, F32), ((t, 1), jnp.int32), ((1, t), jnp.int32))
    scratch += [pltpu.SemaphoreType.DMA((6 * GROUPS + 7,))]
    return call(kernel, scalars, [], ins, outs, scratch, "attention_forward", 44)


def mlp_forward(scalars, x, vectors, up, down, early):
    t, d = x.shape
    ff = up[0].shape[1]

    def kernel(s_ref, vec, x_ref, uo, ug, do, dg, _, y_out, w_up, w_down, sems):
        need_up, need_down = Mlp.fetch(Copies(s_ref[0], sems), (uo, ug), (do, dg), w_up, w_down)
        sub = Mlp(vec, d, ff)
        x_now = x_ref[...]
        y_out[...] = sub.forward(x_now, sub.normed(x_now), w_up, w_down, need_up, need_down)

    outs = (((t, d), BF), ((d, ff), BF), ((ff, d), BF))
    scratch = [pltpu.SemaphoreType.DMA((3 * Mlp.steps,))]
    return call(kernel, scalars, [vectors, x], [*up, *down, early], outs, scratch, "mlp_forward", 8)


def layer(scalars, x, g, vectors, mask, weights):
    t, d = x.shape()
    ff = weights[2].shape[1]

    def kernel(s_ref, vec, mask_ref, w_qkv, w_out, w_up, w_down, *refs):
        *refs, g_s, o_s, act_s, sems = refs
        x_s, qkv_s, p_s, r1, slope_s = refs[-5:]
        c = s_ref[0]
        copies = Copies(c, sems)
        need_x, refs = x.fetch(copies, s_ref, refs[:-5], x_s)
        need_g, outs = g.fetch(copies, s_ref, refs, g_s)
        y_out, gi_out, a1_keep, a1_send, o_keep, o_send, a2_keep, a2_send, act_keep, act_send = outs
        attention, mlp = Attention(vec, d, ff), Mlp(vec, d, ff)
        none = [[]] * max(GROUPS, Mlp.steps)
        wait(need_x)
        x_now = x_s[...]
        a = attention.normed(x_now)
        split_halves(c, a, a1_keep, a1_send)
        r = attention.forward(x_now, a, mask_ref[...], w_qkv, w_out, none, [], o_s, qkv_s, p_s)
        r1[...] = r
        split_halves(c, o_s[...], o_keep, o_send)
        a = mlp.normed(r)
        split_halves(c, a, a2_keep, a2_send)
        y_out[...] = mlp.forward(r, a, w_up, w_down, none, none, act_s, slope_s)
        split_halves(c, act_s[...], act_keep, act_send)
        wait(need_g)
        mid, _, _ = mlp.backward(g_s[...], r1, slope_s, w_up, w_down, none, none)
        (gi, _, _), _ = attention.backward(mid, x_s, qkv_s, p_s, w_qkv, w_out, [], [])
        gi_out[...] = gi

    row, half = ((t, d), BF), ((t, d // 2), BF)
    outs = (row, row, half, half, half, half, half, half, ((t, ff // 2), BF), ((t, ff // 2), BF))
    outs += (row, ((t, 3 * d), BF), ((GROUPS, t, t * HEADS // GROUPS), BF), row, ((t, ff), BF))
    scratch = rooms(row, row, ((t, ff), BF)) + [pltpu.SemaphoreType.DMA((2,))]
    out = call(kernel, scalars, [vectors, mask, *weights], x.arrays + g.arrays, outs, scratch, "layer", 11)
    return out[:10], out[10:]


def mlp_backward(scalars, g, g_other, act, vectors, r1, slope, weights, blocks, splits):
    t, d = r1.shape
    ff = weights[0].shape[1]

    def kernel(s_ref, vec, x_s, slope_s, w_up, act_keep, act_got, down_ref, *refs):
        *refs, g_s, other_s, w_down, sems = refs
        copies = Copies(s_ref[0], sems)
        need_g, refs = g.fetch(copies, s_ref, refs, g_s)
        need_other, refs = g_other.fetch(copies, s_ref, refs, other_s)
        mid_out, du_out, sums, *halves = refs
        chunks = [pl.ds(i * (ff // Mlp.steps), ff // Mlp.steps) for i in range(Mlp.steps)]
        need_down = [copies.start(down_ref.at[chunk], w_down.at[chunk]) for chunk in chunks]
        sub = Mlp(vec, d, ff)
        wait(need_g)
        wait(need_other)
        g_now = g_s[...]
        rows = ff // 2 // blocks
        for piece, (bit, lo) in enumerate(splits):
            cols = slice(piece * PIECE, (piece + 1) * PIECE)
            group = max(2 * lo, blocks // 4)
            for first in range(0, blocks, group):
                part = slice(first * rows, (first + group) * rows)
                out = t_dot(act_keep[:, part], g_s[:, cols]) + t_dot(act_got[:, part], other_s[:, cols])
                out = out.astype(BF).reshape(group, rows, PIECE)
                split_blocks((s_ref[2] >> bit) & 1, lo, out, first, *halves[2 * piece : 2 * piece + 2], slice(None))

        def emit(j, cols, du):
            du_out[:, cols] = du
            sums[:, cols] = col_sum(du)

        none = [[]] * Mlp.steps
        mid, gain, shift = sub.backward(g_now, x_s, slope_s, w_up, w_down, none, need_down, emit)
        mid_out[...] = mid
        for i, m in enumerate((col_sum(g_now), gain, shift, col_sum(mid))):
            sums[:, ff + i * d : ff + (i + 1) * d] = m

    row = ((t, d), BF)
    outs = [row, ((t, ff), BF), ((1, ff + 4 * d), F32)]
    outs += [((blocks // 2, ff // 2 // blocks, PIECE), BF)] * 2 * len(splits)
    scratch = rooms(row, row, ((ff, d), BF)) + [pltpu.SemaphoreType.DMA((2 + Mlp.steps,))]
    held = [vectors, r1, slope, weights[0], *act]
    ins = [weights[1]] + g.arrays + g_other.arrays
    out = call(kernel, scalars, held, ins, outs, scratch, "mlp_backward", 18)
    return (*out[:3], [out[3 + 2 * i : 5 + 2 * i] for i in range(len(splits))])


def attention_backward(scalars, g, vectors, x, qkv, p, weights):
    t, d = x.shape
    ff = vectors.shape[1] - 8 * d

    def kernel(s_ref, vec, x_s, qkv_s, p_s, w_qkv, w_out, g_ref, gi_out, dqkv_out, sums):
        sub = Attention(vec, d, ff)
        (gi, gain, shift), parts = sub.backward(g_ref[...], x_s, qkv_s, p_s, w_qkv, w_out, [], [])
        for i, m in enumerate(parts):
            dqkv_out[:, i * d : (i + 1) * d] = m
        gi_out[...] = gi
        for i, m in enumerate((col_sum(parts[0]), col_sum(parts[2]), gain, shift)):
            sums[:, i * d : (i + 1) * d] = m

    outs = (((t, d), BF), ((t, 3 * d), BF), ((1, 4 * d), F32))
    return call(kernel, scalars, [vectors, x, qkv, p, *weights, g], [], outs, [], "attention_backward", 10)


def weight_grads(scalars, tasks, blocks):
    arrays, outs = [], []

    def index_of(m):
        for i, known in enumerate(arrays):
            if known is m:
                return i
        arrays.append(m)
        return len(arrays) - 1

    tasks = [(tuple(map(index_of, left)), tuple(map(index_of, right)), *rest) for left, right, *rest in tasks]
    for left, _, _, n, _, _ in tasks:
        outs += [((blocks // 2, arrays[left[0]].shape[1] // blocks, n), BF)] * 2

    def kernel(s_ref, *refs):
        ins, targets = refs[: len(arrays)], refs[len(arrays) :]
        for k, (left, right, first, n, bit, lo) in enumerate(tasks):
            for at in range(0, n, PIECE):
                cols = slice(first + at, first + at + PIECE)
                out = sum(t_dot(ins[i][...], ins[j][:, cols]) for i, j in zip(left, right))
                out = out.astype(BF).reshape(blocks, -1, PIECE)
                split_blocks((s_ref[2] >> bit) & 1, lo, out, 0, *targets[2 * k : 2 * k + 2], slice(at, at + PIECE))

    out = call(kernel, scalars, arrays, [], outs, [], "weight_grads", 8)
    return [(out[2 * k], out[2 * k + 1]) for k in range(len(tasks))]


def folded(scalars, mine, got, bit, lo):
    shape = mine.shape

    def kernel(s_ref, a, b, *outs):
        if bit is None:
            outs[0][...] = a[0].astype(F32) + b[0].astype(F32)
            return
        side = (s_ref[2] >> bit) & 1
        for k in range(shape[0] // 2):
            base = k // lo * 2 * lo + k % lo
            for ref, at in ((outs[0], base + side * lo), (outs[1], base + (1 - side) * lo)):
                ref[k] = (a[at].astype(F32) + b[at].astype(F32)).astype(ref.dtype)

    outs = [(shape[1:], F32)] if bit is None else [((shape[0] // 2,) + shape[1:], mine.dtype)] * 2
    return call(kernel, scalars, [mine, got], [], outs, [], "folded", 6)


def core_swap(x):
    return lax.ppermute(x, "section", [(i, i ^ 1) for i in range(lax.axis_size("section"))])


def x_hop(x, pairs):
    return lax.ppermute(x, "section", pairs)


def dp_swap(x, bit):
    return lax.ppermute(x, "dp", [(i, i ^ 1 << bit) for i in range(lax.axis_size("dp"))])


def lower(bits, k):
    return 1 << sum(b < bits[k] for b in bits[k:])


def scatter_steps(scalars, bits, mine, send):
    for k, bit in enumerate(bits):
        got = yield dp_swap(send, bit), send
        if k + 1 < len(bits):
            mine, send = folded(scalars, mine, got, bits[k + 1], lower(bits, k + 1))
    return folded(scalars, mine, got, None, None)[0]


def all_sum_steps(x):
    x = x + (yield core_swap(x), x)
    for bit in range(lax.axis_size("dp").bit_length() - 1):
        x = x + (yield dp_swap(x, bit), x)
    return x


class Order:
    def __init__(self):
        self.last = None
        self.running = {}
        self.results = {}

    def after(self, x):
        if self.last is None:
            return x
        return lax.optimization_barrier((x, self.last))[0]

    def done(self, x):
        self.last = jax.tree.leaves(x)[0]
        return x

    def begin(self, name, steps):
        self.running[name] = (steps, next(steps)[0])

    def drain(self):
        while self.running:
            self.advance(*self.running)

    def advance(self, *names):
        for name in names:
            steps, arriving = self.running.pop(name)
            try:
                arriving, out = steps.send(self.after(arriving))
                self.running[name] = (steps, arriving)
                self.done(out)
            except StopIteration as stop:
                self.results[name] = self.done(stop.value)


KINDS = {"d0": "z", "d1": "y", "u0": "y", "u1": "y", "q": "y", "k": "y", "o": "z", "v": "y"}
STEPS = (
    "sums", "d0", "d1", "grads", "d0", "d1", "u0", "o", "small", "columns", "u0", "u1", "o", "q", "d1", "columns end",
    "k", "u1", "u0", "small", "q", "k", "v", "d0", "small", "q", "u1", "v", "small", "o", "k", "v",
)


def per_device(
    tokens, segments, qkv_weight, qv_bias, out_weight, out_bias, up_weight, up_bias, down_weight, down_bias,
    norm_gain, norm_shift, cotangent,
):
    d = tokens.shape[1]
    t = segments.shape[1]
    section = lax.axis_index("section")
    core, x = section % 2, section // 2
    dp = lax.axis_index("dp")
    n_dp = lax.axis_size("dp")
    later = x == 1
    fwd_pairs, bwd_pairs = [(0, 2), (1, 3)], [(2, 0), (3, 1)]
    scalars = jnp.stack([core, x, dp]).astype(jnp.int32)

    both = lambda m: (m, core_swap(m))
    qkv, out = both(qkv_weight), both(out_weight)
    vectors = [qv_bias, out_bias, up_bias, down_bias, norm_gain, norm_shift]
    vectors = both(jnp.concatenate([m.reshape(1, -1).astype(F32) for m in vectors], axis=1))
    token_rows, cot_rows = tokens.reshape(2, t, d), cotangent.reshape(2, t, d)
    seg = lax.dynamic_index_in_dim(segments, core, 0, False)
    segs = [seg[:, None], seg[None, :]]
    (up_weight, down_weight), qkv, out, vectors, scalars, segs = lax.optimization_barrier(
        ((up_weight, down_weight), qkv, out, vectors, scalars, segs)
    )
    up, down = both(up_weight), both(down_weight)

    r1, w_qkv, w_out, vec, mask = attention_forward(scalars, Chosen(rows=token_rows), segs, *vectors, qkv, out)
    early = x_hop(norm_gain, fwd_pairs + bwd_pairs)
    r2, w_up, w_down = mlp_forward(scalars, r1, vec, up, down, early)
    entering = Chosen(rows=token_rows, other=x_hop(r2, fwd_pairs))
    outs, held = layer(scalars, entering, Chosen(rows=cot_rows), vec, mask, (w_qkv, w_out, w_up, w_down))
    r2, g0, a1_keep, a1_send, o_keep, o_send, a2_keep, a2_send, act_keep, act_send = outs
    x_held, qkv, p, r1, slope = held

    swaps = ((a1_keep, a1_send), (o_keep, o_send), (a2_keep, a2_send), (act_keep, act_send))
    a1, o, a2, act = ((keep, core_swap(send)) for keep, send in swaps)

    hopped = x_hop(g0, bwd_pairs)
    hopped, hopped_other, a1, o, a2, act = lax.optimization_barrier((hopped, core_swap(hopped), a1, o, a2, act))
    g_own = Chosen(rows=cot_rows, other=hopped, at=0)
    g_other = Chosen(rows=cot_rows, other=hopped_other, at=0, flip=True)
    bits = list(range(n_dp.bit_length() - 1))
    kinds = {"y": bits, "z": bits[1:] + bits[:1], "c": bits[1:2] + bits[:1] + bits[2:]}
    kinds = {name: kinds[kind] for name, kind in KINDS.items()}
    first_half = lambda name: (kinds[name][0], lower(kinds[name], 0))
    g_attn, du, mlp_sums, downs = mlp_backward(
        scalars, g_own, g_other, act, vec, r1, slope, (w_up, w_down), n_dp, [first_half(n) for n in ("d0", "d1")]
    )
    du, g_attn_all = both(du), both(g_attn)
    order = Order()

    def begin(names, rights):
        rights = order.after(rights)
        tasks = []
        for name in names:
            left, right, first, n = sources[name]
            tasks.append((left, rights[right], first, n, *first_half(name)))
        for name, pair in zip(names, order.done(weight_grads(scalars, tasks, n_dp))):
            order.begin(name, scatter_steps(scalars, kinds[name], *pair))

    for name, pair in zip(("d0", "d1"), downs):
        order.begin(name, scatter_steps(scalars, kinds[name], *order.done(pair)))
    ff = up_weight.shape[1]
    named = lambda base: [name for name in kinds if name[0] == base]
    sources = {}
    for base, left, right, first, n in (
        ("u", a2, "du", 0, ff), ("q", a1, "dqkv", 0, d), ("k", a1, "dqkv", d, d), ("v", a1, "dqkv", 2 * d, d),
        ("o", o, "g", 0, d),
    ):
        width = n // len(named(base))
        for i, name in enumerate(named(base)):
            sources[name] = (left, right, first + i * width, width)
    begin(named("u"), {"du": du})
    g_in, dqkv, attn_sums = order.done(
        attention_backward(scalars, order.after(g_attn), vec, x_held, qkv, p, (w_qkv, w_out))
    )
    dqkv = both(dqkv)
    crossed = x_hop(jnp.where(later, r2[:, : d // 2], g_in[:, d // 2 :]), fwd_pairs + bwd_pairs)

    def columns(here, there, keep_side):
        mine = jnp.where(keep_side, here, there)
        half = mine.shape[1] // 2
        part = lambda index: lax.dynamic_slice_in_dim(mine, index * half, half, 1)
        own, other = part(core), core_swap(part(1 - core))
        return jnp.where(core == 0, jnp.concatenate([own, other]), jnp.concatenate([other, own]))

    def vector_parts(small):
        vectors = []
        small = small[0]
        at, parts = 0, {}
        for name, width in zip(("up", "down", "gain1", "shift1", "out", "q", "v", "gain0", "shift0"), (ff,) + (d,) * 8):
            parts[name] = small[at : at + width]
            at += width
        for names in (("q", "v"), ("out",), ("up",), ("down",), ("gain0", "gain1"), ("shift0", "shift1")):
            vector = jnp.concatenate([parts[name] for name in names])
            part = vector.shape[0] // (2 * n_dp)
            vectors.append(lax.dynamic_slice_in_dim(vector, (core * n_dp + dp) * part, part))
        return vectors

    vectors = []
    for name in STEPS:
        if name == "sums":
            small = jnp.concatenate(order.after([mlp_sums, attn_sums]), axis=1)
            order.begin("small", all_sum_steps(order.done(small)))
        elif name == "grads":
            begin([n for n in kinds if n[0] in "qkvo"], {"g": g_attn_all, "dqkv": dqkv})
        elif name == "columns":
            crossed = order.after(crossed)
            block_output = columns(r2[:, d // 2 :], crossed, later)
            input_gradient = columns(g_in[:, : d // 2], crossed, jnp.logical_not(later))
        elif name == "columns end":
            block_output, input_gradient = order.done(order.after((block_output, input_gradient)))
        else:
            order.advance(name)
            if name in order.results and name == "small":
                order.last = vectors = vector_parts(order.results[name])
    order.drain()
    if not vectors:
        vectors = vector_parts(order.results["small"])
    done = order.results
    g_qv, g_out_b, g_up_b, g_down_b, g_gain, g_shift = vectors
    joined = lambda bases: jnp.concatenate([done[name] for base in bases for name in named(base)], axis=1)
    return (
        block_output,
        input_gradient,
        joined("qkv"),
        g_qv,
        joined("o"),
        g_out_b,
        joined("u"),
        g_up_b,
        joined("d"),
        g_down_b,
        g_gain[None],
        g_shift[None],
    )


def solution(mesh):
    placed = (
        P("dp", None), P("dp", None), P("section", None), P("section"), P("section", None), P("section"),
        P("section", None), P("section"), P("section", None), P("section"), P("section", None), P("section", None),
        P("dp", None),
    )
    both = ("section", "dp")
    return jax.shard_map(
        per_device,
        mesh=mesh,
        in_specs=placed,
        out_specs=(
            P("dp", "section"), P("dp", "section"), P(both, None), P(both), P(both, None), P(both), P(both, None),
            P(both), P(both, None), P(both), P("section", "dp"), P("section", "dp"),
        ),
        check_vma=False,
    )
```
